32 devices in a mesh: img: 16 (over z, x, core), rows: 2 (over y).
Axes of the slice: x: 2, y: 2, z: 4, core: 2. Of those that a mesh axis runs over, the one named last changes fastest.
Arguments:
- inputs: float32 [16, 48, 24, 512], P('img', 'rows'), may hold values from -6 to 6
- cotangent: float32 [16, 48, 24, 512], P('img', 'rows'), may hold values from -6 to 6
- region: int32 [16, 48, 24], P('img', 'rows'), may hold values from 0 to 7, as said below
- rel_index: int32 [576, 576], replicated, may hold values from 0 to 2208, as said below
- qkv_weight: bfloat16 [2, 512, 1536], replicated, may hold values from -0.25 to 0.25
- qv_bias: float32 [2, 2, 512], replicated, may hold values from -3 to 3
- logit_scale: float32 [2, 16], replicated, may hold values from 1.8 to 2.6
- place_in: float32 [2, 2, 512], replicated, may hold values from -5 to 5
- place_bias: float32 [2, 512], replicated, may hold values from -3 to 3
- place_out: float32 [2, 512, 16], replicated, may hold values from -0.25 to 0.25
- proj_weight: bfloat16 [2, 512, 512], replicated, may hold values from -0.25 to 0.25
- up_weight: bfloat16 [2, 512, 2048], replicated, may hold values from -0.25 to 0.25
- up_bias: float32 [2, 2048], replicated, may hold values from -3 to 3
- down_weight: bfloat16 [2, 2048, 512], replicated, may hold values from -0.125 to 0.125
- out_bias: float32 [2, 2, 512], replicated, may hold values from -3 to 3
- norm_gain: float32 [2, 2, 512], replicated, may hold values from 0.5 to 1.5
- norm_shift: float32 [2, 2, 512], replicated, may hold values from -2 to 2
Outputs:
- output: float32 [16, 48, 24, 512], P('img', 'rows')
- input_grad: float32 [16, 48, 24, 512], P('img', 'rows')
- qkv_grad: float32 [2, 512, 1536], P(None, 'img', 'rows')
- qv_bias_grad: float32 [2, 2, 512], replicated
- logit_scale_grad: float32 [2, 16], replicated
- place_in_grad: float32 [2, 2, 512], replicated
- place_bias_grad: float32 [2, 512], replicated
- place_out_grad: float32 [2, 512, 16], replicated
- proj_grad: float32 [2, 512, 512], P(None, 'img', 'rows')
- up_grad: float32 [2, 512, 2048], P(None, 'img', 'rows')
- up_bias_grad: float32 [2, 2048], replicated
- down_grad: float32 [2, 2048, 512], P(None, 'img', 'rows')
- out_bias_grad: float32 [2, 2, 512], replicated
- norm_gain_grad: float32 [2, 2, 512], replicated
- norm_shift_grad: float32 [2, 2, 512], replicated
The draws below stay inside these ranges and needn't reach their ends.
Inputs may be any that keep to these rules, and one draw needn't show every extreme that they name: `region`: in each 24-row band of an image the labels split the band at one row and one column into up to four rectangles, with labels 4 * band + 2 * (lower part) + (right part). rel_index[i, j] names the table entry of the row and column offsets between tokens i and j of a window (row-major order), the same signs or swapping for all pairs.
All inputs are finite; a program needn't handle non-finite values.
Results may differ from the reference program's by a relative error of at most 0.017.
Values may be sent and summed in bfloat16 or wider, within the bound.
A program may use at most 576 MiB of HBM per device.

```python
import jax
import jax.numpy as jnp
from jax import lax

D = 512
HEADS = 16
FF = 2048
WIN = 24
BIAS_HIDDEN = 512
IMAGES = 16
ROWS = 48


def draw_region(key, part):
    key = jax.random.fold_in(key, 11)
    bands = ROWS // WIN
    row_cut = jax.random.randint(jax.random.fold_in(key, 1), (IMAGES, bands), 1, WIN)
    col_cut = jax.random.randint(jax.random.fold_in(key, 2), (IMAGES, bands), 1, WIN)
    inner = jnp.arange(WIN, dtype=jnp.int32)
    lower = (inner[None, None, :, None] >= row_cut[:, :, None, None]).astype(jnp.int32)
    right = (inner[None, None, None, :] >= col_cut[:, :, None, None]).astype(jnp.int32)
    band_id = jnp.arange(bands, dtype=jnp.int32)[None, :, None, None]
    labels = band_id * 4 + lower * 2 + right
    return labels.reshape(IMAGES, ROWS, WIN)


def draw_rel_index(key, part):
    key = jax.random.fold_in(key, 23)
    flips = jax.random.randint(key, (3,), 0, 2)
    places = jnp.arange(WIN * WIN, dtype=jnp.int32)
    row_pos = places // WIN
    col_pos = places % WIN
    down = (row_pos[:, None] - row_pos[None, :]) * (1 - 2 * flips[0])
    across = (col_pos[:, None] - col_pos[None, :]) * (1 - 2 * flips[1])
    first = jnp.where(flips[2] == 1, across, down)
    second = jnp.where(flips[2] == 1, down, across)
    return ((first + WIN - 1) * (2 * WIN - 1) + second + WIN - 1).astype(jnp.int32)


def block_scale(rng, shape, cuts, low, top_value):
    loudness = 1.0
    for position, blocks in cuts:
        draws = jax.random.uniform(jax.random.fold_in(jax.random.fold_in(rng, 6), position), (blocks,), jnp.float32, low / len(cuts), top_value / len(cuts))
        loudness = loudness * jnp.repeat(jnp.exp(draws), shape[position] // blocks).reshape((-1,) + (1,) * (len(shape) - 1 - position))
    return loudness


def normal_values(key, dims, scale, limit, shards=(), held_as=jnp.bfloat16):
    values = jax.random.normal(key, dims, jnp.float32) * scale
    if len(shards) > 0:
        values = block_scale(key, dims, shards, -0.22, 0.18) * values
    return jnp.clip(values, min=-limit, max=limit).astype(held_as)


def setup_inputs(seed: int = 0) -> dict:
    seeds = jax.random.split(jax.random.key(seed), 18)
    inputs = normal_values(seeds[0], (IMAGES, ROWS, WIN, D), 1.0, 6.0, ((0, 16), (1, 2)), jnp.float32)
    cotangent = normal_values(seeds[1], (IMAGES, ROWS, WIN, D), 1.0, 6.0, ((0, 16), (1, 2)), jnp.float32)
    region = draw_region(jax.random.fold_in(seeds[17], 71), 0)
    rel_index = draw_rel_index(jax.random.fold_in(seeds[17], 71), 0)
    qkv_weight = normal_values(seeds[4], (2, D, 3 * D), D ** -0.5, 0.25)
    qv_bias = normal_values(seeds[5], (2, 2, D), 0.5, 3.0, (), jnp.float32)
    logit_scale = jnp.clip(jax.random.uniform(seeds[6], (2, HEADS), jnp.float32, 1.8, 2.6), 1.8, 2.6)
    place_in = normal_values(seeds[7], (2, 2, BIAS_HIDDEN), 1.0, 5.0, (), jnp.float32)
    place_bias = normal_values(seeds[8], (2, BIAS_HIDDEN), 0.5, 3.0, (), jnp.float32)
    place_out = normal_values(seeds[9], (2, BIAS_HIDDEN, HEADS), BIAS_HIDDEN ** -0.5, 0.25, (), jnp.float32)
    proj_weight = normal_values(seeds[10], (2, D, D), D ** -0.5, 0.25)
    up_weight = normal_values(seeds[11], (2, D, FF), D ** -0.5, 0.25)
    up_bias = normal_values(seeds[12], (2, FF), 0.5, 3.0, (), jnp.float32)
    down_weight = normal_values(seeds[13], (2, FF, D), FF ** -0.5, 0.125)
    out_bias = normal_values(seeds[14], (2, 2, D), 0.5, 3.0, (), jnp.float32)
    norm_gain = jnp.clip(1.0 + 0.1 * jax.random.normal(seeds[15], (2, 2, D), jnp.float32), 0.5, 1.5)
    norm_shift = normal_values(seeds[16], (2, 2, D), 0.3, 2.0, (), jnp.float32)
    return dict(inputs=inputs, cotangent=cotangent, region=region, rel_index=rel_index, qkv_weight=qkv_weight, qv_bias=qv_bias, logit_scale=logit_scale, place_in=place_in, place_bias=place_bias, place_out=place_out, proj_weight=proj_weight, up_weight=up_weight, up_bias=up_bias, down_weight=down_weight, out_bias=out_bias, norm_gain=norm_gain, norm_shift=norm_shift)


@jax.custom_vjp
def low(v):
    return lax.optimization_barrier(v.astype(jnp.bfloat16)).astype(jnp.float32)

@jax.custom_vjp
def low_back(v):
    return v

def low_keep(v):
    return (low(v), None)

def low_pass(kept, grad):
    return (grad,)

def back_keep(v):
    return (v, None)

def back_low(kept, grad):
    return (low(grad),)
low.defvjp(low_keep, low_pass)
low_back.defvjp(back_keep, back_low)
HIGH = lax.Precision.HIGHEST

def table_coords(window):
    span = 2 * window - 1
    offsets = jnp.arange(span, dtype=jnp.float32) - (window - 1)
    scaled = offsets * (8.0 / (window - 1))
    logged = jnp.sign(scaled) * jnp.log2(jnp.abs(scaled) + 1.0) / 3.0
    first = jnp.repeat(logged, span)
    second = jnp.tile(logged, span)
    return jnp.stack([first, second], axis=1)

def position_bias(coords, rel_index, weight_in, bias_in, weight_out):
    hidden_net = jax.nn.gelu(jnp.dot(coords, weight_in, precision=HIGH) + bias_in, approximate=False)
    table = 16.0 * jax.nn.sigmoid(jnp.dot(hidden_net, weight_out, precision=HIGH))
    heads_first = jnp.transpose(table)
    return heads_first[:, rel_index]

def layer_norm(values, gain, shift):
    centre = values - lax.optimization_barrier(jnp.mean(values, axis=-1, keepdims=True))
    spread = lax.optimization_barrier(jnp.mean(centre * centre, axis=-1, keepdims=True))
    return centre * lax.rsqrt(spread + 1e-05) * gain + shift

def unit(values):
    return values * lax.rsqrt(lax.optimization_barrier(jnp.sum(values * values, axis=-1, keepdims=True)) + 1e-06)

def window_attention(entry, same_mask, bias, w_qkv, q_bias, v_bias, scale_log):
    tokens = entry.shape[0]
    heads = scale_log.shape[0]
    qkv_bias = jnp.concatenate([q_bias, jnp.zeros_like(q_bias), v_bias])
    projected = low_back(jnp.dot(entry, w_qkv, precision=HIGH) + qkv_bias)
    parts = projected.reshape(tokens, 3, heads, -1)
    queries = low(unit(parts[:, 0]))
    keys = low(unit(parts[:, 1]))
    values = low(parts[:, 2])
    cosine = low_back(jnp.einsum('thd,shd->hts', queries, keys, precision=HIGH))
    scores = cosine * jnp.exp(scale_log)[:, None, None] + bias
    scores = jnp.where(same_mask[None], scores, -1000000000.0)
    expo = jnp.exp(scores - lax.optimization_barrier(jnp.max(scores, axis=-1, keepdims=True)))
    probs = low(expo / lax.optimization_barrier(jnp.sum(expo, axis=-1, keepdims=True)))
    mixed = jnp.einsum('hts,shd->thd', probs, values, precision=HIGH).reshape(tokens, -1)
    return low(low_back(mixed))

def swin_block(x_img, same_mask, bias, params, layer, shifted):
    w_qkv, qv_bias, logit_scale, w_proj, w_up, up_bias, w_down, out_bias, norm_gain, norm_shift = params
    height, breadth, width = x_img.shape
    halfway = breadth // 2
    if shifted:
        entry = low(low_back(x_img))
        entry = jnp.roll(entry, (-halfway, -halfway), axis=(0, 1))
    else:
        entry = low(x_img)
    windows = entry.reshape(-1, breadth * breadth, width)
    mixed = jax.vmap(window_attention, in_axes=(0, 0, None, None, None, None, None))(windows, same_mask, bias, w_qkv[layer], qv_bias[layer, 0], qv_bias[layer, 1], logit_scale[layer])
    mixed = mixed.reshape(height, breadth, width)
    if shifted:
        mixed = jnp.roll(mixed, (halfway, halfway), axis=(0, 1))
    flat_mixed = mixed.reshape(-1, width)
    attn_out = low_back(jnp.dot(flat_mixed, w_proj[layer], precision=HIGH) + out_bias[layer, 0])
    resid = x_img.reshape(-1, width) + layer_norm(attn_out, norm_gain[layer, 0], norm_shift[layer, 0])
    pre_act = low_back(jnp.dot(low(resid), w_up[layer], precision=HIGH) + up_bias[layer])
    act_low = low(jax.nn.gelu(pre_act, approximate=False))
    mlp_out = low_back(jnp.dot(act_low, w_down[layer], precision=HIGH) + out_bias[layer, 1])
    result = resid + layer_norm(mlp_out, norm_gain[layer, 1], norm_shift[layer, 1])
    return result.reshape(height, breadth, width)

def forward(params, inputs, region, rel_index):
    w_qkv, qv_bias, logit_scale, place_in, place_bias, place_out, w_proj, w_up, up_bias, w_down, out_bias, norm_gain, norm_shift = params
    block_params = (w_qkv, qv_bias, logit_scale, w_proj, w_up, up_bias, w_down, out_bias, norm_gain, norm_shift)
    window = inputs.shape[2]
    coords = table_coords(window)
    bias_zero = position_bias(coords, rel_index, place_in[0], place_bias[0], place_out[0])
    bias_one = position_bias(coords, rel_index, place_in[1], place_bias[1], place_out[1])

    def one_image(item):
        x_img, region_img = item
        labels = region_img.reshape(-1, window * window)
        same_mask = labels[:, :, None] == labels[:, None, :]
        open_mask = jnp.ones_like(same_mask)
        hidden = swin_block(x_img, open_mask, bias_zero, block_params, 0, False)
        return swin_block(hidden, same_mask, bias_one, block_params, 1, True)
    return lax.map(jax.checkpoint(one_image), (inputs, region))

def reference(inputs, cotangent, region, rel_index, qkv_weight, qv_bias, logit_scale, place_in, place_bias, place_out, proj_weight, up_weight, up_bias, down_weight, out_bias, norm_gain, norm_shift):
    params = tuple((item.astype(jnp.float32) for item in (qkv_weight, qv_bias, logit_scale, place_in, place_bias, place_out, proj_weight, up_weight, up_bias, down_weight, out_bias, norm_gain, norm_shift)))

    def apply(param_set, values):
        return forward(param_set, values, region, rel_index)
    output, pull = jax.vjp(apply, params, inputs)
    grads, input_grad = pull(cotangent)
    return (output, input_grad, grads[0], grads[1], grads[2], grads[3], grads[4], grads[5], grads[6], grads[7], grads[8], grads[9], grads[10], grads[11], grads[12])
```

```python
import functools

import jax
import jax.numpy as jnp
from jax import lax
from jax.experimental import pallas as pl
from jax.experimental.pallas import tpu as pltpu
from jax.sharding import PartitionSpec as P

BF = jnp.bfloat16
F32 = jnp.float32
LOG2E = 1.4426950408889634
MASKED = 1.0e9
LANES = 128


def passed_along(array, axis, by):
    devices = lax.axis_size(axis)
    return lax.ppermute(array, axis, [(i, (i + by) % devices) for i in range(devices)])


def mm(a, b):
    return lax.dot_general(a, b, (((1,), (0,)), ((), ())), preferred_element_type=F32)


def mm_nt(a, b):
    return lax.dot_general(a, b, (((1,), (1,)), ((), ())), preferred_element_type=F32)


def mm_tn(a, b):
    return lax.dot_general(a, b, (((0,), (0,)), ((), ())), preferred_element_type=F32)


def group_sum(values, depth):
    rows = lax.broadcasted_iota(jnp.int32, (LANES, LANES), 0) // depth
    cols = lax.broadcasted_iota(jnp.int32, (LANES, LANES), 1) // depth
    ones = jnp.where(rows == cols, 1.0, 0.0).astype(BF)
    high = values.astype(BF)
    low = (values - high.astype(F32)).astype(BF)
    return mm(high, ones) + mm(low, ones)


def normal_parts(values):
    gauss = jnp.exp2(values * values * (-0.5 * LOG2E))
    size = jnp.abs(values)
    t = 1.0 / (1.0 + size * (0.3275911 * 0.7071067811865476))
    poly = t * (
        0.127414796
        + t * (-0.142248368 + t * (0.7107068705 + t * (-0.7265760135 + t * 0.5307027145)))
    )
    tail = poly * gauss
    cdf = jnp.where(values >= 0.0, 1.0 - tail, tail)
    return cdf, gauss * 0.3989422804014327


def norm_stats(values):
    centre = values - jnp.mean(values, axis=-1, keepdims=True)
    spread = jnp.mean(centre * centre, axis=-1, keepdims=True)
    rstd = lax.rsqrt(spread + 1e-05)
    return centre * rstd, rstd


def norm_pull(values, gain, grad):
    hat, rstd = norm_stats(values)
    scaled = grad * gain
    first = jnp.mean(scaled, axis=-1, keepdims=True)
    second = jnp.mean(scaled * hat, axis=-1, keepdims=True)
    pulled = rstd * (scaled - first - hat * second)
    gain_grad = jnp.sum(grad * hat, axis=0, keepdims=True)
    shift_grad = jnp.sum(grad, axis=0, keepdims=True)
    return pulled, gain_grad, shift_grad


Q_BIAS, K_BIAS, V_BIAS, OUT0, GAIN0, SHIFT0, OUT1, GAIN1, SHIFT1, SCALE = range(10)


def forward_kernel(
    masked, window, depth, groups, chunks,
    x_ref, qm_ref, km_ref, wq_ref, wk_ref, wv_ref, vec_ref, gvec_ref, bias_ref,
    wp_ref, wu_ref, wd_ref, ub_ref,
    out_ref, e_ref, qn_ref, kn_ref, v_ref, o_ref, iq_ref, ik_ref, rinv_ref, p_ref,
    a_ref, zr_ref, g_ref, gd_ref, m_ref,
    o_s, z_s, m_s,
):
    step = pl.program_id(0)
    tokens = window * window
    per = LANES // depth
    lane = lax.broadcasted_iota(jnp.int32, (1, LANES), 1) // depth

    @pl.when(step == 0)
    def _():
        e_ref[...] = x_ref[...].astype(BF)

    @pl.when(step < groups)
    def _():
        entry = e_ref[...]
        q = mm(entry, wq_ref[0]) + gvec_ref[Q_BIAS : Q_BIAS + 1]
        k = mm(entry, wk_ref[0])
        v = mm(entry, wv_ref[0]) + gvec_ref[V_BIAS : V_BIAS + 1]
        iq = lax.rsqrt(group_sum(q * q, depth) + 1e-06)
        ik = lax.rsqrt(group_sum(k * k, depth) + 1e-06)
        qn = q * iq
        kn = (k * ik).astype(BF)
        iq_ref[...] = iq
        ik_ref[...] = ik
        qn_ref[...] = qn.astype(BF)
        kn_ref[...] = kn
        v_ref[...] = v.astype(BF)
        rhs = jnp.concatenate([kn, km_ref[...]], axis=1) if masked else kn
        total = jnp.zeros((tokens, 2 * LANES), F32)
        for h in range(per):
            mine = lane == h
            lhs = jnp.where(mine, qn, 0.0).astype(BF)
            if masked:
                lhs = jnp.concatenate([lhs, qm_ref[...]], axis=1)
            cosine = mm_nt(lhs, rhs)
            scale = gvec_ref[SCALE : SCALE + 1, h * depth : h * depth + 1] * LOG2E
            table = bias_ref[h]
            for pair in range(window // 2):
                parts = []
                for r in (2 * pair, 2 * pair + 1):
                    at = window * (window - 1 - r)
                    parts.append(
                        cosine[r * window : (r + 1) * window] * scale + table[:, at : at + tokens]
                    )
                both = jnp.concatenate(parts, axis=0)
                p_ref[h, 2 * pair * window : (2 * pair + 2) * window, :] = jnp.exp2(both).astype(BF)
            weights = jnp.concatenate(
                [jnp.where(mine, v, 0.0), jnp.where(mine, jnp.ones_like(v), 0.0)], axis=1
            ).astype(BF)
            total = total + mm(p_ref[h], weights)
        rinv = 1.0 / total[:, LANES:]
        rinv_ref[...] = rinv
        o32 = total[:, :LANES] * rinv
        o_ref[...] = o32
        o = o32.astype(BF)
        o_s[:, pl.ds(pl.multiple_of(step * LANES, LANES), LANES)] = o

    @pl.when(step == groups)
    def _():
        a = mm(o_s[...], wp_ref[0]) + vec_ref[OUT0 : OUT0 + 1]
        a_ref[...] = a
        hat, _ = norm_stats(a)
        z = x_ref[...] + (hat * vec_ref[GAIN0 : GAIN0 + 1] + vec_ref[SHIFT0 : SHIFT0 + 1])
        z_s[...] = z
        zr_ref[...] = z.astype(BF)
        m_s[...] = jnp.zeros_like(m_s)

    @pl.when(step >= groups)
    def _():
        pre = mm(zr_ref[...], wu_ref[0]) + ub_ref[0]
        cdf, density = normal_parts(pre)
        act = (pre * cdf).astype(BF)
        g_ref[...] = act
        gd_ref[...] = (cdf + pre * density).astype(BF)
        m_s[...] += mm(act, wd_ref[0])

    @pl.when(step == groups + chunks - 1)
    def _():
        m = m_s[...] + vec_ref[OUT1 : OUT1 + 1]
        m_ref[...] = m
        hat, _ = norm_stats(m)
        out_ref[...] = z_s[...] + (hat * vec_ref[GAIN1 : GAIN1 + 1] + vec_ref[SHIFT1 : SHIFT1 + 1])


def block_forward(layer, x, vec, tables, labels_low, w_qkv, w_proj, w_up, up_bias, w_down, window, heads):
    tokens, width = x.shape
    depth = width // heads
    ff = w_up.shape[2]
    groups = width // LANES
    per = LANES // depth
    chunk = 512
    chunks = ff // chunk
    masked = labels_low is not None
    if masked:
        queries_mask, keys_mask = labels_low
    else:
        queries_mask = jnp.zeros((16, LANES), BF)
        keys_mask = queries_mask
    at_group = lambda s: jnp.minimum(s, groups - 1)
    at_chunk = lambda s: jnp.maximum(s - groups, 0)
    whole = lambda shape: pl.BlockSpec(shape, lambda s: (0,) * len(shape))
    by_group = pl.BlockSpec((tokens, LANES), lambda s: (0, at_group(s)))
    by_chunk = pl.BlockSpec((tokens, chunk), lambda s: (0, at_chunk(s)))
    kernel = functools.partial(forward_kernel, masked, window, depth, groups, chunks)
    tok = lambda dt, cols=width: jax.ShapeDtypeStruct((tokens, cols), dt)
    return pl.pallas_call(
        kernel,
        grid=(groups + chunks,),
        in_specs=[
            whole((tokens, width)),
            whole(queries_mask.shape),
            whole(keys_mask.shape),
            pl.BlockSpec((1, width, LANES), lambda s: (layer, 0, at_group(s))),
            pl.BlockSpec((1, width, LANES), lambda s: (layer, 0, groups + at_group(s))),
            pl.BlockSpec((1, width, LANES), lambda s: (layer, 0, 2 * groups + at_group(s))),
            whole(vec.shape),
            pl.BlockSpec((vec.shape[0], LANES), lambda s: (0, at_group(s))),
            pl.BlockSpec((per,) + tables.shape[1:], lambda s: (at_group(s), 0, 0)),
            pl.BlockSpec((1, width, width), lambda s: (layer, 0, 0)),
            pl.BlockSpec((1, width, chunk), lambda s: (layer, 0, at_chunk(s))),
            pl.BlockSpec((1, chunk, width), lambda s: (layer, at_chunk(s), 0)),
            pl.BlockSpec((1, 1, chunk), lambda s: (layer, 0, at_chunk(s))),
        ],
        out_specs=[
            whole((tokens, width)),
            whole((tokens, width)),
            by_group, by_group, by_group, by_group, by_group, by_group, by_group,
            pl.BlockSpec((per, tokens, tokens), lambda s: (at_group(s), 0, 0)),
            whole((tokens, width)),
            whole((tokens, width)),
            by_chunk, by_chunk,
            whole((tokens, width)),
        ],
        out_shape=[
            tok(F32), tok(BF),
            tok(BF), tok(BF), tok(BF), tok(F32), tok(F32), tok(F32), tok(F32),
            jax.ShapeDtypeStruct((heads, tokens, tokens), BF),
            tok(F32), tok(BF), tok(BF, ff), tok(BF, ff), tok(F32),
        ],
        scratch_shapes=[
            pltpu.VMEM((tokens, width), BF),
            pltpu.VMEM((tokens, width), F32),
            pltpu.VMEM((tokens, width), F32),
        ],
        compiler_params=pltpu.CompilerParams(vmem_limit_bytes=56 * 2**20),
        name="block_forward_%d" % layer,
    )(x, queries_mask, keys_mask, w_qkv, w_qkv, w_qkv, vec, vec, tables, w_proj, w_up, w_down, up_bias)


def feed_back_kernel(
    chunks,
    dy_ref, m_ref, a_ref, zr_ref, o_ref, g_ref, gd_ref, vec_ref, wd_ref, wu_ref, wp_ref,
    down_ref, up_ref, ub_ref, proj_ref, do_ref, dz_ref, sums_ref,
    dm_s, acc_s,
):
    step = pl.program_id(0)

    @pl.when(step == 0)
    def _():
        dm, gain_grad, shift_grad = norm_pull(m_ref[...], vec_ref[GAIN1 : GAIN1 + 1], dy_ref[...])
        low = dm.astype(BF)
        dm_s[...] = low
        sums_ref[...] = jnp.zeros_like(sums_ref)
        sums_ref[0:1] = jnp.sum(low.astype(F32), axis=0, keepdims=True)
        sums_ref[1:2] = gain_grad
        sums_ref[2:3] = shift_grad
        acc_s[...] = dy_ref[...]

    dm = dm_s[...]
    down_ref[...] = mm_tn(g_ref[...], dm).astype(BF)
    dh = (mm_nt(dm, wd_ref[0]) * gd_ref[...].astype(F32)).astype(BF)
    ub_ref[0] = jnp.sum(dh.astype(F32), axis=0, keepdims=True)
    up_ref[...] = mm_tn(zr_ref[...], dh).astype(BF)
    acc_s[...] += mm_nt(dh, wu_ref[0])

    @pl.when(step == chunks - 1)
    def _():
        dz = acc_s[...]
        dz_ref[...] = dz
        da, gain_grad, shift_grad = norm_pull(a_ref[...], vec_ref[GAIN0 : GAIN0 + 1], dz)
        low = da.astype(BF)
        sums_ref[3:4] = jnp.sum(low.astype(F32), axis=0, keepdims=True)
        sums_ref[4:5] = gain_grad
        sums_ref[5:6] = shift_grad
        proj_ref[...] = mm_tn(o_ref[...].astype(BF), low).astype(BF)
        do_ref[...] = mm_nt(low, wp_ref[0]).astype(BF)


def feed_backward(layer, dy, m, a, zr, o, g, gd, vec, w_down, w_up, w_proj):
    tokens, width = dy.shape
    ff = g.shape[1]
    chunk = 512
    chunks = ff // chunk
    whole = lambda shape: pl.BlockSpec(shape, lambda s: (0,) * len(shape))
    full = whole((tokens, width))
    by_chunk = pl.BlockSpec((tokens, chunk), lambda s: (0, s))
    sds = jax.ShapeDtypeStruct
    return pl.pallas_call(
        functools.partial(feed_back_kernel, chunks),
        grid=(chunks,),
        in_specs=[
            full, full, full, full, full, by_chunk, by_chunk, whole(vec.shape),
            pl.BlockSpec((1, chunk, width), lambda s: (layer, s, 0)),
            pl.BlockSpec((1, width, chunk), lambda s: (layer, 0, s)),
            pl.BlockSpec((1, width, width), lambda s: (layer, 0, 0)),
        ],
        out_specs=[
            pl.BlockSpec((chunk, width), lambda s: (s, 0)),
            pl.BlockSpec((width, chunk), lambda s: (0, s)),
            pl.BlockSpec((1, 1, chunk), lambda s: (0, 0, s)),
            whole((width, width)),
            full, full, whole((8, width)),
        ],
        out_shape=[
            sds((ff, width), BF), sds((width, ff), BF), sds((1, 1, ff), F32), sds((width, width), BF),
            sds((tokens, width), BF), sds((tokens, width), F32), sds((8, width), F32),
        ],
        scratch_shapes=[pltpu.VMEM((tokens, width), BF), pltpu.VMEM((tokens, width), F32)],
        compiler_params=pltpu.CompilerParams(vmem_limit_bytes=56 * 2**20),
        name="feed_backward_%d" % layer,
    )(dy, m, a, zr, o, g, gd, vec, w_down, w_up, w_proj)


def attend_back_kernel(
    window, depth, groups,
    e_ref, do_ref, o_ref, qn_ref, kn_ref, v_ref, iq_ref, ik_ref, rinv_ref, p_ref, gvec_ref,
    wq_ref, wk_ref, wv_ref, dz_ref,
    dx_ref, grads_ref, sums_ref, table_ref,
    et_s, ds_s,
):
    step = pl.program_id(0)
    tokens = window * window
    per = LANES // depth
    lane = lax.broadcasted_iota(jnp.int32, (1, LANES), 1)

    @pl.when(step == 0)
    def _():
        et_s[...] = e_ref[...].T
        dx_ref[...] = dz_ref[...]

    scale = gvec_ref[SCALE : SCALE + 1]
    v = v_ref[...]
    kn = kn_ref[...]
    qn = qn_ref[...]
    dor = (do_ref[...].astype(F32) * rinv_ref[...]).astype(BF)
    dor32 = dor.astype(F32)
    less = -group_sum(dor32 * o_ref[...], depth)
    high = less.astype(BF).astype(F32)
    extra = jnp.where(lane % depth == 0, high, jnp.where(lane % depth == 1, less - high, 0.0))
    dor_t = dor.T
    qn_t = qn.T
    rhs = jnp.concatenate([v, jnp.ones_like(v)], axis=1)
    wide = table_ref.shape[2]
    shifted = (tokens + LANES - 1) // LANES * LANES + LANES
    dq = jnp.zeros((tokens, LANES), F32)
    dk_t = []
    dv_t = []
    for h in range(per):
        mine = lane // depth == h
        lhs = jnp.concatenate(
            [jnp.where(mine, dor32, 0.0), jnp.where(mine, extra, 0.0)], axis=1
        ).astype(BF)
        t = mm_nt(lhs, rhs)
        table_ref[h] = jnp.zeros(table_ref.shape[1:], F32)
        for pair in range(window // 2):
            rows = slice(2 * pair * window, (2 * pair + 2) * window)
            ds = p_ref[h, rows, :].astype(F32) * t[rows]
            ds_s[h, rows, :] = ds.astype(BF)
            for i in range(2):
                at = window * (window - 1 - (2 * pair + i))
                block = ds[i * window : (i + 1) * window]
                table_ref[h, :, at : at + tokens] += block
        low = ds_s[h]
        keys = jnp.where(mine, kn.astype(F32), 0.0).astype(BF)
        dq = dq + mm(low, keys)
        dk_t.append(mm(qn_t[h * depth : (h + 1) * depth], low))
        dv_t.append(mm(dor_t[h * depth : (h + 1) * depth], p_ref[h]))
    dqn = dq * scale
    dkn = jnp.concatenate(dk_t, axis=0).T * scale
    dv = jnp.concatenate(dv_t, axis=0).T
    qn32 = qn.astype(F32)
    kn32 = kn.astype(F32)
    along_q = qn32 * dqn
    dq = iq_ref[...] * (dqn - qn32 * group_sum(along_q, depth))
    dk = ik_ref[...] * (dkn - kn32 * group_sum(kn32 * dkn, depth))
    sums_ref[...] = jnp.zeros_like(sums_ref)
    sums_ref[0:1] = jnp.sum(along_q, axis=0, keepdims=True)
    parts = []
    for i, part in enumerate((dq, dk, dv)):
        low = part.astype(BF)
        parts.append(low)
        sums_ref[i + 1 : i + 2] = jnp.sum(low.astype(F32), axis=0, keepdims=True)
    low = jnp.concatenate(parts, axis=1)
    grads = mm(et_s[...], low)
    for i in range(3):
        grads_ref[i] = grads[:, i * LANES : (i + 1) * LANES].astype(BF)
    weights = jnp.concatenate([wq_ref[0], wk_ref[0], wv_ref[0]], axis=1)
    dx_ref[...] += mm_nt(low, weights)


def attend_backward(layer, entry, do, saved, vec, w_qkv, dz, table_shape, window, heads):
    qn, kn, v, o, iq, ik, rinv, p = saved
    tokens, width = entry.shape
    depth = width // heads
    groups = width // LANES
    per = LANES // depth
    whole = lambda shape: pl.BlockSpec(shape, lambda s: (0,) * len(shape))
    by_group = pl.BlockSpec((tokens, LANES), lambda s: (0, s))
    full = whole((tokens, width))
    sds = jax.ShapeDtypeStruct
    return pl.pallas_call(
        functools.partial(attend_back_kernel, window, depth, groups),
        grid=(groups,),
        in_specs=[full] + [by_group] * 8 + [
            pl.BlockSpec((per, tokens, tokens), lambda s: (s, 0, 0)),
            pl.BlockSpec((vec.shape[0], LANES), lambda s: (0, s)),
            pl.BlockSpec((1, width, LANES), lambda s: (layer, 0, s)),
            pl.BlockSpec((1, width, LANES), lambda s: (layer, 0, groups + s)),
            pl.BlockSpec((1, width, LANES), lambda s: (layer, 0, 2 * groups + s)),
            full,
        ],
        out_specs=[
            full,
            pl.BlockSpec((3, width, LANES), lambda s: (0, 0, s)),
            pl.BlockSpec((8, LANES), lambda s: (0, s)),
            pl.BlockSpec((per,) + table_shape[1:], lambda s: (s, 0, 0)),
        ],
        out_shape=[
            sds((tokens, width), F32),
            sds((3, width, width), BF),
            sds((8, width), F32),
            sds(table_shape, F32),
        ],
        scratch_shapes=[
            pltpu.VMEM((width, tokens), BF),
            pltpu.VMEM((per, tokens, tokens), BF),
        ],
        compiler_params=pltpu.CompilerParams(vmem_limit_bytes=56 * 2**20),
        name="attend_backward_%d" % layer,
    )(entry, do, o, qn, kn, v, iq, ik, rinv, p, vec, w_qkv, w_qkv, w_qkv, dz)


def entry_logs(first, count, window):
    at = first + lax.broadcasted_iota(jnp.int32, (8, count), 1)
    row = at // (2 * window)
    col = at % (2 * window)
    real = (row < 2 * window - 1) & (col < 2 * window - 1)
    def logs(offset):
        size = jnp.log2(jnp.abs(offset).astype(F32) * (8.0 / (window - 1)) + 1.0) / 3.0
        return jnp.where(offset < 0, -size, size)
    by_row = jnp.where(real, logs(window - 1 - row), 0.0)
    by_col = jnp.where(real, logs(col - (window - 1)), 0.0)
    return by_row, by_col, real


def column_of(token_col, window, shifted):
    if not shifted:
        return token_col
    return jnp.where(token_col >= window // 2, token_col - window // 2, token_col + window // 2)


def table_kernel(window, shifted, chunk, w_ref, out_w_ref, rows_ref, tab_ref, hid_ref, slope_ref):
    step = pl.program_id(0)
    steps = pl.num_programs(0)
    heads = tab_ref.shape[0]
    by_row, by_col, _ = entry_logs(step * chunk, chunk, window)
    pre = w_ref[:, 0:1] * by_row[0:1] + w_ref[:, 1:2] * by_col[0:1] + w_ref[:, 2:3]
    cdf, density = normal_parts(pre)
    act = pre * cdf
    hidden = act.astype(BF)
    hid_ref[...] = hidden
    slope_ref[...] = (cdf + pre * density).astype(BF)
    rest = (act - hidden.astype(F32)).astype(BF)
    both = mm(out_w_ref[...], hidden)
    logits = both[:heads] + both[heads:] + mm(out_w_ref[:heads], rest)
    tab_ref[:, pl.ds(pl.multiple_of(step * chunk, chunk), chunk)] = 16.0 / (1.0 + jnp.exp(-logits))

    @pl.when(step == steps - 1)
    def _():
        spans = tab_ref.shape[1] // LANES
        wide = rows_ref.shape[2]
        row8 = lax.broadcasted_iota(jnp.int32, (8, LANES), 0)
        lane = lax.broadcasted_iota(jnp.int32, (8, LANES), 1)
        for tile in range(window // 8):
            c1 = column_of(row8 + 8 * tile, window, shifted)
            for k in range(wide // LANES):
                at = lane + LANES * k
                m = at // window
                source = 2 * window * m + c1 - column_of(at % window, window, shifted) + window - 1
                low = 2 * window * (LANES * k // window) // LANES
                high = min((2 * window * ((LANES * k + LANES - 1) // window) + 2 * window - 2) // LANES, spans - 1)
                for h in range(heads):
                    got = jnp.zeros((8, LANES), F32)
                    for s in range(low, high + 1):
                        piece = jnp.broadcast_to(tab_ref[h : h + 1, s * LANES : (s + 1) * LANES], (8, LANES))
                        near = source - s * LANES
                        inside = (near >= 0) & (near < LANES)
                        picked = jnp.take_along_axis(piece, jnp.where(inside, near, 0), axis=1)
                        got = jnp.where(inside, picked, got)
                    rows_ref[h, 8 * tile : 8 * tile + 8, k * LANES : (k + 1) * LANES] = got * LOG2E


def bias_table(layer, weights, out_weights, window, shifted):
    hidden, heads = weights.shape[0], out_weights.shape[0] // 2
    entries = 4 * window * window
    chunk = 256
    wide = ((2 * window - 1) * window + LANES - 1) // LANES * LANES
    whole = lambda shape: pl.BlockSpec(shape, lambda s: (0,) * len(shape))
    by_chunk = pl.BlockSpec((hidden, chunk), lambda s: (0, s))
    sds = jax.ShapeDtypeStruct
    return pl.pallas_call(
        functools.partial(table_kernel, window, shifted, chunk),
        grid=(entries // chunk,),
        in_specs=[whole(weights.shape), whole(out_weights.shape)],
        out_specs=[whole((heads, window, wide)), whole((heads, entries)), by_chunk, by_chunk],
        out_shape=[
            sds((heads, window, wide), F32), sds((heads, entries), F32),
            sds((hidden, entries), BF), sds((hidden, entries), BF),
        ],
        compiler_params=pltpu.CompilerParams(vmem_limit_bytes=40 * 2**20),
        name="bias_table_%d" % layer,
    )(weights, out_weights)


def table_back_kernel(window, shifted, chunk, rows_ref, tab_ref, hid_ref, slope_ref, out_w_ref, grads_ref, outs_ref, dlog_s):
    step = pl.program_id(0)
    heads, entries = tab_ref.shape

    @pl.when(step == 0)
    def _():
        grads_ref[...] = jnp.zeros_like(grads_ref)
        outs_ref[...] = jnp.zeros_like(outs_ref)
        spans = rows_ref.shape[2] // LANES
        row8 = lax.broadcasted_iota(jnp.int32, (8, LANES), 0)
        lane = lax.broadcasted_iota(jnp.int32, (8, LANES), 1)
        for k in range(entries // LANES):
            at = lane + LANES * k
            m = at // (2 * window)
            d = at % (2 * window)
            sums = [jnp.zeros((8, LANES), F32) for _ in range(heads)]
            for tile in range(window // 8):
                c1 = column_of(row8 + 8 * tile, window, shifted)
                c2 = c1 - d + window - 1
                real = (c2 >= 0) & (c2 < window) & (m < 2 * window - 1)
                source = window * m + column_of(c2, window, shifted)
                low = window * (LANES * k // (2 * window)) // LANES
                high = min((window * ((LANES * k + LANES - 1) // (2 * window)) + window - 1) // LANES, spans - 1)
                for s in range(low, high + 1):
                    near = source - s * LANES
                    inside = (near >= 0) & (near < LANES) & real
                    near = jnp.where(inside, near, 0)
                    for h in range(heads):
                        piece = rows_ref[h, 8 * tile : 8 * tile + 8, s * LANES : (s + 1) * LANES]
                        picked = jnp.take_along_axis(piece, near, axis=1)
                        sums[h] = sums[h] + jnp.where(inside, picked, 0.0)
            for h in range(heads):
                dlog_s[h : h + 1, k * LANES : (k + 1) * LANES] = jnp.sum(sums[h], axis=0, keepdims=True)
        tab = tab_ref[...]
        dlog_s[...] = dlog_s[...] * tab * (1.0 - tab * 0.0625)

    by_row, by_col, real = entry_logs(step * chunk, chunk, window)
    dlog = dlog_s[:, pl.ds(pl.multiple_of(step * chunk, chunk), chunk)]
    low = dlog.astype(BF)
    outs_ref[...] += mm_nt(hid_ref[...], low)
    dhid = mm_tn(out_w_ref[...], low)
    dpre = (dhid * slope_ref[...].astype(F32)).astype(BF)
    which = lax.broadcasted_iota(jnp.int32, (16, chunk), 0)
    pick = lambda y: jnp.broadcast_to(y[0:1], (16, chunk))
    high_row = by_row.astype(BF).astype(F32)
    high_col = by_col.astype(BF).astype(F32)
    factors = jnp.where(which == 0, pick(high_row), 0.0)
    factors = jnp.where(which == 1, pick(high_col), factors)
    factors = jnp.where(which == 2, 1.0, factors)
    factors = jnp.where(which == 3, pick(by_row - high_row), factors)
    factors = jnp.where(which == 4, pick(by_col - high_col), factors)
    grads_ref[...] += mm_nt(dpre, factors.astype(BF))


def bias_table_backward(layer, rows, tab, hid, slope, out_weights, window, shifted):
    heads, entries = tab.shape
    hidden = hid.shape[0]
    chunk = 256
    whole = lambda shape: pl.BlockSpec(shape, lambda s: (0,) * len(shape))
    by_chunk = pl.BlockSpec((hidden, chunk), lambda s: (0, s))
    sds = jax.ShapeDtypeStruct
    return pl.pallas_call(
        functools.partial(table_back_kernel, window, shifted, chunk),
        grid=(entries // chunk,),
        in_specs=[whole(rows.shape), whole(tab.shape), by_chunk, by_chunk, whole(out_weights.shape)],
        out_specs=[whole((hidden, 16)), whole((hidden, heads))],
        out_shape=[sds((hidden, 16), F32), sds((hidden, heads), F32)],
        scratch_shapes=[pltpu.VMEM((heads, entries), F32)],
        compiler_params=pltpu.CompilerParams(vmem_limit_bytes=40 * 2**20),
        name="bias_table_backward_%d" % layer,
    )(rows, tab, hid, slope, out_weights)


def net_weights(steps, span, weight_in, bias_in):
    down, across = steps
    straight = jnp.abs(down) == span
    by_rows = jnp.where(straight, weight_in[0], weight_in[1]) * jnp.where(down > 0, 1.0, -1.0)
    by_cols = jnp.where(straight, weight_in[1], weight_in[0]) * jnp.where(across > 0, 1.0, -1.0)
    return jnp.pad(jnp.stack([by_rows, by_cols, bias_in], axis=1), ((0, 0), (0, 5)))


def split_out(weight_out):
    turned = weight_out.T
    high = turned.astype(BF)
    return jnp.concatenate([high, (turned - high.astype(F32)).astype(BF)], axis=0)


def net_grads(steps, span, grads, outs):
    down, across = steps
    straight = jnp.abs(down) == span
    by_rows = (grads[:, 0] + grads[:, 3]) * jnp.where(down > 0, 1.0, -1.0)
    by_cols = (grads[:, 1] + grads[:, 4]) * jnp.where(across > 0, 1.0, -1.0)
    weight_in = jnp.stack([jnp.where(straight, by_rows, by_cols), jnp.where(straight, by_cols, by_rows)])
    return weight_in, grads[:, 2], outs


def exchange(x, half_rows, by):
    return passed_along(x[:half_rows].astype(BF), "rows", by).astype(F32)


def take_shifted(x):
    half = x.shape[0] // 2
    return jnp.concatenate([x[half:], exchange(x, half, -1)], axis=0)


def give_back(x):
    half = x.shape[0] // 2
    returned = passed_along(x[half:].astype(BF), "rows", 1).astype(F32)
    return jnp.concatenate([returned, x[:half]], axis=0)


def shares(array, images, bands):
    rows, cols = array.shape
    cut = array.reshape(images, rows // images, bands, cols // bands)
    return jnp.transpose(cut, (0, 2, 1, 3)).reshape(images * bands, -1)


def summed_shares(arrays):
    images, bands = lax.axis_size("img"), lax.axis_size("rows")
    joined = jnp.concatenate([shares(array, images, bands) for array in arrays], axis=1)
    mine = lax.psum_scatter(joined, ("img", "rows"), scatter_dimension=0, tiled=True)
    mine = mine.reshape(-1).astype(F32)
    out = []
    at = 0
    for array in arrays:
        rows, cols = array.shape[0] // images, array.shape[1] // bands
        out.append(mine[at : at + rows * cols].reshape(rows, cols))
        at += rows * cols
    return out


def per_device(
    inputs,
    cotangent,
    region,
    rel_index,
    qkv_weight,
    qv_bias,
    logit_scale,
    place_in,
    place_bias,
    place_out,
    proj_weight,
    up_weight,
    up_bias,
    down_weight,
    out_bias,
    norm_gain,
    norm_shift,
):
    window, width = inputs.shape[2], inputs.shape[3]
    heads = logit_scale.shape[1]
    depth = width // heads
    tokens = window * window
    x = inputs.reshape(tokens, width)
    steps = (rel_index[window, 0] - rel_index[0, 0], rel_index[1, 0] - rel_index[0, 0])
    scales = jnp.repeat(jnp.exp(logit_scale), depth, axis=1)
    vecs = []
    for b in (0, 1):
        rows = [
            qv_bias[b, 0], jnp.zeros_like(qv_bias[b, 0]), qv_bias[b, 1],
            out_bias[b, 0], norm_gain[b, 0], norm_shift[b, 0],
            out_bias[b, 1], norm_gain[b, 1], norm_shift[b, 1], scales[b],
        ]
        vecs.append(jnp.pad(jnp.stack(rows), ((0, 6), (0, 0))))
    up_bias3 = up_bias[:, None, :]
    labels = jnp.roll(region.reshape(window, window), window // 2, axis=1).reshape(tokens, 1)
    same = labels == jnp.arange(LANES)
    low_labels = (
        same.astype(BF),
        jnp.where(same | (jnp.arange(LANES) >= 8), 0.0, -MASKED).astype(BF),
    )

    span = 2 * window - 1
    outs_low = [split_out(place_out[b]) for b in (0, 1)]

    def table_of(b):
        weights = net_weights(steps, span, place_in[b], place_bias[b])
        return bias_table(b, weights, outs_low[b], window, b == 1)

    table_zero, *net_zero = table_of(0)
    table_one, *net_one = table_of(1)

    def forward(b, x, table, masks):
        return block_forward(
            b, x, vecs[b], table, masks, qkv_weight, proj_weight, up_weight,
            up_bias3, down_weight, window, heads,
        )

    def backward(b, dy, saved):
        entry, qn, kn, v, o, iq, ik, rinv, p, a, zr, g, gd, m = saved
        down_grad, up_grad, ub_grad, proj_grad, do, dz, sums = feed_backward(
            b, dy, m, a, zr, o, g, gd, vecs[b], down_weight, up_weight, proj_weight
        )
        first = summed_shares((proj_grad, up_grad, down_grad))
        rows_shape = (heads, window, ((2 * window - 1) * window + LANES - 1) // LANES * LANES)
        dx, qkv3, qsums, table_grad = attend_backward(
            b, entry, do, (qn, kn, v, o, iq, ik, rinv, p), vecs[b], qkv_weight, dz, rows_shape, window, heads
        )
        qkv_grad = jnp.transpose(qkv3, (1, 0, 2)).reshape(width, 3 * width)
        second = summed_shares((qkv_grad,))
        matrices = second + first
        vectors = (
            qsums[0].reshape(heads, depth).sum(axis=1),
            ub_grad.reshape(-1),
            jnp.stack([qsums[1], qsums[3]]),
            jnp.stack([sums[3], sums[0]]),
            jnp.stack([sums[4], sums[1]]),
            jnp.stack([sums[5], sums[2]]),
        )
        return dx, matrices, vectors, table_grad

    band = lambda y: y.reshape(window, window, width)
    flat = lambda y: y.reshape(tokens, width)
    hidden, *saved_zero = forward(0, x, table_zero, None)
    x_one = flat(take_shifted(band(hidden)))
    dy_one = flat(take_shifted(band(cotangent.reshape(tokens, width))))
    shifted_out, *saved_one = forward(1, x_one, table_one, low_labels)
    output = give_back(band(shifted_out)).reshape(inputs.shape)
    dx_one, matrices_one, vectors_one, rows_one = backward(1, dy_one, saved_one)
    dy_zero = flat(give_back(band(dx_one)))
    dx_zero, matrices_zero, vectors_zero, rows_zero = backward(0, dy_zero, saved_zero)

    def pull(b, rows, net):
        grads = bias_table_backward(b, rows, *net, outs_low[b][:heads], window, b == 1)
        return net_grads(steps, span, *grads)

    net_zero = pull(0, rows_zero, net_zero)
    net_one = pull(1, rows_one, net_one)
    small = tuple(
        jnp.stack([first, second])
        for first, second in zip(vectors_zero + net_zero, vectors_one + net_one)
    )
    scale_grad, up_bias_grad, qv_grad, out_bias_grad, gain_grad, shift_grad, in_grad, bias_grad, out_grad = lax.psum(
        small, ("img", "rows")
    )
    qkv_grad, proj_grad, up_grad, down_grad = (
        jnp.stack([first, second]) for first, second in zip(matrices_zero, matrices_one)
    )
    return (
        output,
        dx_zero.reshape(inputs.shape),
        qkv_grad,
        qv_grad,
        scale_grad,
        in_grad,
        bias_grad,
        out_grad,
        proj_grad,
        up_grad,
        up_bias_grad,
        down_grad,
        out_bias_grad,
        gain_grad,
        shift_grad,
    )


def solution(mesh):
    token = P("img", "rows", None, None)
    matrix = P(None, "img", "rows")
    return jax.shard_map(
        per_device,
        mesh=mesh,
        in_specs=(token, token, P("img", "rows", None)) + (P(),) * 14,
        out_specs=(
            token, token, matrix, P(), P(), P(), P(), P(), matrix, matrix, P(), matrix, P(), P(), P(),
        ),
        check_vma=False,
    )
```

```python
import functools

import jax
import jax.numpy as jnp
from jax import lax
from jax.experimental import pallas as pl
from jax.experimental.pallas import tpu as pltpu
from jax.sharding import PartitionSpec as P

BF = jnp.bfloat16
F32 = jnp.float32
LOG2E = 1.4426950408889634
MASKED = 1.0e9
LANES = 128


def passed_along(array, axis, by):
    devices = lax.axis_size(axis)
    return lax.ppermute(array, axis, [(i, (i + by) % devices) for i in range(devices)])


def mm(a, b):
    return lax.dot_general(a, b, (((1,), (0,)), ((), ())), preferred_element_type=F32)


def mm_nt(a, b):
    return lax.dot_general(a, b, (((1,), (1,)), ((), ())), preferred_element_type=F32)


def mm_tn(a, b):
    return lax.dot_general(a, b, (((0,), (0,)), ((), ())), preferred_element_type=F32)


def group_ones(depth):
    rows = lax.broadcasted_iota(jnp.int32, (LANES, LANES), 0) // depth
    cols = lax.broadcasted_iota(jnp.int32, (LANES, LANES), 1) // depth
    return jnp.where(rows == cols, 1.0, 0.0).astype(BF)


def group_sums(ones, first, second):
    rows = first.shape[0]
    both = group_sum(ones, jnp.concatenate([first, second], axis=0))
    return both[:rows], both[rows:]


def group_sum(ones, values):
    high, low = split(values)
    return mm(jnp.concatenate([high, low], axis=1), jnp.concatenate([ones, ones], axis=0))


def split(values):
    high = values.astype(BF)
    return high, (values - high.astype(F32)).astype(BF)


def head_scales(logit_ref, layer, width):
    heads = logit_ref.shape[1]
    column = jnp.broadcast_to(logit_ref[layer : layer + 1], (heads, heads)).T[:, :1]
    head = lax.broadcasted_iota(jnp.int32, (heads, width), 0)
    owner = lax.broadcasted_iota(jnp.int32, (heads, width), 1) // (width // heads)
    return jnp.exp(jnp.sum(jnp.where(head == owner, column, 0.0), axis=0, keepdims=True))


def normal_parts(values):
    cdf = 0.5 + 0.5 * lax.erf(values * 0.7071067811865476)
    return cdf, jnp.exp2(values * values * (-0.5 * LOG2E)) * 0.3989422804014327


def norm_stats(values):
    centre = values - jnp.mean(values, axis=-1, keepdims=True)
    spread = jnp.mean(centre * centre, axis=-1, keepdims=True)
    rstd = lax.rsqrt(spread + 1e-05)
    return centre * rstd, rstd


def norm_pull(values, gain, grad):
    hat, rstd = norm_stats(values)
    scaled = grad * gain
    first = jnp.mean(scaled, axis=-1, keepdims=True)
    second = jnp.mean(scaled * hat, axis=-1, keepdims=True)
    pulled = rstd * (scaled - first - hat * second)
    gain_grad = jnp.sum(grad * hat, axis=0, keepdims=True)
    shift_grad = jnp.sum(grad, axis=0, keepdims=True)
    return pulled, gain_grad, shift_grad


def place():
    me, y = lax.axis_index("img"), lax.axis_index("rows")
    return me, me % 2, (me // 2) % 2, me // 4, y


def partner(which, step=1):
    me, core, x, z, y = place()
    if which == "core":
        return (me + 1 - 2 * core, y)
    if which == "x":
        return (me + 2 - 4 * x, y)
    if which == "y":
        return (me, 1 - y)
    depth = lax.axis_size("img") // 4
    return ((z + step) % depth * 4 + me % 4, y)


def greet(which):
    depth = lax.axis_size("img") // 4
    others = []
    for name in which:
        others += [partner("z", step) for step in range(1, depth)] if name == "z" else [partner(name)]
    barrier = pltpu.get_barrier_semaphore()
    for other in others:
        pl.semaphore_signal(barrier, inc=1, device_id=other, device_id_type=pl.DeviceIdType.MESH)
    pl.semaphore_wait(barrier, len(others))


def remote(source, target, sems, at, device):
    return pltpu.make_async_remote_copy(
        src_ref=source, dst_ref=target, send_sem=sems[0].at[at], recv_sem=sems[1].at[at],
        device_id=device, device_id_type=pl.DeviceIdType.MESH,
    )


def half_at(index, size):
    return pl.ds(pl.multiple_of(index * size, LANES), size)


class Across:
    copies = 4

    def __init__(self, first, second):
        (za, _, ra, ca), (zb, _, rb, cb) = first, second
        ca, cb = ca // 2, cb // 2
        self.sums = [(za, ra, ca), (zb, rb, cb)]
        self.scratch = [
            pltpu.VMEM((za, ra, 2 * ca), BF), pltpu.VMEM((za, ra, 2 * ca), BF), pltpu.VMEM((za, ra, ca), BF),
            pltpu.VMEM((zb, 2, rb, cb), BF), pltpu.VMEM((zb, 2, rb, cb), BF), pltpu.VMEM((zb, rb, cb), BF),
        ]

    def bind(self, ins, outs, scratch, sems, base):
        self.refs = list(ins) + list(outs) + list(scratch)
        self.sems, self.base = sems, base

    def copy(self, which):
        a, b, _, _, got_a, sum_a, last_a, got_b, sum_b, last_b = self.refs
        _, _, x, _, y = place()
        ca, cb = a.shape[3] // 2, b.shape[3] // 2
        at = self.base + which
        if which == 0:
            return remote(a.at[:, 1 - x], got_a, self.sems, at, partner("x"))
        if which == 1:
            return remote(b.at[:, :, :, half_at(1 - y, cb)], got_b, self.sems, at, partner("y"))
        if which == 2:
            return remote(sum_a.at[:, :, half_at(1 - y, ca)], last_a, self.sems, at, partner("y"))
        return remote(sum_b.at[:, 1 - x], last_b, self.sems, at, partner("x"))

    def start(self):
        self.copy(0).start()
        self.copy(1).start()

    def turn(self):
        a, b, _, _, got_a, sum_a, _, got_b, sum_b, _ = self.refs
        _, _, x, _, y = place()
        self.copy(0).wait()
        sum_a[...] = a[:, x] + got_a[...]
        self.copy(2).start()
        self.copy(1).wait()
        sum_b[...] = b[:, :, :, half_at(y, b.shape[3] // 2)] + got_b[...]
        self.copy(3).start()

    def finish(self):
        a, b, out_a, out_b, _, sum_a, last_a, _, sum_b, last_b = self.refs
        _, _, x, _, y = place()
        self.copy(2).wait()
        out_a[...] = sum_a[:, :, half_at(y, a.shape[3] // 2)] + last_a[...]
        self.copy(3).wait()
        out_b[...] = sum_b[:, x] + last_b[...]


PICKS = {
    "down": lambda z: (z % 2, z // 2),
    "up": lambda z: (slice(None), z),
    "flow": lambda z: (z,),
}


class Along:
    def __init__(self, depth, kinds, shapes):
        self.depth = depth
        self.picks = [PICKS[kind] for kind in kinds]
        drop = {"down": lambda shape: shape[2:], "up": lambda shape: shape[:1] + shape[2:], "flow": lambda shape: shape[1:]}
        self.sums = [drop[kind](shape) for kind, shape in zip(kinds, shapes)]
        self.scratch = [pltpu.VMEM((depth - 1,) + shape, BF) for shape in self.sums]
        self.copies = (depth - 1) * len(shapes)

    def bind(self, ins, outs, scratch, sems, base):
        self.ins, self.outs, self.got = ins, outs, scratch
        self.sems, self.base = sems, base

    def each(self):
        _, _, _, z, _ = place()
        for i, (source, got, pick) in enumerate(zip(self.ins, self.got, self.picks)):
            for step in range(1, self.depth):
                at = self.base + i * (self.depth - 1) + step - 1
                share = source.at[pick((z + step) % self.depth)]
                yield remote(share, got.at[step - 1], self.sems, at, partner("z", step))

    def start(self):
        for copy in self.each():
            copy.start()

    def finish(self):
        _, _, _, z, _ = place()
        for copy in self.each():
            copy.wait()
        for source, out, got, pick in zip(self.ins, self.outs, self.got, self.picks):
            total = source[pick(z)].astype(F32)
            for step in range(1, self.depth):
                total = total + got[step - 1].astype(F32)
            out[...] = total


def sems_for(count):
    return [pltpu.SemaphoreType.DMA((count,)), pltpu.SemaphoreType.DMA((count,))]


def take(refs, *counts):
    out = []
    at = 0
    for count in counts:
        out.append(refs[at : at + count])
        at += count
    assert at == len(refs), (at, len(refs))
    return out


def whole(shape):
    return pl.BlockSpec(shape, lambda *s: (0,) * len(shape))


VM = pl.BlockSpec(memory_space=pltpu.VMEM)
AN = pl.BlockSpec(memory_space=pl.ANY)
LIMIT = 62 * 2**20


def params(number=None):
    if number is None:
        return pltpu.CompilerParams(vmem_limit_bytes=LIMIT)
    return pltpu.CompilerParams(vmem_limit_bytes=LIMIT, collective_id=number, has_side_effects=True)


def lanes_of(group, size=LANES):
    return pl.ds(pl.multiple_of(group * size, size), size)


CHUNK = 512


def forward_kernel(layer, window, depth, *refs):
    masked = layer == 1
    tokens = window * window
    width = refs[0].shape[1]
    groups = width // LANES
    per = LANES // depth
    (
        x_refs, region_refs, (qv_ref, ob_ref, gain_ref, shift_ref, logit_ref, ub_ref, bias_ref),
        (wqkv, wp, wu, wd), (out_ref, send_ref), saved, keep, (z_s, m_s, qkv_s, scale_s, qm_s, km_s),
        (wqkv_s, wp_s, wu_s, wd_s), (load, store),
    ) = take(refs, 2 if masked else 1, 1 if masked else 0, 7, 4, 2, 14, 14, 6, 4, 2)
    chunks = ub_ref.shape[1] // CHUNK
    e_s, qn_s, kn_s, v_s, o_s, iq_s, ik_s, rinv_s, p_s, a_s, zr_s, g_s, gd_s, mo_s = keep
    lane = lax.broadcasted_iota(jnp.int32, (1, LANES), 1) // depth

    def load_qkv(i):
        return pltpu.make_async_copy(wqkv.at[layer, :, lanes_of(i, width)], wqkv_s.at[i], load.at[i])

    def load_rest(i):
        source, target = ((wp, wp_s), (wu, wu_s), (wd, wd_s))[i]
        return pltpu.make_async_copy(source.at[layer], target, load.at[3 + i])

    def put(i):
        return pltpu.make_async_copy(keep[i], saved[i], store.at[i])

    def put_p(g):
        rows = pl.ds(g * per, per)
        return pltpu.make_async_copy(p_s.at[rows], saved[8].at[rows], store.at[14 + g])

    def put_g(i, c):
        cols = lanes_of(c, CHUNK)
        return pltpu.make_async_copy(
            keep[11 + i].at[:, cols], saved[11 + i].at[:, cols], store.at[14 + groups + 2 * c + i]
        )

    for i in range(3):
        load_qkv(i).start()
    for i in range(3):
        load_rest(i).start()
    scale_s[...] = head_scales(logit_ref, layer, width) * LOG2E
    ones = group_ones(depth)
    if masked:
        token = lax.broadcasted_iota(jnp.int32, (tokens, window), 0)
        place_in_row = lax.broadcasted_iota(jnp.int32, (tokens, window), 1)
        rows_pick = jnp.where(token // window == place_in_row, 1.0, 0.0).astype(BF)
        labels = mm(rows_pick, region_refs[0][...].astype(F32).astype(BF))
        mine = column_of(token % window, window, True) == place_in_row
        labels = jnp.sum(jnp.where(mine, labels, 0.0), axis=1, keepdims=True)
        each = lax.broadcasted_iota(jnp.int32, (tokens, LANES), 1)
        same = labels == each.astype(F32)
        qm_s[...] = jnp.where(same, 1.0, 0.0).astype(BF)
        km_s[...] = jnp.where(same | (each >= 8), 0.0, -MASKED).astype(BF)
    half = tokens // 2
    if masked:
        z_s[:half] = x_refs[0][half:]
        z_s[half:] = x_refs[1][...].astype(F32)
        x_ref = z_s
    else:
        x_ref = x_refs[0]
    e_s[...] = x_ref[...].astype(BF)
    put(0).start()
    for i in range(3):
        load_qkv(i).wait()
        raw = mm(e_s[...], wqkv_s[i])
        if i != 1:
            raw = raw + qv_ref[layer, i // 2 : i // 2 + 1]
        qkv_s[i] = raw

    def group_step(g, carry):
        cols = lanes_of(g)
        q = qkv_s[0, :, cols]
        k = qkv_s[1, :, cols]
        v = qkv_s[2, :, cols]
        iq, ik = group_sums(ones, q * q, k * k)
        iq = lax.rsqrt(iq + 1e-06)
        ik = lax.rsqrt(ik + 1e-06)
        qn = q * iq
        kn = (k * ik).astype(BF)
        iq_s[:, cols] = iq
        ik_s[:, cols] = ik
        qn_s[:, cols] = qn.astype(BF)
        kn_s[:, cols] = kn
        v_s[:, cols] = v.astype(BF)
        scales = scale_s[:, cols]
        rhs = jnp.concatenate([kn, km_s[...]], axis=1) if masked else kn
        mixed = jnp.zeros((tokens, LANES), F32)
        total = mixed
        for h in range(per):
            mine = lane == h
            lhs = jnp.where(mine, qn, 0.0).astype(BF)
            if masked:
                lhs = jnp.concatenate([lhs, qm_s[...]], axis=1)
            cosine = mm_nt(lhs, rhs)
            scale = scales[:, h * depth : h * depth + 1]
            table = bias_ref[g * per + h]
            for pair in range(window // 2):
                parts = []
                for r in (2 * pair, 2 * pair + 1):
                    at = window * (window - 1 - r)
                    parts.append(
                        cosine[r * window : (r + 1) * window] * scale + table[:, at : at + tokens]
                    )
                both = jnp.concatenate(parts, axis=0)
                p_s[g * per + h, 2 * pair * window : (2 * pair + 2) * window, :] = jnp.exp2(both).astype(BF)
            both = mm(p_s[g * per + h], jnp.where(mine, v, 1.0).astype(BF))
            mixed = jnp.where(mine, both, mixed)
            total = jnp.where(lane == (h + 1) % per, both, total)
        rinv = pltpu.roll(1.0 / total, LANES - depth, 1)
        rinv_s[:, cols] = rinv
        o_s[:, cols] = mixed * rinv
        put_p(g).start()
        return carry

    lax.fori_loop(0, groups, group_step, 0)
    for i in range(1, 8):
        put(i).start()
    load_rest(0).wait()
    a = mm(o_s[...].astype(BF), wp_s[...]) + ob_ref[layer, 0:1]
    a_s[...] = a
    put(9).start()
    hat, _ = norm_stats(a)
    z = x_ref[...] + (hat * gain_ref[layer, 0:1] + shift_ref[layer, 0:1])
    z_s[...] = z
    zr_s[...] = z.astype(BF)
    put(10).start()
    m_s[...] = jnp.zeros_like(m_s)
    load_rest(1).wait()
    load_rest(2).wait()

    def chunk_step(c, carry):
        cols = lanes_of(c, CHUNK)
        pre = mm(zr_s[...], wu_s[:, cols]) + ub_ref[layer : layer + 1, cols]
        cdf, density = normal_parts(pre)
        act = (pre * cdf).astype(BF)
        g_s[:, cols] = act
        gd_s[:, cols] = (cdf + pre * density).astype(BF)
        put_g(0, c).start()
        put_g(1, c).start()
        m_s[...] += mm(act, wd_s[cols, :])
        return carry

    lax.fori_loop(0, chunks, chunk_step, 0)
    m = m_s[...] + ob_ref[layer, 1:2]
    mo_s[...] = m
    put(13).start()
    hat, _ = norm_stats(m)
    out = z_s[...] + (hat * gain_ref[layer, 1:2] + shift_ref[layer, 1:2])
    out_ref[...] = out
    send_ref[...] = (out[half:] if masked else out[:half]).astype(BF)
    for i in range(14):
        if i not in (8, 11, 12):
            put(i).wait()
    for g in range(groups):
        put_p(g).wait()
    for c in range(chunks):
        put_g(0, c).wait()
        put_g(1, c).wait()


def block_forward(layer, xs, region, vectors, table, weights, window, heads):
    tokens, width = window * window, xs[0].shape[1]
    depth = width // heads
    w_qkv, w_proj, w_up, w_down = weights
    ff = w_up.shape[2]
    groups = width // LANES
    sds = jax.ShapeDtypeStruct
    tok = lambda dt, cols=width: sds((tokens, cols), dt)
    saved = [
        tok(BF), tok(BF), tok(BF), tok(BF), tok(F32), tok(F32), tok(F32), tok(F32),
        sds((heads, tokens, tokens), BF), tok(F32), tok(BF), tok(BF, ff), tok(BF, ff), tok(F32),
    ]
    ins = list(xs) + list(region) + list(vectors) + [table]
    stores = 14 + groups + 2 * (ff // CHUNK)
    return pl.pallas_call(
        functools.partial(forward_kernel, layer, window, depth),
        in_specs=[VM] * len(ins) + [AN] * 4,
        out_specs=[VM] * 2 + [AN] * 14,
        out_shape=[tok(F32), sds((tokens // 2, width), BF)] + saved,
        scratch_shapes=[pltpu.VMEM(item.shape, item.dtype) for item in saved]
        + [
            pltpu.VMEM((tokens, width), F32), pltpu.VMEM((tokens, width), F32), pltpu.VMEM((3, tokens, width), F32),
            pltpu.VMEM((1, width), F32), pltpu.VMEM((tokens, LANES), BF), pltpu.VMEM((tokens, LANES), BF),
            pltpu.VMEM((3, width, width), BF), pltpu.VMEM((width, width), BF),
            pltpu.VMEM((width, ff), BF), pltpu.VMEM((ff, width), BF),
            pltpu.SemaphoreType.DMA((6,)), pltpu.SemaphoreType.DMA((stores,)),
        ],
        compiler_params=params(),
        name="block_forward_%d" % layer,
    )(*ins, w_qkv, w_proj, w_up, w_down)


UP_BIAS, QV, OUT_BIAS, GAIN, SHIFT, PLACE_IN, PLACE_BIAS, LOGIT, PLACE_OUT = 0, 4, 6, 8, 10, 12, 14, 15, 16
SMALL = 32


class Plan:
    def __init__(self, width, ff, images, follows):
        deep = images // 4
        self.deep = deep
        self.down = (2, deep // 2, 2, 2, ff // images, width)
        self.up = (2, deep, 2, 2, width // images, ff // 2)
        half = lambda shape: shape[:3] + shape[4:]
        self.half_down, self.half_up = half(self.down), half(self.up)
        self.flow = (deep, 2, 2, width // images, 2 * width)
        self.half_flow = self.flow[:2] + self.flow[3:]
        self.parts = [Across(self.half_down[1:], self.half_up[1:]) for _ in range(2)]
        sums = [(2,) + shape for shape in self.parts[0].sums]
        self.outs = [(shape, BF) for shape in sums] + [(self.half_flow, BF)] * 2
        self.scratch = [pltpu.VMEM(shape, BF) for shape in (
            self.down, self.up, self.half_down, self.half_up, self.flow, self.flow, self.half_flow, self.half_flow,
        )] + self.parts[0].scratch + self.parts[1].scratch
        self.core = 8 + 14
        self.copies = self.core + 8
        self.ins = []
        self.follows = follows
        if follows:
            self.old = Along(deep, ("down", "up"), sums)
            self.turned = Across(self.half_flow, self.half_flow)
            self.late = Along(deep, ("flow", "flow"), self.turned.sums)
            self.ins = sums + [self.half_flow] * 2
            self.outs += [(shape, F32) for shape in self.old.sums + self.late.sums]
            self.scratch += [pltpu.VMEM(shape, BF) for shape in self.turned.sums]
            self.scratch += self.old.scratch + self.turned.scratch + self.late.scratch
            self.copies += self.old.copies + self.turned.copies + self.late.copies
        self.scratch = self.scratch + sems_for(self.copies)

    def bind(self, ins, outs, scratch):
        sems = scratch[-2:]
        self.sems = sems
        self.down_s, self.up_s, self.got_down, self.got_up = scratch[:4]
        self.flows = ((scratch[4], scratch[6]), (scratch[5], scratch[7]))
        self.flow_outs = outs[2:4]
        for c, part in enumerate(self.parts):
            part.bind(
                [self.got_down.at[c], self.got_up.at[c]], [outs[0].at[c], outs[1].at[c]],
                scratch[8 + 6 * c : 14 + 6 * c], sems, self.core + 4 * c,
            )
        if self.follows:
            rest = scratch[20:-2]
            at = self.core + 8
            between, old, turned, late = take(rest, 2, 2, 6, 2)
            self.old.bind(ins[:2], outs[4:6], old, sems, at)
            at += self.old.copies
            self.turned.bind(ins[2:4], between, turned, sems, at)
            at += self.turned.copies
            self.late.bind(between, outs[6:8], late, sems, at)

    def feed_copy(self, c, i, which):
        _, core, _, _, _ = place()
        at = 4 * c + 2 * i + which
        if which == 0:
            return remote(
                self.down_s.at[c, i, :, 1 - core], self.got_down.at[c, i], self.sems, at, partner("core")
            )
        cols = pl.ds(i * CHUNK, CHUNK)
        return remote(
            self.up_s.at[c, :, :, 1 - core, :, cols], self.got_up.at[c, :, :, :, cols], self.sems, at, partner("core"),
        )

    def flow_copy(self, flow, cols, at):
        _, core, _, _, _ = place()
        source, target = self.flows[flow]
        return remote(
            source.at[:, :, 1 - core, :, cols], target.at[:, :, :, cols], self.sems, 8 + at, partner("core")
        )

    def begin(self):
        greet(["core", "x", "y"] + (["z"] if self.follows else []))
        if self.follows:
            self.turned.start()
            self.old.start()

    def feed_step(self, c, down, up):
        for i in range(2):
            rows = slice(i * CHUNK, (i + 1) * CHUNK)
            self.down_s[c, i] = down[rows].reshape(self.down[2:])
            self.up_s[c, :, :, :, :, rows] = up[:, rows].reshape(self.up[1:5] + (CHUNK,))
            self.feed_copy(c, i, 0).start()
            self.feed_copy(c, i, 1).start()

    def ready(self, c):
        _, core, _, _, _ = place()
        for i in range(2):
            for which in range(2):
                self.feed_copy(c, i, which).wait()
        self.got_down[c] = self.got_down[c] + self.down_s[c, :, :, core]
        self.got_up[c] = self.got_up[c] + self.up_s[c, :, :, core]
        self.parts[c].start()

    def midway(self):
        self.ready(0)

    def between(self, proj):
        flow_b = self.flows[1][0]
        half = proj.shape[1] // 2
        for i in range(2):
            cols = pl.ds(i * 512 + 256, half)
            flow_b[:, :, :, :, cols] = proj[:, i * half : (i + 1) * half].reshape(flow_b.shape[:4] + (half,))
            self.flow_copy(1, cols, 12 + i).start()
        self.ready(1)
        if self.follows:
            self.turned.turn()
            self.old.finish()
        self.parts[0].turn()

    def attend_begin(self, half):
        @pl.when(half == 1)
        def _():
            self.parts[1].turn()
            if self.follows:
                self.turned.finish()
                self.late.start()

    def attend_step(self, g, grads):
        groups = 4

        def put(i, flow, at):
            source = self.flows[flow][0]
            cols = lanes_of(at)
            block = grads[:, i * LANES : (i + 1) * LANES]
            source[:, :, :, :, cols] = block.reshape(source.shape[:4] + (LANES,))
            self.flow_copy(flow, cols, 3 * g + i).start()

        put(0, 0, g)

        @pl.when(g < groups // 2)
        def _():
            put(1, 1, g)
            put(2, 0, 6 + g)

        @pl.when(g >= groups // 2)
        def _():
            put(1, 0, 2 + g)
            put(2, 1, 2 + g)

    def end(self):
        _, core, _, _, _ = place()
        groups = 4
        self.parts[0].finish()
        for g in range(groups):
            for i in range(3):
                flow = 0 if i == 0 or (i == 1) == (g >= groups // 2) else 1
                self.flow_copy(flow, pl.ds(0, LANES), 3 * g + i).wait()
        for i in range(2):
            self.flow_copy(1, pl.ds(i * 512 + 256, 256), 12 + i).wait()
        for (source, got), out in zip(self.flows, self.flow_outs):
            for z in range(source.shape[0]):
                out[z] = source[z, :, core] + got[z]
        if self.follows:
            self.late.finish()
        self.parts[1].finish()


def backward_kernel(layer, window, depth, plan, *refs):
    tokens = window * window
    half = tokens // 2
    n_plan_in = len(plan.ins) if plan else 0
    n_plan_out = len(plan.outs) if plan else 4
    n_plan_scratch = len(plan.scratch) if plan else 0
    (
        (own_ref, in_ref, gain_ref, logit_ref), plan_ins, saved, (wqkv, wp, wu, wd),
        (dx_ref, send_ref, sums_ref, table_ref), plan_outs, keep,
        (wqkv_s, wp_s, wu_s, wd_s, dm_s, do_s, et_s, ds_s, scale_s, load), plan_scratch,
    ) = take(refs, 4, n_plan_in, 14, 4, 4, n_plan_out, 14, 10, n_plan_scratch)
    e_s, qn_s, kn_s, v_s, o_s, iq_s, ik_s, rinv_s, p_s, a_s, zr_s, g_s, gd_s, m_s = keep
    width = own_ref.shape[1]
    ff = g_s.shape[1]
    groups = width // LANES
    per = LANES // depth
    chunks = ff // CHUNK
    wide = tokens
    lane = lax.broadcasted_iota(jnp.int32, (1, LANES), 1)

    def load_kept(i):
        return pltpu.make_async_copy(saved[i], keep[i], load.at[i])

    def load_p(g):
        return pltpu.make_async_copy(saved[8].at[pl.ds(g * per, per)], p_s.at[g % 2], load.at[14 + g])

    def load_weights(i):
        source, target = ((wqkv, wqkv_s), (wp, wp_s))[i]
        return pltpu.make_async_copy(source.at[layer], target, load.at[14 + groups + i])

    def load_chunk(c):
        here = lanes_of(c, CHUNK)
        cols = lanes_of(c // 2 + c % 2 * 2, CHUNK)
        at = 16 + groups + 4 * c
        return [
            pltpu.make_async_copy(saved[11].at[:, cols], g_s.at[:, here], load.at[at]),
            pltpu.make_async_copy(saved[12].at[:, cols], gd_s.at[:, here], load.at[at + 1]),
            pltpu.make_async_copy(wd.at[layer, cols], wd_s.at[here], load.at[at + 2]),
            pltpu.make_async_copy(wu.at[layer, :, cols], wu_s.at[:, here], load.at[at + 3]),
        ]

    load_kept(13).start()
    load_kept(10).start()
    for c in range(chunks):
        for copy in load_chunk(c):
            copy.start()
    load_kept(9).start()
    load_kept(4).start()
    load_weights(1).start()
    if plan:
        plan.bind(plan_ins, plan_outs, plan_scratch)
        plan.begin()
    if layer == 1:
        dx_ref[:half] = own_ref[half:]
        dx_ref[half:] = in_ref[...].astype(F32)
    else:
        dx_ref[:half] = in_ref[...].astype(F32)
        dx_ref[half:] = own_ref[:half]
    scale_s[...] = head_scales(logit_ref, layer, width)
    ones = group_ones(depth)
    load_kept(13).wait()
    dm, gain_grad, shift_grad = norm_pull(m_s[...], gain_ref[layer, 1:2], dx_ref[...])
    low = dm.astype(BF)
    dm_s[...] = low
    sums_ref[...] = jnp.zeros_like(sums_ref)
    sums_ref[OUT_BIAS + 1 : OUT_BIAS + 2] = jnp.sum(low.astype(F32), axis=0, keepdims=True)
    sums_ref[GAIN + 1 : GAIN + 2] = gain_grad
    sums_ref[SHIFT + 1 : SHIFT + 2] = shift_grad
    load_kept(10).wait()

    for c in range(chunks // 2):
        for i in range(2):
            for copy in load_chunk(2 * c + i):
                copy.wait()
        if c == 0:
            for i in (0, 1, 2, 3, 5, 6, 7):
                load_kept(i).start()
            load_p(0).start()
            load_weights(0).start()
            load_p(1).start()
        cols = slice(2 * c * CHUNK, (2 * c + 2) * CHUNK)
        dm = dm_s[...]
        dh = (mm_nt(dm, wd_s[cols]) * gd_s[:, cols].astype(F32)).astype(BF)
        if plan and c == 1:
            plan.midway()
        up = mm_tn(zr_s[...], dh).astype(BF)
        down = mm_tn(g_s[:, cols], dm).astype(BF)
        bias_grad = jnp.sum(dh.astype(F32), axis=0, keepdims=True)
        for i in range(2):
            sums_ref[UP_BIAS + c + 2 * i : UP_BIAS + c + 2 * i + 1] = bias_grad[:, i * CHUNK : (i + 1) * CHUNK]
        if plan:
            plan.feed_step(c, down, up)
        else:
            for i in range(2):
                out_cols = slice((c + 2 * i) * CHUNK, (c + 2 * i + 1) * CHUNK)
                plan_outs[0][out_cols] = down[i * CHUNK : (i + 1) * CHUNK]
                plan_outs[1][:, out_cols] = up[:, i * CHUNK : (i + 1) * CHUNK]
        dx_ref[...] += mm_nt(dh, wu_s[:, cols])
    load_kept(9).wait()
    load_kept(4).wait()
    load_weights(1).wait()
    da, gain_grad, shift_grad = norm_pull(a_s[...], gain_ref[layer, 0:1], dx_ref[...])
    low = da.astype(BF)
    sums_ref[OUT_BIAS : OUT_BIAS + 1] = jnp.sum(low.astype(F32), axis=0, keepdims=True)
    sums_ref[GAIN : GAIN + 1] = gain_grad
    sums_ref[SHIFT : SHIFT + 1] = shift_grad
    proj = mm_tn(o_s[...].astype(BF), low).astype(BF)
    do_s[...] = mm_nt(low, wp_s[...]).astype(BF)
    if plan:
        plan.between(proj)
    else:
        plan_outs[2][...] = proj
    for i in (0, 1, 2, 3, 5, 6, 7):
        load_kept(i).wait()
    load_weights(0).wait()
    et_s[...] = e_s[...].T

    def one_group(g, slot):
        cols = lanes_of(g)
        load_p(g).wait()
        scale = scale_s[:, cols]
        v = v_s[:, cols]
        kn = kn_s[:, cols]
        qn = qn_s[:, cols]
        dor = (do_s[:, cols].astype(F32) * rinv_s[:, cols]).astype(BF)
        dor32 = dor.astype(F32)
        less = -group_sum(ones, dor32 * o_s[:, cols])
        high = less.astype(BF).astype(F32)
        extra = jnp.where(lane % depth == 0, high, jnp.where(lane % depth == 1, less - high, 0.0))
        extra = pltpu.roll(extra, depth, 1)
        dor_t = dor.T
        qn_t = qn.T
        v32 = v.astype(F32)
        kn32 = kn.astype(F32)
        qn32 = qn.astype(F32)
        dq = jnp.zeros((tokens, LANES), F32)
        dk_t = []
        dv_t = []
        for h in range(per):
            mine = lane // depth == h
            after = lane // depth == (h + 1) % per
            lhs = jnp.where(mine, dor32, jnp.where(after, extra, 0.0)).astype(BF)
            t = mm_nt(lhs, jnp.where(mine, v32, 1.0).astype(BF))
            head = g * per + h
            table_ref[head] = jnp.zeros(table_ref.shape[1:], F32)
            for pair in range(window // 2):
                rows = slice(2 * pair * window, (2 * pair + 2) * window)
                ds = p_s[slot, h, rows, :].astype(F32) * t[rows]
                ds_s[h % 2, rows, :] = ds.astype(BF)
                for i in range(2):
                    at = window * (window - 1 - (2 * pair + i))
                    table_ref[head, :, at : at + tokens] += ds[i * window : (i + 1) * window]
            low = ds_s[h % 2]
            dq = dq + mm(low, jnp.where(mine, kn32, 0.0).astype(BF))
            dk_t.append(mm(qn_t[h * depth : (h + 1) * depth], low))
            dv_t.append(mm(dor_t[h * depth : (h + 1) * depth], p_s[slot, h]))

        @pl.when(g + 2 < groups)
        def _():
            load_p(g + 2).start()

        dqn = dq * scale
        dkn = jnp.concatenate(dk_t, axis=0).T * scale
        dv = jnp.concatenate(dv_t, axis=0).T
        along_q = qn32 * dqn
        sum_q, sum_k = group_sums(ones, along_q, kn32 * dkn)
        dq = iq_s[:, cols] * (dqn - qn32 * sum_q)
        dk = ik_s[:, cols] * (dkn - kn32 * sum_k)
        sums_ref[LOGIT : LOGIT + 1, cols] = jnp.sum(along_q, axis=0, keepdims=True)
        parts = [part.astype(BF) for part in (dq, dk, dv)]
        sums_ref[QV : QV + 1, cols] = jnp.sum(parts[0].astype(F32), axis=0, keepdims=True)
        sums_ref[QV + 1 : QV + 2, cols] = jnp.sum(parts[2].astype(F32), axis=0, keepdims=True)
        return parts

    def group_step(j, carry):
        if plan:
            plan.attend_begin(j)
        parts = one_group(2 * j, 0) + one_group(2 * j + 1, 1)
        low = jnp.concatenate(parts, axis=1)
        grads = mm(et_s[...], low).astype(BF)
        if plan:
            plan.attend_step(2 * j, grads[:, : 3 * LANES])
            plan.attend_step(2 * j + 1, grads[:, 3 * LANES :])
        else:
            for i in range(6):
                plan_outs[3][i % 3, :, lanes_of(2 * j + i // 3)] = grads[:, i * LANES : (i + 1) * LANES]
        weights = jnp.concatenate(
            [wqkv_s[:, lanes_of(i % 3 * groups + 2 * j + i // 3)] for i in range(6)], axis=1
        )
        dx_ref[...] += mm_nt(low, weights)
        return carry

    lax.fori_loop(0, groups // 2, group_step, 0)
    if layer == 1:
        send_ref[...] = dx_ref[half:].astype(BF)
    else:
        send_ref[...] = jnp.zeros_like(send_ref)
    if plan:
        plan.end()


def block_backward(layer, own, incoming, gain, logits, saved, weights, table_shape, window, heads, riding, left):
    tokens, width = own.shape
    depth = width // heads
    ff = saved[11].shape[1]
    groups = width // LANES
    per = LANES // depth
    sds = jax.ShapeDtypeStruct
    plan = Plan(width, ff, lax.axis_size("img"), bool(left)) if riding else None
    plan_ins = list(left)
    if riding:
        plan_outs = [sds(shape, dt) for shape, dt in plan.outs]
        plan_scratch = plan.scratch
    else:
        plan_outs = [sds((ff, width), BF), sds((width, ff), BF), sds((width, width), BF), sds((3, width, width), BF)]
        plan_scratch = []
    keep = [pltpu.VMEM(item.shape, item.dtype) for item in saved]
    keep[8] = pltpu.VMEM((2, per, tokens, tokens), BF)
    return pl.pallas_call(
        functools.partial(backward_kernel, layer, window, depth, plan),
        in_specs=[VM] * (4 + len(plan_ins)) + [AN] * 18,
        out_specs=[VM] * (4 + len(plan_outs)),
        out_shape=[
            sds((tokens, width), F32), sds((tokens // 2 if layer == 1 else 16, width), BF), sds((16, width), F32),
            sds(table_shape, F32),
        ] + plan_outs,
        scratch_shapes=keep
        + [
            pltpu.VMEM((width, 3 * width), BF), pltpu.VMEM((width, width), BF),
            pltpu.VMEM((width, ff), BF), pltpu.VMEM((ff, width), BF),
            pltpu.VMEM((tokens, width), BF), pltpu.VMEM((tokens, width), BF), pltpu.VMEM((width, tokens), BF),
            pltpu.VMEM((2, tokens, tokens), BF), pltpu.VMEM((1, width), F32),
            pltpu.SemaphoreType.DMA((16 + groups + 4 * (ff // CHUNK),)),
        ]
        + plan_scratch,
        compiler_params=params(2 - layer if riding else None),
        name="block_backward_%d" % layer,
    )(own, incoming, gain, logits, *plan_ins, *saved, *weights)


def entry_logs(first, count, window):
    at = first + lax.broadcasted_iota(jnp.int32, (8, count), 1)
    row = at // (2 * window)
    col = at % (2 * window)
    real = (row < 2 * window - 1) & (col < 2 * window - 1)

    def logs(offset):
        size = jnp.log2(jnp.abs(offset).astype(F32) * (8.0 / (window - 1)) + 1.0) / 3.0
        return jnp.where(offset < 0, -size, size)

    by_row = jnp.where(real, logs(window - 1 - row), 0.0)
    by_col = jnp.where(real, logs(col - (window - 1)), 0.0)
    return by_row, by_col


def column_of(token_col, window, shifted):
    if not shifted:
        return token_col
    return jnp.where(token_col >= window // 2, token_col - window // 2, token_col + window // 2)


def slopes(rel_ref, window):
    first = rel_ref[0:1, 0:1]
    down = rel_ref[window : window + 1, 0:1] - first
    across = rel_ref[1:2, 0:1] - first
    straight = jnp.abs(down) == 2 * window - 1
    sign = lambda step: jnp.where(step > 0, 1.0, -1.0)
    return straight, sign(down), sign(across)


TABLE_CHUNK = 768


def table_kernel(
    layer, window, in_ref, bias_ref, outw_ref, rel, rows_ref, tab_ref, hid_out, slope_out,
    hid_s, slope_s, w_s, rel_ref, sems,
):
    fetch = pltpu.make_async_copy(rel.at[pl.ds(0, rel_ref.shape[0]), pl.ds(0, LANES)], rel_ref, sems.at[0])
    fetch.start()
    fetch.wait()
    shifted = layer == 1
    heads, entries = tab_ref.shape
    straight, down, across = slopes(rel_ref, window)
    first, second = in_ref[layer, 0:1], in_ref[layer, 1:2]
    by_rows = jnp.where(straight, first, second) * down
    by_cols = jnp.where(straight, second, first) * across
    w_s[...] = jnp.concatenate(
        [by_rows, by_cols, bias_ref[layer : layer + 1], jnp.zeros((LANES - 3, by_rows.shape[1]), F32)], axis=0
    ).T
    out_high, out_low = split(outw_ref[layer])
    both_w = jnp.concatenate([out_high, out_low], axis=0)

    def put(i, c):
        cols = lanes_of(c, TABLE_CHUNK)
        source, target = ((hid_s, hid_out), (slope_s, slope_out))[i]
        return pltpu.make_async_copy(source.at[:, cols], target.at[:, cols], sems.at[2 * c + i])

    def chunk_step(c, carry):
        cols = lanes_of(c, TABLE_CHUNK)
        by_row, by_col = entry_logs(c * TABLE_CHUNK, TABLE_CHUNK, window)
        pre = w_s[:, 0:1] * by_row[0:1] + w_s[:, 1:2] * by_col[0:1] + w_s[:, 2:3]
        cdf, density = normal_parts(pre)
        hidden, rest = split(pre * cdf)
        hid_s[:, cols] = hidden
        slope_s[:, cols] = (cdf + pre * density).astype(BF)
        put(0, c).start()
        put(1, c).start()
        both = mm(both_w, hidden)
        logits = both[:heads] + both[heads:] + mm(out_high, rest)
        tab_ref[:, cols] = 16.0 / (1.0 + jnp.exp(-logits))
        return carry

    steps = entries // TABLE_CHUNK
    lax.fori_loop(0, steps, chunk_step, 0)
    spans = entries // LANES
    wide = rows_ref.shape[2]
    row8 = lax.broadcasted_iota(jnp.int32, (8, LANES), 0)
    lane = lax.broadcasted_iota(jnp.int32, (8, LANES), 1)
    for k in range(wide // LANES):
        at = lane + LANES * k
        low = 2 * window * (LANES * k // window) // LANES
        high = min((2 * window * ((LANES * k + LANES - 1) // window) + 2 * window - 2) // LANES, spans - 1)
        picks = []
        for tile in range(window // 8):
            c1 = column_of(row8 + 8 * tile, window, shifted)
            source = 2 * window * (at // window) + c1 - column_of(at % window, window, shifted) + window - 1
            for s in range(low, high + 1):
                near = source - s * LANES
                inside = (near >= 0) & (near < LANES)
                picks.append((inside, jnp.where(inside, near, 0)))
        for h in range(heads):
            for tile in range(window // 8):
                got = jnp.zeros((8, LANES), F32)
                for s in range(low, high + 1):
                    piece = jnp.broadcast_to(tab_ref[h : h + 1, s * LANES : (s + 1) * LANES], (8, LANES))
                    inside, near = picks[tile * (high + 1 - low) + s - low]
                    got = jnp.where(inside, jnp.take_along_axis(piece, near, axis=1), got)
                rows_ref[h, 8 * tile : 8 * tile + 8, k * LANES : (k + 1) * LANES] = got * LOG2E
    for c in range(steps):
        put(0, c).wait()
        put(1, c).wait()


def bias_table(layer, rel, place_in, place_bias, place_out, window):
    _, heads, hidden = place_out.shape
    entries = 4 * window * window
    wide = ((2 * window - 1) * window + LANES - 1) // LANES * LANES
    sds = jax.ShapeDtypeStruct
    return pl.pallas_call(
        functools.partial(table_kernel, layer, window),
        in_specs=[VM] * 3 + [AN],
        out_specs=[VM] * 2 + [AN] * 2,
        out_shape=[
            sds((heads, window, wide), F32), sds((heads, entries), F32),
            sds((hidden, entries), BF), sds((hidden, entries), BF),
        ],
        scratch_shapes=[
            pltpu.VMEM((hidden, entries), BF), pltpu.VMEM((hidden, entries), BF), pltpu.VMEM((hidden, LANES), F32),
            pltpu.VMEM((32, LANES), jnp.int32),
            pltpu.SemaphoreType.DMA((2 * (entries // TABLE_CHUNK),)),
        ],
        compiler_params=params(),
        name="bias_table_%d" % layer,
    )(place_in, place_bias, place_out, rel)


class Tail:
    def __init__(self, depth, shapes):
        down, up, flow_a, flow_b, small = shapes
        self.depth = depth
        self.ins = list(shapes)
        self.along = Along(depth, ("down", "up"), [down, up])
        self.across = Across(flow_a, flow_b)
        self.after = Along(depth, ("flow", "flow"), self.across.sums)
        every = (2 * small[0],) + small[1:]
        piece = (every[0] // 8,) + small[1:]
        self.outs = [(shape, F32) for shape in self.along.sums + self.after.sums + [every]]
        self.small = 7 + depth - 1 + 7
        self.copies = self.along.copies + self.across.copies + self.after.copies + self.small
        self.scratch = (
            self.along.scratch + self.across.scratch + self.after.scratch
            + [pltpu.VMEM(shape, BF) for shape in self.across.sums]
            + [
                pltpu.VMEM(every, F32), pltpu.VMEM((7,) + piece, F32), pltpu.VMEM((depth - 1,) + piece, F32),
                pltpu.VMEM((7,) + piece, F32), pltpu.VMEM(piece, F32), pltpu.VMEM(piece, F32),
            ]
            + sems_for(self.copies)
        )

    def bind(self, ins, outs, scratch):
        along, across, after, between, small, sems = take(scratch, 2, 6, 2, 2, 6, 2)
        self.other_small, self.out_small, self.sems = ins[4], outs[4], sems
        self.all_s, self.got, self.deep_got, self.back, self.part, self.total = small
        at = 0
        self.along.bind(ins[:2], outs[:2], along, sems, at)
        at += self.along.copies
        self.across.bind(ins[2:4], between, across, sems, at)
        at += self.across.copies
        self.after.bind(between, outs[2:4], after, sems, at)
        self.at = at + self.after.copies

    def fellow(self, step):
        me, core, x, z, y = place()
        other = (core + 2 * x + 4 * y + step) % 8
        return (4 * z + other % 4, other // 4)

    def mine(self, step=0):
        _, core, x, _, y = place()
        return (core + 2 * x + 4 * y + step) % 8

    def rows(self, which):
        size = self.part.shape[0]
        return pl.ds(pl.multiple_of(which * size, size), size)

    def scatter(self, step):
        return remote(
            self.all_s.at[self.rows(self.mine(step))], self.got.at[step - 1], self.sems, self.at + step - 1,
            self.fellow(step),
        )

    def deep(self, step):
        return remote(self.part, self.deep_got.at[step - 1], self.sems, self.at + 6 + step, partner("z", step))

    def gather(self, step):
        return remote(
            self.total, self.back.at[step - 1], self.sems, self.at + 6 + self.depth - 1 + step, self.fellow(step)
        )

    def begin(self):
        barrier = pltpu.get_barrier_semaphore()
        others = [self.fellow(step) for step in range(1, 8)]
        others += [partner("z", step) for step in range(1, self.depth)]
        for other in others:
            pl.semaphore_signal(barrier, inc=1, device_id=other, device_id_type=pl.DeviceIdType.MESH)
        pl.semaphore_wait(barrier, len(others))
        self.across.start()
        self.along.start()

    def end(self, small_ref):
        count = small_ref.shape[0]
        self.all_s[:count] = small_ref[...]
        self.all_s[count:] = self.other_small[...]
        for step in range(1, 8):
            self.scatter(step).start()
        self.across.turn()
        self.along.finish()
        part = self.all_s[self.rows(self.mine())]
        for step in range(1, 8):
            self.scatter(step).wait()
            part = part + self.got[step - 1]
        self.part[...] = part
        for step in range(1, self.depth):
            self.deep(step).start()
        self.across.finish()
        self.after.start()
        for step in range(1, self.depth):
            self.deep(step).wait()
            part = part + self.deep_got[step - 1]
        self.total[...] = part
        for step in range(1, 8):
            self.gather(step).start()
        self.out_small[self.rows(self.mine())] = part
        for step in range(1, 8):
            self.gather(step).wait()
            self.out_small[self.rows(self.mine(8 - step))] = self.back[step - 1]
        self.after.finish()


def table_back_kernel(layer, window, tail, *refs):
    n_in, n_out, n_scratch = (len(tail.ins), len(tail.outs), len(tail.scratch)) if tail else (0, 0, 0)
    (
        (rows_ref, tab_ref, outw_ref, sums_ref), tail_ins, (hid_in, slope_in, rel), (small_ref,), tail_outs,
        (hid_s, slope_s, dlog_s, rel_ref, sems), tail_scratch,
    ) = take(refs, 4, n_in, 3, 1, n_out, 5, n_scratch)
    shifted = layer == 1
    heads, entries = tab_ref.shape
    hidden = hid_s.shape[0]
    steps = entries // TABLE_CHUNK

    def get(i, c):
        cols = lanes_of(c, TABLE_CHUNK)
        source, target = ((hid_in, hid_s), (slope_in, slope_s))[i]
        return pltpu.make_async_copy(source.at[:, cols], target.at[:, cols], sems.at[2 * c + i])

    fetch = pltpu.make_async_copy(rel.at[pl.ds(0, rel_ref.shape[0]), pl.ds(0, LANES)], rel_ref, sems.at[2 * steps])
    fetch.start()
    for c in range(steps):
        get(0, c).start()
        get(1, c).start()
    if tail:
        tail.bind(tail_ins, tail_outs, tail_scratch)
        tail.begin()
    spans = rows_ref.shape[2] // LANES
    row8 = lax.broadcasted_iota(jnp.int32, (8, LANES), 0)
    lane = lax.broadcasted_iota(jnp.int32, (8, LANES), 1)
    for k in range(entries // LANES):
        at = lane + LANES * k
        m = at // (2 * window)
        d = at % (2 * window)
        sums = [jnp.zeros((8, LANES), F32) for _ in range(heads)]
        for tile in range(window // 8):
            c1 = column_of(row8 + 8 * tile, window, shifted)
            c2 = c1 - d + window - 1
            real = (c2 >= 0) & (c2 < window) & (m < 2 * window - 1)
            source = window * m + column_of(c2, window, shifted)
            low = window * (LANES * k // (2 * window)) // LANES
            high = min((window * ((LANES * k + LANES - 1) // (2 * window)) + window - 1) // LANES, spans - 1)
            for s in range(low, high + 1):
                near = source - s * LANES
                inside = (near >= 0) & (near < LANES) & real
                near = jnp.where(inside, near, 0)
                for h in range(heads):
                    piece = rows_ref[h, 8 * tile : 8 * tile + 8, s * LANES : (s + 1) * LANES]
                    picked = jnp.take_along_axis(piece, near, axis=1)
                    sums[h] = sums[h] + jnp.where(inside, picked, 0.0)
        for h in range(heads):
            dlog_s[h : h + 1, k * LANES : (k + 1) * LANES] = jnp.sum(sums[h], axis=0, keepdims=True)
    tab = tab_ref[...]
    dlog_s[...] = dlog_s[...] * tab * (1.0 - tab * 0.0625)
    out_high, out_low = split(outw_ref[layer])
    weights = jnp.concatenate([out_high, out_low, out_high], axis=0)

    def chunk_step(c, carry):
        grads, outs = carry
        cols = lanes_of(c, TABLE_CHUNK)
        by_row, by_col = entry_logs(c * TABLE_CHUNK, TABLE_CHUNK, window)
        low, rest = split(dlog_s[:, cols])
        get(0, c).wait()
        get(1, c).wait()
        outs = outs + mm_nt(jnp.concatenate([low, rest], axis=0), hid_s[:, cols])
        dhid = mm_tn(weights, jnp.concatenate([low, low, rest], axis=0))
        dpre, spare = split(dhid * slope_s[:, cols].astype(F32))
        which = lax.broadcasted_iota(jnp.int32, (16, TABLE_CHUNK), 0)
        pick = lambda y: jnp.broadcast_to(y[0:1], (16, TABLE_CHUNK))
        high_row = by_row.astype(BF).astype(F32)
        high_col = by_col.astype(BF).astype(F32)
        factors = jnp.where(which == 0, pick(high_row), 0.0)
        factors = jnp.where(which == 1, pick(high_col), factors)
        factors = jnp.where(which == 2, 1.0, factors)
        factors = jnp.where(which == 3, pick(by_row - high_row), factors)
        factors = jnp.where(which == 4, pick(by_col - high_col), factors)
        factors = factors.astype(BF)
        grads = grads + mm_nt(factors, dpre) + mm_nt(factors, spare)
        return grads, outs

    grads, outs = lax.fori_loop(
        0, steps, chunk_step, (jnp.zeros((16, hidden), F32), jnp.zeros((2 * heads, hidden), F32))
    )
    fetch.wait()
    straight, down, across = slopes(rel_ref, window)
    by_rows = (grads[0:1] + grads[3:4]) * down
    by_cols = (grads[1:2] + grads[4:5]) * across
    small_ref[:PLACE_OUT] = sums_ref[...]
    small_ref[PLACE_IN : PLACE_IN + 1] = jnp.where(straight, by_rows, by_cols)
    small_ref[PLACE_IN + 1 : PLACE_IN + 2] = jnp.where(straight, by_cols, by_rows)
    small_ref[PLACE_BIAS : PLACE_BIAS + 1] = grads[2:3]
    small_ref[PLACE_OUT:] = outs[:heads] + outs[heads:]
    if tail:
        tail.end(small_ref)


def bias_table_backward(layer, rel, rows, net, place_out, sums, window, left):
    tab, hid, slope = net
    heads, entries = tab.shape
    hidden = hid.shape[0]
    tail = Tail(lax.axis_size("img") // 4, [item.shape for item in left]) if left else None
    sds = jax.ShapeDtypeStruct
    return pl.pallas_call(
        functools.partial(table_back_kernel, layer, window, tail),
        in_specs=[VM] * (4 + len(left)) + [AN] * 3,
        out_specs=[VM] * (1 + (len(tail.outs) if tail else 0)),
        out_shape=[sds((SMALL, hidden), F32)] + ([sds(shape, dt) for shape, dt in tail.outs] if tail else []),
        scratch_shapes=[
            pltpu.VMEM((hidden, entries), BF), pltpu.VMEM((hidden, entries), BF), pltpu.VMEM((heads, entries), F32),
            pltpu.VMEM((32, LANES), jnp.int32), pltpu.SemaphoreType.DMA((2 * (entries // TABLE_CHUNK) + 1,)),
        ] + (tail.scratch if tail else []),
        compiler_params=params(3 if tail else None),
        name="bias_table_backward_%d" % layer,
    )(rows, tab, place_out, sums, *left, hid, slope, rel)


def final_kernel(window, depth, split_matrices, *refs):
    (
        (out_ref, in_ref, dx_ref, small_ref), matrices,
        (
            output, input_grad, qkv_grad, qv_grad, scale_grad, place_in_grad, place_bias_grad, place_out_grad,
            proj_grad, up_grad, up_bias_grad, down_grad, out_bias_grad, gain_grad, shift_grad,
        ),
    ) = take(refs, 4, len(refs) - 19, 15)
    half = out_ref.shape[0] // 2
    width = out_ref.shape[1]
    output[:half] = in_ref[...].astype(F32)
    output[half:] = out_ref[:half]
    input_grad[...] = dx_ref[...]
    small = small_ref
    wide = width // 2
    for b in range(2):
        if split_matrices:
            down, up, flow_a, flow_b = matrices[4 * b : 4 * b + 4]
            qkv_grad[b, :, :width] = flow_a[...]
            qkv_grad[b, :, width:] = flow_b[:, :wide]
            proj_grad[b] = flow_b[:, wide:]
            part = up.shape[2]
            for c in range(2):
                up_grad[b, :, c * part : (c + 1) * part] = up[c]
        else:
            qkv, proj, up, down = matrices[4 * b : 4 * b + 4]
            qkv_grad[b] = qkv[...]
            proj_grad[b] = proj[...]
            up_grad[b] = up[...]
        down_grad[b] = down[...]
        at = b * SMALL
        for i in range(4):
            up_bias_grad[b : b + 1, i * width : (i + 1) * width] = small[at + UP_BIAS + i : at + UP_BIAS + i + 1]
        qv_grad[b] = small[at + QV : at + QV + 2]
        out_bias_grad[b] = small[at + OUT_BIAS : at + OUT_BIAS + 2]
        gain_grad[b] = small[at + GAIN : at + GAIN + 2]
        shift_grad[b] = small[at + SHIFT : at + SHIFT + 2]
        place_in_grad[b] = small[at + PLACE_IN : at + PLACE_IN + 2]
        place_bias_grad[b : b + 1] = small[at + PLACE_BIAS : at + PLACE_BIAS + 1]
        place_out_grad[b] = small[at + PLACE_OUT : at + SMALL]
        heads = width // depth
        head = lax.broadcasted_iota(jnp.int32, (heads, width), 0)
        owner = lax.broadcasted_iota(jnp.int32, (heads, width), 1) // depth
        logit = jnp.where(head == owner, small[at + LOGIT : at + LOGIT + 1], 0.0)
        scale_grad[b : b + 1] = jnp.sum(logit, axis=1, keepdims=True).T


def final_outputs(out, incoming, dx, small, matrices, shapes, window, depth, split_matrices):
    ins = [out, incoming, dx, small] + list(matrices)
    return pl.pallas_call(
        functools.partial(final_kernel, window, depth, split_matrices),
        in_specs=[VM] * len(ins),
        out_specs=[VM] * len(shapes),
        out_shape=[jax.ShapeDtypeStruct(shape, F32) for shape in shapes],
        compiler_params=params(),
        name="final_outputs",
    )(*ins)


def shares(array, images, bands):
    rows, cols = array.shape
    cut = array.reshape(images, rows // images, bands, cols // bands)
    return jnp.transpose(cut, (0, 2, 1, 3)).reshape(images * bands, -1)


def summed_shares(arrays):
    images, bands = lax.axis_size("img"), lax.axis_size("rows")
    joined = jnp.concatenate([shares(array, images, bands) for array in arrays], axis=1)
    mine = lax.psum_scatter(joined, ("img", "rows"), scatter_dimension=0, tiled=True)
    mine = mine.reshape(-1).astype(F32)
    out = []
    at = 0
    for array in arrays:
        rows, cols = array.shape[0] // images, array.shape[1] // bands
        out.append(mine[at : at + rows * cols].reshape(rows, cols))
        at += rows * cols
    return out


def per_device(
    inputs,
    cotangent,
    region,
    rel_index,
    qkv_weight,
    qv_bias,
    logit_scale,
    place_in,
    place_bias,
    place_out,
    proj_weight,
    up_weight,
    up_bias,
    down_weight,
    out_bias,
    norm_gain,
    norm_shift,
):
    window, width = inputs.shape[2], inputs.shape[3]
    heads = logit_scale.shape[1]
    depth = width // heads
    tokens = window * window
    half = tokens // 2
    ff = up_weight.shape[2]
    images, bands = lax.axis_size("img"), lax.axis_size("rows")
    riding = images * bands == 32 and bands == 2
    x = inputs.reshape(tokens, width)
    cot = cotangent.reshape(tokens, width)
    cot_low = cot[:half].astype(BF)
    vectors = (qv_bias, out_bias, norm_gain, norm_shift, logit_scale, up_bias)
    turned_out = jnp.transpose(place_out, (0, 2, 1))
    weights = (qkv_weight, proj_weight, up_weight, down_weight)
    table_zero, *net_zero = bias_table(0, rel_index, place_in, place_bias, turned_out, window)
    hidden, sent, *saved_zero = block_forward(0, (x,), (), vectors, table_zero, weights, window, heads)
    came = passed_along(sent, "rows", -1)
    table_one, *net_one = bias_table(1, rel_index, place_in, place_bias, turned_out, window)
    cot_low, table_one = lax.optimization_barrier((cot_low, table_one))
    cot_in = passed_along(cot_low, "rows", -1)
    shifted_out, sent, *saved_one = block_forward(
        1, (hidden, came), (region.reshape(window, window),), vectors, table_one, weights, window, heads
    )
    out_in = passed_along(sent, "rows", 1)

    def backward(b, own, incoming, saved, left):
        return block_backward(
            b, own, incoming, norm_gain, logit_scale, saved, weights, table_zero.shape, window, heads, riding, left
        )

    def pull(b, rows, net, sums, left=()):
        return bias_table_backward(b, rel_index, rows, net, turned_out, sums, window, left)

    dx_one, sent, sums_one, rows_one, *left = backward(1, cot, cot_in, saved_one, ())
    came = passed_along(sent, "rows", 1)
    (small_one,) = pull(1, rows_one, net_one, sums_one)
    if riding:
        dx_zero, _, sums_zero, rows_zero, *left = backward(0, dx_one, came, saved_zero, left)
        matrices_one = left[4:]
        _, *matrices_zero, small = pull(0, rows_zero, net_zero, sums_zero, (*left[:4], small_one))
    else:
        down, up, proj, qkv = left
        matrix = lambda qkv: jnp.transpose(qkv, (1, 0, 2)).reshape(width, 3 * width)
        matrices_one = summed_shares((matrix(qkv), proj, up, down))
        dx_zero, _, sums_zero, rows_zero, down, up, proj, qkv = backward(0, dx_one, came, saved_zero, ())
        matrices_zero = summed_shares((matrix(qkv), proj, up, down))
        (small_zero,) = pull(0, rows_zero, net_zero, sums_zero)
        small = lax.psum(jnp.concatenate([small_zero, small_one], axis=0), ("img", "rows"))
    cut = lambda rows, cols: (2, rows // images, cols // bands)
    shapes = [
        (tokens, width), (tokens, width), cut(width, 3 * width), (2, 2, width), (2, heads), (2, 2, width), (2, width),
        (2, heads, width), cut(width, width), cut(width, ff), (2, ff), cut(ff, width), (2, 2, width), (2, 2, width),
        (2, 2, width),
    ]
    output, input_grad, *rest = final_outputs(
        shifted_out, out_in, dx_zero, small, list(matrices_zero) + list(matrices_one), shapes, window, depth, riding
    )
    rest[5] = jnp.transpose(rest[5], (0, 2, 1))
    return (output.reshape(inputs.shape), input_grad.reshape(inputs.shape), *rest)


def solution(mesh):
    token = P("img", "rows", None, None)
    matrix = P(None, "img", "rows")
    return jax.shard_map(
        per_device,
        mesh=mesh,
        in_specs=(token, token, P("img", "rows", None)) + (P(),) * 14,
        out_specs=(
            token, token, matrix, P(), P(), P(), P(), P(), matrix, matrix, P(), matrix, P(), P(), P(),
        ),
        check_vma=False,
    )
```

```python
import functools

import jax
import jax.numpy as jnp
from jax import lax
from jax.experimental import pallas as pl
from jax.experimental.pallas import tpu as pltpu
from jax.sharding import PartitionSpec as P

BF = jnp.bfloat16
F32 = jnp.float32
LOG2E = 1.4426950408889634
MASKED = 1.0e9
LANES = 128


def passed_along(array, axis, by):
    devices = lax.axis_size(axis)
    return lax.ppermute(array, axis, [(i, (i + by) % devices) for i in range(devices)])


def mm(a, b):
    return lax.dot_general(a, b, (((1,), (0,)), ((), ())), preferred_element_type=F32)


def mm_nt(a, b):
    return lax.dot_general(a, b, (((1,), (1,)), ((), ())), preferred_element_type=F32)


def mm_tn(a, b):
    return lax.dot_general(a, b, (((0,), (0,)), ((), ())), preferred_element_type=F32)


def group_ones(depth):
    rows = lax.broadcasted_iota(jnp.int32, (LANES, LANES), 0) // depth
    cols = lax.broadcasted_iota(jnp.int32, (LANES, LANES), 1) // depth
    return jnp.where(rows == cols, 1.0, 0.0).astype(BF)


def group_sums(ones, first, second):
    rows = first.shape[0]
    both = group_sum(ones, jnp.concatenate([first, second], axis=0))
    return both[:rows], both[rows:]


def group_sum(ones, values):
    high, low = split(values)
    return mm(jnp.concatenate([high, low], axis=1), jnp.concatenate([ones, ones], axis=0))


def split(values):
    high = values.astype(BF)
    return high, (values - high.astype(F32)).astype(BF)


def head_scales(logit_ref, layer, width):
    heads = logit_ref.shape[1]
    column = jnp.broadcast_to(logit_ref[layer : layer + 1], (heads, heads)).T[:, :1]
    head = lax.broadcasted_iota(jnp.int32, (heads, width), 0)
    owner = lax.broadcasted_iota(jnp.int32, (heads, width), 1) // (width // heads)
    return jnp.exp(jnp.sum(jnp.where(head == owner, column, 0.0), axis=0, keepdims=True))


def normal_parts(values):
    cdf = 0.5 + 0.5 * lax.erf(values * 0.7071067811865476)
    return cdf, jnp.exp2(values * values * (-0.5 * LOG2E)) * 0.3989422804014327


def norm_stats(values):
    centre = values - jnp.mean(values, axis=-1, keepdims=True)
    spread = jnp.mean(centre * centre, axis=-1, keepdims=True)
    rstd = lax.rsqrt(spread + 1e-05)
    return centre * rstd, rstd


def norm_pull(values, gain, grad):
    hat, rstd = norm_stats(values)
    scaled = grad * gain
    first = jnp.mean(scaled, axis=-1, keepdims=True)
    second = jnp.mean(scaled * hat, axis=-1, keepdims=True)
    pulled = rstd * (scaled - first - hat * second)
    gain_grad = jnp.sum(grad * hat, axis=0, keepdims=True)
    shift_grad = jnp.sum(grad, axis=0, keepdims=True)
    return pulled, gain_grad, shift_grad


def place():
    me, y = lax.axis_index("img"), lax.axis_index("rows")
    return me, me % 2, (me // 2) % 2, me // 4, y


def partner(which, step=1):
    me, core, x, z, y = place()
    if which == "core":
        return (me + 1 - 2 * core, y)
    if which == "x":
        return (me + 2 - 4 * x, y)
    if which == "y":
        return (me, 1 - y)
    depth = lax.axis_size("img") // 4
    return ((z + step) % depth * 4 + me % 4, y)


def greet(which):
    depth = lax.axis_size("img") // 4
    others = []
    for name in which:
        others += [partner("z", step) for step in range(1, depth)] if name == "z" else [partner(name)]
    barrier = pltpu.get_barrier_semaphore()
    for other in others:
        pl.semaphore_signal(barrier, inc=1, device_id=other, device_id_type=pl.DeviceIdType.MESH)
    pl.semaphore_wait(barrier, len(others))


def remote(source, target, sems, at, device):
    return pltpu.make_async_remote_copy(
        src_ref=source, dst_ref=target, send_sem=sems[0].at[at], recv_sem=sems[1].at[at],
        device_id=device, device_id_type=pl.DeviceIdType.MESH,
    )


def half_at(index, size):
    return pl.ds(pl.multiple_of(index * size, LANES), size)


class Across:
    copies = 4

    def __init__(self, first, second):
        self.sums = [first[2:], second[2:]]
        self.scratch = []
        for shape in (first, second):
            self.scratch += [pltpu.VMEM(shape[1:], BF), pltpu.VMEM(shape[1:], BF), pltpu.VMEM(shape[2:], BF)]

    def bind(self, ins, outs, scratch, sems, base):
        self.flows = [(ins[i], outs[i]) + tuple(scratch[3 * i : 3 * i + 3]) for i in range(2)]
        self.sems, self.base = sems, base

    def axes(self, flow):
        _, _, x, _, y = place()
        return (("x", x), ("y", y)) if flow == 0 else (("y", y), ("x", x))

    def copy(self, flow, stage):
        source, _, got, sums, last = self.flows[flow]
        name, here = self.axes(flow)[stage]
        if stage == 0:
            return remote(source.at[1 - here], got, self.sems, self.base + flow, partner(name))
        return remote(sums.at[1 - here], last, self.sems, self.base + 2 + flow, partner(name))

    def start(self):
        self.copy(0, 0).start()
        self.copy(1, 0).start()

    def turn(self):
        for flow in range(2):
            source, _, got, sums, _ = self.flows[flow]
            here = self.axes(flow)[0][1]
            self.copy(flow, 0).wait()
            sums[...] = source[here] + got[...]
            self.copy(flow, 1).start()

    def finish(self):
        for flow in range(2):
            _, out, _, sums, last = self.flows[flow]
            here = self.axes(flow)[1][1]
            self.copy(flow, 1).wait()
            out[...] = sums[here] + last[...]


PICKS = {
    "down": lambda z: (z % 2, z // 2),
    "up": lambda z: (slice(None), z),
    "flow": lambda z: (slice(None), z),
}


class Along:
    def __init__(self, depth, kinds, shapes):
        self.depth = depth
        self.picks = [PICKS[kind] for kind in kinds]
        drop = {"down": lambda shape: shape[2:], "up": lambda shape: shape[:1] + shape[2:], "flow": lambda shape: shape[:1] + shape[2:]}
        self.sums = [drop[kind](shape) for kind, shape in zip(kinds, shapes)]
        self.scratch = [pltpu.VMEM((depth - 1,) + shape, BF) for shape in self.sums]
        self.copies = (depth - 1) * len(shapes)

    def bind(self, ins, outs, scratch, sems, base):
        self.ins, self.outs, self.got = ins, outs, scratch
        self.sems, self.base = sems, base

    def each(self):
        _, _, _, z, _ = place()
        for i, (source, got, pick) in enumerate(zip(self.ins, self.got, self.picks)):
            for step in range(1, self.depth):
                at = self.base + i * (self.depth - 1) + step - 1
                share = source.at[pick((z + step) % self.depth)]
                yield remote(share, got.at[step - 1], self.sems, at, partner("z", step))

    def start(self):
        for copy in self.each():
            copy.start()

    def finish(self):
        _, _, _, z, _ = place()
        for copy in self.each():
            copy.wait()
        for source, out, got, pick in zip(self.ins, self.outs, self.got, self.picks):
            total = source[pick(z)].astype(F32)
            for step in range(1, self.depth):
                total = total + got[step - 1].astype(F32)
            out[...] = total


def sems_for(count):
    return [pltpu.SemaphoreType.DMA((count,)), pltpu.SemaphoreType.DMA((count,))]


def take(refs, *counts):
    out = []
    at = 0
    for count in counts:
        out.append(refs[at : at + count])
        at += count
    assert at == len(refs), (at, len(refs))
    return out


def whole(shape):
    return pl.BlockSpec(shape, lambda *s: (0,) * len(shape))


VM = pl.BlockSpec(memory_space=pltpu.VMEM)
AN = pl.BlockSpec(memory_space=pl.ANY)
LIMIT = 62 * 2**20


def params(number=None):
    if number is None:
        return pltpu.CompilerParams(vmem_limit_bytes=LIMIT)
    return pltpu.CompilerParams(vmem_limit_bytes=LIMIT, collective_id=number, has_side_effects=True)


def lanes_of(group, size=LANES):
    return pl.ds(pl.multiple_of(group * size, size), size)


CHUNK = 512


def forward_kernel(layer, window, depth, *refs):
    masked = layer == 1
    tokens = window * window
    width = refs[0].shape[1]
    groups = width // LANES
    per = LANES // depth
    (
        x_refs, region_refs, (qv_ref, ob_ref, gain_ref, shift_ref, logit_ref, ub_ref, bias_ref),
        (wqkv, wp, wu, wd), (out_ref, send_ref), saved, keep, (z_s, m_s, qkv_s, scale_s, qm_s, km_s),
        (wqkv_s, wp_s, wu_s, wd_s), (load, store),
    ) = take(refs, 2 if masked else 1, 1 if masked else 0, 7, 4, 2, 14, 14, 6, 4, 2)
    chunks = ub_ref.shape[1] // CHUNK
    e_s, qn_s, kn_s, v_s, o_s, iq_s, ik_s, rinv_s, p_s, a_s, zr_s, g_s, gd_s, mo_s = keep
    lane = lax.broadcasted_iota(jnp.int32, (1, LANES), 1) // depth

    def load_qkv(i):
        return pltpu.make_async_copy(wqkv.at[layer, :, lanes_of(i, width)], wqkv_s.at[i], load.at[i])

    def load_rest(i):
        source, target = ((wp, wp_s), (wu, wu_s), (wd, wd_s))[i]
        return pltpu.make_async_copy(source.at[layer], target, load.at[3 + i])

    def put(i):
        return pltpu.make_async_copy(keep[i], saved[i], store.at[i])

    def put_p(g):
        rows = pl.ds(g * per, per)
        return pltpu.make_async_copy(p_s.at[rows], saved[8].at[rows], store.at[14 + g])

    def put_g(i, c):
        cols = lanes_of(c, CHUNK)
        return pltpu.make_async_copy(
            keep[11 + i].at[:, cols], saved[11 + i].at[:, cols], store.at[14 + groups + 2 * c + i]
        )

    for i in range(3):
        load_qkv(i).start()
    for i in range(3):
        load_rest(i).start()
    scale_s[...] = head_scales(logit_ref, layer, width) * LOG2E
    ones = group_ones(depth)
    if masked:
        token = lax.broadcasted_iota(jnp.int32, (tokens, window), 0)
        place_in_row = lax.broadcasted_iota(jnp.int32, (tokens, window), 1)
        rows_pick = jnp.where(token // window == place_in_row, 1.0, 0.0).astype(BF)
        labels = mm(rows_pick, region_refs[0][...].astype(F32).astype(BF))
        mine = column_of(token % window, window, True) == place_in_row
        labels = jnp.sum(jnp.where(mine, labels, 0.0), axis=1, keepdims=True)
        each = lax.broadcasted_iota(jnp.int32, (tokens, LANES), 1)
        same = labels == each.astype(F32)
        qm_s[...] = jnp.where(same, 1.0, 0.0).astype(BF)
        km_s[...] = jnp.where(same | (each >= 8), 0.0, -MASKED).astype(BF)
    half = tokens // 2
    if masked:
        z_s[:half] = x_refs[0][half:]
        z_s[half:] = x_refs[1][...].astype(F32)
        x_ref = z_s
    else:
        x_ref = x_refs[0]
    e_s[...] = x_ref[...].astype(BF)
    put(0).start()
    for i in range(3):
        load_qkv(i).wait()
        raw = mm(e_s[...], wqkv_s[i])
        if i != 1:
            raw = raw + qv_ref[layer, i // 2 : i // 2 + 1]
        qkv_s[i] = raw

    def group_step(g, carry):
        cols = lanes_of(g)
        q = qkv_s[0, :, cols]
        k = qkv_s[1, :, cols]
        v = qkv_s[2, :, cols]
        iq, ik = group_sums(ones, q * q, k * k)
        iq = lax.rsqrt(iq + 1e-06)
        ik = lax.rsqrt(ik + 1e-06)
        qn = q * iq
        kn = (k * ik).astype(BF)
        iq_s[:, cols] = iq
        ik_s[:, cols] = ik
        qn_s[:, cols] = qn.astype(BF)
        kn_s[:, cols] = kn
        v_s[:, cols] = v.astype(BF)
        scales = scale_s[:, cols]
        rhs = jnp.concatenate([kn, km_s[...]], axis=1) if masked else kn
        mixed = jnp.zeros((tokens, LANES), F32)
        total = mixed
        for h in range(per):
            mine = lane == h
            lhs = jnp.where(mine, qn, 0.0).astype(BF)
            if masked:
                lhs = jnp.concatenate([lhs, qm_s[...]], axis=1)
            cosine = mm_nt(lhs, rhs)
            scale = scales[:, h * depth : h * depth + 1]
            table = bias_ref[g * per + h]
            for pair in range(window // 2):
                parts = []
                for r in (2 * pair, 2 * pair + 1):
                    at = window * (window - 1 - r)
                    parts.append(
                        cosine[r * window : (r + 1) * window] * scale + table[:, at : at + tokens]
                    )
                both = jnp.concatenate(parts, axis=0)
                p_s[g * per + h, 2 * pair * window : (2 * pair + 2) * window, :] = jnp.exp2(both).astype(BF)
            both = mm(p_s[g * per + h], jnp.where(mine, v, 1.0).astype(BF))
            mixed = jnp.where(mine, both, mixed)
            total = jnp.where(lane == (h + 1) % per, both, total)
        rinv = pltpu.roll(1.0 / total, LANES - depth, 1)
        rinv_s[:, cols] = rinv
        o_s[:, cols] = mixed * rinv
        put_p(g).start()
        return carry

    lax.fori_loop(0, groups, group_step, 0)
    for i in range(1, 8):
        put(i).start()
    load_rest(0).wait()
    a = mm(o_s[...].astype(BF), wp_s[...]) + ob_ref[layer, 0:1]
    a_s[...] = a
    put(9).start()
    hat, _ = norm_stats(a)
    z = x_ref[...] + (hat * gain_ref[layer, 0:1] + shift_ref[layer, 0:1])
    z_s[...] = z
    zr_s[...] = z.astype(BF)
    put(10).start()
    m_s[...] = jnp.zeros_like(m_s)
    load_rest(1).wait()
    load_rest(2).wait()

    def chunk_step(c, carry):
        cols = lanes_of(c, CHUNK)
        pre = mm(zr_s[...], wu_s[:, cols]) + ub_ref[layer : layer + 1, cols]
        cdf, density = normal_parts(pre)
        act = (pre * cdf).astype(BF)
        g_s[:, cols] = act
        gd_s[:, cols] = (cdf + pre * density).astype(BF)
        put_g(0, c).start()
        put_g(1, c).start()
        m_s[...] += mm(act, wd_s[cols, :])
        return carry

    lax.fori_loop(0, chunks, chunk_step, 0)
    m = m_s[...] + ob_ref[layer, 1:2]
    mo_s[...] = m
    put(13).start()
    hat, _ = norm_stats(m)
    out = z_s[...] + (hat * gain_ref[layer, 1:2] + shift_ref[layer, 1:2])
    out_ref[...] = out
    send_ref[...] = (out[half:] if masked else out[:half]).astype(BF)
    for i in range(14):
        if i not in (8, 11, 12):
            put(i).wait()
    for g in range(groups):
        put_p(g).wait()
    for c in range(chunks):
        put_g(0, c).wait()
        put_g(1, c).wait()


def block_forward(layer, xs, region, vectors, table, weights, window, heads):
    tokens, width = window * window, xs[0].shape[1]
    depth = width // heads
    w_qkv, w_proj, w_up, w_down = weights
    ff = w_up.shape[2]
    groups = width // LANES
    sds = jax.ShapeDtypeStruct
    tok = lambda dt, cols=width: sds((tokens, cols), dt)
    saved = [
        tok(BF), tok(BF), tok(BF), tok(BF), tok(F32), tok(F32), tok(F32), tok(F32),
        sds((heads, tokens, tokens), BF), tok(F32), tok(BF), tok(BF, ff), tok(BF, ff), tok(F32),
    ]
    ins = list(xs) + list(region) + list(vectors) + [table]
    stores = 14 + groups + 2 * (ff // CHUNK)
    return pl.pallas_call(
        functools.partial(forward_kernel, layer, window, depth),
        in_specs=[VM] * len(ins) + [AN] * 4,
        out_specs=[VM] * 2 + [AN] * 14,
        out_shape=[tok(F32), sds((tokens // 2, width), BF)] + saved,
        scratch_shapes=[pltpu.VMEM(item.shape, item.dtype) for item in saved]
        + [
            pltpu.VMEM((tokens, width), F32), pltpu.VMEM((tokens, width), F32), pltpu.VMEM((3, tokens, width), F32),
            pltpu.VMEM((1, width), F32), pltpu.VMEM((tokens, LANES), BF), pltpu.VMEM((tokens, LANES), BF),
            pltpu.VMEM((3, width, width), BF), pltpu.VMEM((width, width), BF),
            pltpu.VMEM((width, ff), BF), pltpu.VMEM((ff, width), BF),
            pltpu.SemaphoreType.DMA((6,)), pltpu.SemaphoreType.DMA((stores,)),
        ],
        compiler_params=params(),
        name="block_forward_%d" % layer,
    )(*ins, w_qkv, w_proj, w_up, w_down)


UP_BIAS, QV, OUT_BIAS, GAIN, SHIFT, PLACE_IN, PLACE_BIAS, LOGIT, PLACE_OUT = 0, 4, 6, 8, 10, 12, 14, 15, 16
SMALL = 32


class Plan:
    def __init__(self, width, ff, images, follows):
        deep = images // 4
        self.deep = deep
        self.down = (2, 2, 2, 2, deep // 2, ff // images, width // 2)
        self.up = (2, 2, 2, 2, deep, width // images, ff // 4)
        half = lambda shape: shape[:1] + shape[2:]
        self.half_down, self.half_up = half(self.down), half(self.up)
        self.flow = (2, 2, 2, 2, deep, width // images, width // 2)
        self.got_flow = half(self.flow)
        self.half_flow = self.flow[2:4] + (2,) + self.flow[4:]
        self.parts = [Across(self.half_down[1:], self.half_up[1:]) for _ in range(2)]
        sums = [(2,) + shape for shape in self.parts[0].sums]
        self.outs = [(shape, BF) for shape in sums] + [(self.half_flow, BF)] * 2
        self.scratch = [pltpu.VMEM(shape, BF) for shape in (
            self.down, self.up, self.half_down, self.half_up, self.flow, self.flow, self.got_flow, self.got_flow,
        )] + self.parts[0].scratch + self.parts[1].scratch
        self.core = 8
        self.copies = self.core + 8
        self.ins = []
        self.follows = follows
        if follows:
            self.old = Along(deep, ("down", "up"), sums)
            self.turned = Across(self.half_flow, self.half_flow)
            self.late = Along(deep, ("flow", "flow"), self.turned.sums)
            self.ins = sums + [self.half_flow] * 2
            self.outs += [(shape, F32) for shape in self.old.sums + self.late.sums]
            self.scratch += [pltpu.VMEM(shape, BF) for shape in self.turned.sums]
            self.scratch += self.old.scratch + self.turned.scratch + self.late.scratch
            self.copies += self.old.copies + self.turned.copies + self.late.copies
        self.scratch = self.scratch + sems_for(self.copies)

    def bind(self, ins, outs, scratch):
        sems = scratch[-2:]
        self.sems = sems
        self.down_s, self.up_s, self.got_down, self.got_up = scratch[:4]
        self.flows = ((scratch[4], scratch[6]), (scratch[5], scratch[7]))
        self.flow_outs = outs[2:4]
        for c, part in enumerate(self.parts):
            part.bind(
                [self.got_down.at[c], self.got_up.at[c]], [outs[0].at[c], outs[1].at[c]],
                scratch[8 + 6 * c : 14 + 6 * c], sems, self.core + 4 * c,
            )
        if self.follows:
            rest = scratch[20:-2]
            at = self.core + 8
            between, old, turned, late = take(rest, 2, 2, 6, 2)
            self.old.bind(ins[:2], outs[4:6], old, sems, at)
            at += self.old.copies
            self.turned.bind(ins[2:4], between, turned, sems, at)
            at += self.turned.copies
            self.late.bind(between, outs[6:8], late, sems, at)

    def feed_copy(self, c, which):
        _, core, _, _, _ = place()
        source, target = ((self.down_s, self.got_down), (self.up_s, self.got_up))[which]
        return remote(source.at[c, 1 - core], target.at[c], self.sems, 2 * c + which, partner("core"))

    def flow_copy(self, part, flow):
        _, core, _, _, _ = place()
        source, target = self.flows[flow]
        return remote(source.at[part, 1 - core], target.at[part], self.sems, 4 + 2 * part + flow, partner("core"))

    def begin(self):
        greet(["core", "x", "y"] + (["z"] if self.follows else []))
        if self.follows:
            self.turned.start()
            self.old.start()

    def feed_step(self, c, down, up):
        rows = self.down[5]
        wide = self.down[6]
        for i in range(2):
            for x in range(2):
                for core in range(2):
                    at = i * CHUNK + (2 * x + core) * rows
                    for y in range(2):
                        self.down_s[c, core, x, y, i] = down[at : at + rows, y * wide : (y + 1) * wide]
        self.feed_copy(c, 0).start()
        self.spread(self.up_s, c, 1, None, up)
        self.feed_copy(c, 1).start()

    def spread(self, target, part, flow, y, block, cols=slice(None)):
        for half in (0, 1) if y is None else (y,):
            piece = block
            if y is None:
                wide = block.shape[1] // 2
                piece = block[:, half * wide : (half + 1) * wide]
            piece = piece.reshape((self.deep, 2, 2, -1, piece.shape[1]))
            for x in range(2):
                for core in range(2):
                    first, second = (x, half) if flow == 0 else (half, x)
                    target[part, core, first, second, :, :, cols] = piece[:, x, core]

    def ready(self, c):
        _, core, _, _, _ = place()
        self.feed_copy(c, 0).wait()
        self.got_down[c] = self.got_down[c] + self.down_s[c, core]
        self.feed_copy(c, 1).wait()
        self.got_up[c] = self.got_up[c] + self.up_s[c, core]
        self.parts[c].start()

    def midway(self):
        self.ready(0)

    def between(self, proj):
        flow_b = self.flows[1][0]
        half = proj.shape[1] // 2
        self.spread(flow_b, 0, 1, 1, proj[:, half:])
        self.spread(flow_b, 1, 1, 0, proj[:, :half])
        self.ready(1)
        if self.follows:
            self.turned.turn()
            self.old.finish()
        self.parts[0].turn()

    def attend_begin(self, half):
        @pl.when(half == 1)
        def _():
            self.parts[1].turn()
            if self.follows:
                self.turned.finish()
                self.late.start()

    def attend_step(self, half, grads):
        flow_a, flow_b = self.flows[0][0], self.flows[1][0]
        wide = grads.shape[1] // 3
        q, k, v = (grads[:, i * wide : (i + 1) * wide] for i in range(3))

        @pl.when(half == 0)
        def _():
            self.spread(flow_b, 0, 1, 0, k)
            self.flow_copy(0, 1).start()
            self.spread(flow_a, 0, 0, 0, q)
            self.spread(flow_a, 0, 0, 1, v)
            self.flow_copy(0, 0).start()

        @pl.when(half == 1)
        def _():
            self.spread(flow_b, 1, 1, 1, v)
            self.flow_copy(1, 1).start()
            self.spread(flow_a, 1, 0, 0, q)
            self.spread(flow_a, 1, 0, 1, k)
            self.flow_copy(1, 0).start()

    def end(self):
        _, core, _, _, _ = place()
        self.parts[0].finish()
        for part in range(2):
            for flow in (1, 0):
                source, got = self.flows[flow]
                self.flow_copy(part, flow).wait()
                self.flow_outs[flow][:, :, part] = source[part, core] + got[part]
        if self.follows:
            self.late.finish()
        self.parts[1].finish()


def backward_kernel(layer, window, depth, plan, *refs):
    tokens = window * window
    half = tokens // 2
    n_plan_in = len(plan.ins) if plan else 0
    n_plan_out = len(plan.outs) if plan else 4
    n_plan_scratch = len(plan.scratch) if plan else 0
    (
        (own_ref, in_ref, gain_ref, logit_ref), plan_ins, saved, (wqkv, wp, wu, wd),
        (dx_ref, send_ref, sums_ref, table_ref), plan_outs, keep,
        (wqkv_s, wp_s, wu_s, wd_s, dm_s, do_s, ds_s, scale_s, load), plan_scratch,
    ) = take(refs, 4, n_plan_in, 14, 4, 4, n_plan_out, 14, 9, n_plan_scratch)
    e_s, qn_s, kn_s, v_s, o_s, iq_s, ik_s, rinv_s, p_s, a_s, zr_s, g_s, gd_s, m_s = keep
    width = own_ref.shape[1]
    ff = g_s.shape[1]
    groups = width // LANES
    per = LANES // depth
    chunks = ff // CHUNK
    wide = tokens
    lane = lax.broadcasted_iota(jnp.int32, (1, LANES), 1)

    def load_kept(i):
        return pltpu.make_async_copy(saved[i], keep[i], load.at[i])

    def load_p(g):
        return pltpu.make_async_copy(saved[8].at[pl.ds(g * per, per)], p_s.at[g % 2], load.at[14 + g])

    def load_weights(i):
        source, target = ((wqkv, wqkv_s), (wp, wp_s))[i]
        return pltpu.make_async_copy(source.at[layer], target, load.at[14 + groups + i])

    def load_chunk(c):
        here = lanes_of(c, CHUNK)
        cols = lanes_of(c // 2 + c % 2 * 2, CHUNK)
        at = 16 + groups + 4 * c
        return [
            pltpu.make_async_copy(saved[11].at[:, cols], g_s.at[:, here], load.at[at]),
            pltpu.make_async_copy(saved[12].at[:, cols], gd_s.at[:, here], load.at[at + 1]),
            pltpu.make_async_copy(wd.at[layer, cols], wd_s.at[here], load.at[at + 2]),
            pltpu.make_async_copy(wu.at[layer, :, cols], wu_s.at[:, here], load.at[at + 3]),
        ]

    load_kept(13).start()
    load_kept(10).start()
    for c in range(chunks):
        for copy in load_chunk(c):
            copy.start()
    load_kept(9).start()
    load_kept(4).start()
    load_weights(1).start()
    if plan:
        plan.bind(plan_ins, plan_outs, plan_scratch)
        plan.begin()
    if layer == 1:
        dx_ref[:half] = own_ref[half:]
        dx_ref[half:] = in_ref[...].astype(F32)
    else:
        dx_ref[:half] = in_ref[...].astype(F32)
        dx_ref[half:] = own_ref[:half]
    scale_s[...] = head_scales(logit_ref, layer, width)
    ones = group_ones(depth)
    load_kept(13).wait()
    dm, gain_grad, shift_grad = norm_pull(m_s[...], gain_ref[layer, 1:2], dx_ref[...])
    low = dm.astype(BF)
    dm_s[...] = low
    sums_ref[...] = jnp.zeros_like(sums_ref)
    sums_ref[OUT_BIAS + 1 : OUT_BIAS + 2] = jnp.sum(low.astype(F32), axis=0, keepdims=True)
    sums_ref[GAIN + 1 : GAIN + 2] = gain_grad
    sums_ref[SHIFT + 1 : SHIFT + 2] = shift_grad
    load_kept(10).wait()

    for c in range(chunks // 2):
        for i in range(2):
            for copy in load_chunk(2 * c + i):
                copy.wait()
        if c == 0:
            for i in (0, 1, 2, 3, 5, 6, 7):
                load_kept(i).start()
            load_p(0).start()
            load_weights(0).start()
            load_p(1).start()
        cols = slice(2 * c * CHUNK, (2 * c + 2) * CHUNK)
        dm = dm_s[...]
        dh = (mm_nt(dm, wd_s[cols]) * gd_s[:, cols].astype(F32)).astype(BF)
        if plan and c == 1:
            plan.midway()
        up = mm_tn(zr_s[...], dh).astype(BF)
        down = mm_tn(g_s[:, cols], dm).astype(BF)
        bias_grad = jnp.sum(dh.astype(F32), axis=0, keepdims=True)
        for i in range(2):
            sums_ref[UP_BIAS + c + 2 * i : UP_BIAS + c + 2 * i + 1] = bias_grad[:, i * CHUNK : (i + 1) * CHUNK]
        if plan:
            plan.feed_step(c, down, up)
        else:
            for i in range(2):
                out_cols = slice((c + 2 * i) * CHUNK, (c + 2 * i + 1) * CHUNK)
                plan_outs[0][out_cols] = down[i * CHUNK : (i + 1) * CHUNK]
                plan_outs[1][:, out_cols] = up[:, i * CHUNK : (i + 1) * CHUNK]
        dx_ref[...] += mm_nt(dh, wu_s[:, cols])
    load_kept(9).wait()
    load_kept(4).wait()
    load_weights(1).wait()
    da, gain_grad, shift_grad = norm_pull(a_s[...], gain_ref[layer, 0:1], dx_ref[...])
    low = da.astype(BF)
    sums_ref[OUT_BIAS : OUT_BIAS + 1] = jnp.sum(low.astype(F32), axis=0, keepdims=True)
    sums_ref[GAIN : GAIN + 1] = gain_grad
    sums_ref[SHIFT : SHIFT + 1] = shift_grad
    proj = mm_tn(o_s[...].astype(BF), low).astype(BF)
    do_s[...] = mm_nt(low, wp_s[...]).astype(BF)
    if plan:
        plan.between(proj)
    else:
        plan_outs[2][...] = proj
    for i in (0, 1, 2, 3, 5, 6, 7):
        load_kept(i).wait()
    load_weights(0).wait()

    def one_group(g, slot):
        cols = lanes_of(g)
        load_p(g).wait()
        scale = scale_s[:, cols]
        v = v_s[:, cols]
        kn = kn_s[:, cols]
        qn = qn_s[:, cols]
        dor = (do_s[:, cols].astype(F32) * rinv_s[:, cols]).astype(BF)
        dor32 = dor.astype(F32)
        less = -group_sum(ones, dor32 * o_s[:, cols])
        high = less.astype(BF).astype(F32)
        extra = jnp.where(lane % depth == 0, high, jnp.where(lane % depth == 1, less - high, 0.0))
        extra = pltpu.roll(extra, depth, 1)
        dor_t = dor.T
        qn_t = qn.T
        v32 = v.astype(F32)
        kn32 = kn.astype(F32)
        qn32 = qn.astype(F32)
        dq = jnp.zeros((tokens, LANES), F32)
        dk_t = []
        dv_t = []
        for h in range(per):
            mine = lane // depth == h
            after = lane // depth == (h + 1) % per
            lhs = jnp.where(mine, dor32, jnp.where(after, extra, 0.0)).astype(BF)
            t = mm_nt(lhs, jnp.where(mine, v32, 1.0).astype(BF))
            head = g * per + h
            table_ref[head] = jnp.zeros(table_ref.shape[1:], F32)
            for pair in range(window // 2):
                rows = slice(2 * pair * window, (2 * pair + 2) * window)
                ds = p_s[slot, h, rows, :].astype(F32) * t[rows]
                ds_s[h % 2, rows, :] = ds.astype(BF)
                for i in range(2):
                    at = window * (window - 1 - (2 * pair + i))
                    table_ref[head, :, at : at + tokens] += ds[i * window : (i + 1) * window]
            low = ds_s[h % 2]
            dv_t.append(mm(dor_t[h * depth : (h + 1) * depth], p_s[slot, h]))
            dk_t.append(mm(qn_t[h * depth : (h + 1) * depth], low))
            dq = dq + mm(low, jnp.where(mine, kn32, 0.0).astype(BF))

        @pl.when(g + 2 < groups)
        def _():
            load_p(g + 2).start()

        dqn = dq * scale
        dkn = jnp.concatenate(dk_t, axis=0).T * scale
        dv = jnp.concatenate(dv_t, axis=0).T
        along_q = qn32 * dqn
        sum_q, sum_k = group_sums(ones, along_q, kn32 * dkn)
        dq = iq_s[:, cols] * (dqn - qn32 * sum_q)
        dk = ik_s[:, cols] * (dkn - kn32 * sum_k)
        sums_ref[LOGIT : LOGIT + 1, cols] = jnp.sum(along_q, axis=0, keepdims=True)
        parts = [part.astype(BF) for part in (dq, dk, dv)]
        sums_ref[QV : QV + 1, cols] = jnp.sum(parts[0].astype(F32), axis=0, keepdims=True)
        sums_ref[QV + 1 : QV + 2, cols] = jnp.sum(parts[2].astype(F32), axis=0, keepdims=True)
        return parts

    def group_step(j, carry):
        if plan:
            plan.attend_begin(j)
        parts = one_group(2 * j, 0) + one_group(2 * j + 1, 1)
        low = jnp.concatenate([parts[i // 2 + 3 * (i % 2)] for i in range(6)], axis=1)
        grads = mm_tn(e_s[...], low).astype(BF)
        if plan:
            plan.attend_step(j, grads)
        else:
            for i in range(6):
                plan_outs[3][i // 2, :, lanes_of(2 * j + i % 2)] = grads[:, i * LANES : (i + 1) * LANES]
        weights = jnp.concatenate(
            [wqkv_s[:, lanes_of(i // 2 * groups + 2 * j + i % 2)] for i in range(6)], axis=1
        )
        dx_ref[...] += mm_nt(low, weights)
        return carry

    lax.fori_loop(0, groups // 2, group_step, 0)
    if layer == 1:
        send_ref[...] = dx_ref[half:].astype(BF)
    else:
        send_ref[...] = jnp.zeros_like(send_ref)
    if plan:
        plan.end()


def block_backward(layer, own, incoming, gain, logits, saved, weights, table_shape, window, heads, riding, left):
    tokens, width = own.shape
    depth = width // heads
    ff = saved[11].shape[1]
    groups = width // LANES
    per = LANES // depth
    sds = jax.ShapeDtypeStruct
    plan = Plan(width, ff, lax.axis_size("img"), bool(left)) if riding else None
    plan_ins = list(left)
    if riding:
        plan_outs = [sds(shape, dt) for shape, dt in plan.outs]
        plan_scratch = plan.scratch
    else:
        plan_outs = [sds((ff, width), BF), sds((width, ff), BF), sds((width, width), BF), sds((3, width, width), BF)]
        plan_scratch = []
    keep = [pltpu.VMEM(item.shape, item.dtype) for item in saved]
    keep[8] = pltpu.VMEM((2, per, tokens, tokens), BF)
    return pl.pallas_call(
        functools.partial(backward_kernel, layer, window, depth, plan),
        in_specs=[VM] * (4 + len(plan_ins)) + [AN] * 18,
        out_specs=[VM] * (4 + len(plan_outs)),
        out_shape=[
            sds((tokens, width), F32), sds((tokens // 2 if layer == 1 else 16, width), BF), sds((16, width), F32),
            sds(table_shape, F32),
        ] + plan_outs,
        scratch_shapes=keep
        + [
            pltpu.VMEM((width, 3 * width), BF), pltpu.VMEM((width, width), BF),
            pltpu.VMEM((width, ff), BF), pltpu.VMEM((ff, width), BF),
            pltpu.VMEM((tokens, width), BF), pltpu.VMEM((tokens, width), BF),
            pltpu.VMEM((2, tokens, tokens), BF), pltpu.VMEM((1, width), F32),
            pltpu.SemaphoreType.DMA((16 + groups + 4 * (ff // CHUNK),)),
        ]
        + plan_scratch,
        compiler_params=params(2 - layer if riding else None),
        name="block_backward_%d" % layer,
    )(own, incoming, gain, logits, *plan_ins, *saved, *weights)


def entry_logs(first, count, window):
    at = first + lax.broadcasted_iota(jnp.int32, (8, count), 1)
    row = at // (2 * window)
    col = at % (2 * window)
    real = (row < 2 * window - 1) & (col < 2 * window - 1)

    def logs(offset):
        size = jnp.log2(jnp.abs(offset).astype(F32) * (8.0 / (window - 1)) + 1.0) / 3.0
        return jnp.where(offset < 0, -size, size)

    by_row = jnp.where(real, logs(window - 1 - row), 0.0)
    by_col = jnp.where(real, logs(col - (window - 1)), 0.0)
    return by_row, by_col


def column_of(token_col, window, shifted):
    if not shifted:
        return token_col
    return jnp.where(token_col >= window // 2, token_col - window // 2, token_col + window // 2)


def slopes(rel_ref, window):
    first = rel_ref[0:1, 0:1]
    down = rel_ref[window : window + 1, 0:1] - first
    across = rel_ref[1:2, 0:1] - first
    straight = jnp.abs(down) == 2 * window - 1
    sign = lambda step: jnp.where(step > 0, 1.0, -1.0)
    return straight, sign(down), sign(across)


TABLE_CHUNK = 768


def table_kernel(
    layer, window, in_ref, bias_ref, outw_ref, rel, rows_ref, tab_ref, hid_out, slope_out,
    hid_s, slope_s, w_s, rel_ref, sems,
):
    fetch = pltpu.make_async_copy(rel.at[pl.ds(0, rel_ref.shape[0]), pl.ds(0, LANES)], rel_ref, sems.at[0])
    fetch.start()
    fetch.wait()
    shifted = layer == 1
    heads, entries = tab_ref.shape
    straight, down, across = slopes(rel_ref, window)
    first, second = in_ref[layer, 0:1], in_ref[layer, 1:2]
    by_rows = jnp.where(straight, first, second) * down
    by_cols = jnp.where(straight, second, first) * across
    w_s[...] = jnp.concatenate(
        [by_rows, by_cols, bias_ref[layer : layer + 1], jnp.zeros((LANES - 3, by_rows.shape[1]), F32)], axis=0
    ).T
    out_high, out_low = split(outw_ref[layer])
    both_w = jnp.concatenate([out_high, out_low], axis=0)

    def put(i, c):
        cols = lanes_of(c, TABLE_CHUNK)
        source, target = ((hid_s, hid_out), (slope_s, slope_out))[i]
        return pltpu.make_async_copy(source.at[:, cols], target.at[:, cols], sems.at[2 * c + i])

    def chunk_step(c, carry):
        cols = lanes_of(c, TABLE_CHUNK)
        by_row, by_col = entry_logs(c * TABLE_CHUNK, TABLE_CHUNK, window)
        pre = w_s[:, 0:1] * by_row[0:1] + w_s[:, 1:2] * by_col[0:1] + w_s[:, 2:3]
        cdf, density = normal_parts(pre)
        hidden, rest = split(pre * cdf)
        hid_s[:, cols] = hidden
        slope_s[:, cols] = (cdf + pre * density).astype(BF)
        put(0, c).start()
        put(1, c).start()
        both = mm(both_w, hidden)
        logits = both[:heads] + both[heads:] + mm(out_high, rest)
        tab_ref[:, cols] = 16.0 / (1.0 + jnp.exp(-logits))
        return carry

    steps = entries // TABLE_CHUNK
    for c in range(steps):
        chunk_step(c, 0)
    spans = entries // LANES
    wide = rows_ref.shape[2]
    row8 = lax.broadcasted_iota(jnp.int32, (8, LANES), 0)
    lane = lax.broadcasted_iota(jnp.int32, (8, LANES), 1)
    for k in range(wide // LANES):
        at = lane + LANES * k
        low = 2 * window * (LANES * k // window) // LANES
        high = min((2 * window * ((LANES * k + LANES - 1) // window) + 2 * window - 2) // LANES, spans - 1)
        picks = []
        for tile in range(window // 8):
            c1 = column_of(row8 + 8 * tile, window, shifted)
            source = 2 * window * (at // window) + c1 - column_of(at % window, window, shifted) + window - 1
            for s in range(low, high + 1):
                near = source - s * LANES
                inside = (near >= 0) & (near < LANES)
                picks.append((inside, jnp.where(inside, near, 0)))
        for h in range(heads):
            for tile in range(window // 8):
                got = jnp.zeros((8, LANES), F32)
                for s in range(low, high + 1):
                    piece = jnp.broadcast_to(tab_ref[h : h + 1, s * LANES : (s + 1) * LANES], (8, LANES))
                    inside, near = picks[tile * (high + 1 - low) + s - low]
                    got = jnp.where(inside, jnp.take_along_axis(piece, near, axis=1), got)
                rows_ref[h, 8 * tile : 8 * tile + 8, k * LANES : (k + 1) * LANES] = got * LOG2E
    for c in range(steps):
        put(0, c).wait()
        put(1, c).wait()


def bias_table(layer, rel, place_in, place_bias, place_out, window):
    _, heads, hidden = place_out.shape
    entries = 4 * window * window
    wide = ((2 * window - 1) * window + LANES - 1) // LANES * LANES
    sds = jax.ShapeDtypeStruct
    return pl.pallas_call(
        functools.partial(table_kernel, layer, window),
        in_specs=[VM] * 3 + [AN],
        out_specs=[VM] * 2 + [AN] * 2,
        out_shape=[
            sds((heads, window, wide), F32), sds((heads, entries), F32),
            sds((hidden, entries), BF), sds((hidden, entries), BF),
        ],
        scratch_shapes=[
            pltpu.VMEM((hidden, entries), BF), pltpu.VMEM((hidden, entries), BF), pltpu.VMEM((hidden, LANES), F32),
            pltpu.VMEM((32, LANES), jnp.int32),
            pltpu.SemaphoreType.DMA((2 * (entries // TABLE_CHUNK),)),
        ],
        compiler_params=params(),
        name="bias_table_%d" % layer,
    )(place_in, place_bias, place_out, rel)


class Tail:
    def __init__(self, depth, shapes):
        down, up, flow_a, flow_b, small = shapes
        self.depth = depth
        self.ins = list(shapes)
        self.along = Along(depth, ("down", "up"), [down, up])
        self.across = Across(flow_a, flow_b)
        self.after = Along(depth, ("flow", "flow"), self.across.sums)
        every = (2 * small[0],) + small[1:]
        piece = (every[0] // 8,) + small[1:]
        self.outs = [(shape, F32) for shape in self.along.sums + self.after.sums + [every]]
        self.small = 7 + depth - 1 + 7
        self.copies = self.along.copies + self.across.copies + self.after.copies + self.small
        self.scratch = (
            self.along.scratch + self.across.scratch + self.after.scratch
            + [pltpu.VMEM(shape, BF) for shape in self.across.sums]
            + [
                pltpu.VMEM(every, F32), pltpu.VMEM((7,) + piece, F32), pltpu.VMEM((depth - 1,) + piece, F32),
                pltpu.VMEM((7,) + piece, F32), pltpu.VMEM(piece, F32), pltpu.VMEM(piece, F32),
            ]
            + sems_for(self.copies)
        )

    def bind(self, ins, outs, scratch):
        along, across, after, between, small, sems = take(scratch, 2, 6, 2, 2, 6, 2)
        self.other_small, self.out_small, self.sems = ins[4], outs[4], sems
        self.all_s, self.got, self.deep_got, self.back, self.part, self.total = small
        at = 0
        self.along.bind(ins[:2], outs[:2], along, sems, at)
        at += self.along.copies
        self.across.bind(ins[2:4], between, across, sems, at)
        at += self.across.copies
        self.after.bind(between, outs[2:4], after, sems, at)
        self.at = at + self.after.copies

    def fellow(self, step):
        me, core, x, z, y = place()
        other = (core + 2 * x + 4 * y + step) % 8
        return (4 * z + other % 4, other // 4)

    def mine(self, step=0):
        _, core, x, _, y = place()
        return (core + 2 * x + 4 * y + step) % 8

    def rows(self, which):
        size = self.part.shape[0]
        return pl.ds(pl.multiple_of(which * size, size), size)

    def scatter(self, step):
        return remote(
            self.all_s.at[self.rows(self.mine(step))], self.got.at[step - 1], self.sems, self.at + step - 1,
            self.fellow(step),
        )

    def deep(self, step):
        return remote(self.part, self.deep_got.at[step - 1], self.sems, self.at + 6 + step, partner("z", step))

    def gather(self, step):
        return remote(
            self.total, self.back.at[step - 1], self.sems, self.at + 6 + self.depth - 1 + step, self.fellow(step)
        )

    def begin(self):
        barrier = pltpu.get_barrier_semaphore()
        others = [self.fellow(step) for step in range(1, 8)]
        others += [partner("z", step) for step in range(1, self.depth)]
        for other in others:
            pl.semaphore_signal(barrier, inc=1, device_id=other, device_id_type=pl.DeviceIdType.MESH)
        pl.semaphore_wait(barrier, len(others))
        self.across.start()
        self.along.start()

    def end(self, small_ref):
        count = small_ref.shape[0]
        self.all_s[:count] = small_ref[...]
        self.all_s[count:] = self.other_small[...]
        for step in range(1, 8):
            self.scatter(step).start()
        self.across.turn()
        self.along.finish()
        part = self.all_s[self.rows(self.mine())]
        for step in range(1, 8):
            self.scatter(step).wait()
            part = part + self.got[step - 1]
        self.part[...] = part
        for step in range(1, self.depth):
            self.deep(step).start()
        self.across.finish()
        self.after.start()
        for step in range(1, self.depth):
            self.deep(step).wait()
            part = part + self.deep_got[step - 1]
        self.total[...] = part
        for step in range(1, 8):
            self.gather(step).start()
        self.out_small[self.rows(self.mine())] = part
        for step in range(1, 8):
            self.gather(step).wait()
            self.out_small[self.rows(self.mine(8 - step))] = self.back[step - 1]
        self.after.finish()


def table_back_kernel(layer, window, tail, *refs):
    n_in, n_out, n_scratch = (len(tail.ins), len(tail.outs), len(tail.scratch)) if tail else (0, 0, 0)
    (
        (rows_ref, tab_ref, outw_ref, sums_ref), tail_ins, (hid_in, slope_in, rel), (small_ref,), tail_outs,
        (hid_s, slope_s, dlog_s, rel_ref, sems), tail_scratch,
    ) = take(refs, 4, n_in, 3, 1, n_out, 5, n_scratch)
    shifted = layer == 1
    heads, entries = tab_ref.shape
    hidden = hid_s.shape[0]
    steps = entries // TABLE_CHUNK

    def get(i, c):
        cols = lanes_of(c, TABLE_CHUNK)
        source, target = ((hid_in, hid_s), (slope_in, slope_s))[i]
        return pltpu.make_async_copy(source.at[:, cols], target.at[:, cols], sems.at[2 * c + i])

    fetch = pltpu.make_async_copy(rel.at[pl.ds(0, rel_ref.shape[0]), pl.ds(0, LANES)], rel_ref, sems.at[2 * steps])
    fetch.start()
    for c in range(steps):
        get(0, c).start()
        get(1, c).start()
    if tail:
        tail.bind(tail_ins, tail_outs, tail_scratch)
        tail.begin()
    spans = rows_ref.shape[2] // LANES
    row8 = lax.broadcasted_iota(jnp.int32, (8, LANES), 0)
    lane = lax.broadcasted_iota(jnp.int32, (8, LANES), 1)
    for k in range(entries // LANES):
        at = lane + LANES * k
        m = at // (2 * window)
        d = at % (2 * window)
        sums = [jnp.zeros((8, LANES), F32) for _ in range(heads)]
        for tile in range(window // 8):
            c1 = column_of(row8 + 8 * tile, window, shifted)
            c2 = c1 - d + window - 1
            real = (c2 >= 0) & (c2 < window) & (m < 2 * window - 1)
            source = window * m + column_of(c2, window, shifted)
            low = window * (LANES * k // (2 * window)) // LANES
            high = min((window * ((LANES * k + LANES - 1) // (2 * window)) + window - 1) // LANES, spans - 1)
            for s in range(low, high + 1):
                near = source - s * LANES
                inside = (near >= 0) & (near < LANES) & real
                near = jnp.where(inside, near, 0)
                for h in range(heads):
                    piece = rows_ref[h, 8 * tile : 8 * tile + 8, s * LANES : (s + 1) * LANES]
                    picked = jnp.take_along_axis(piece, near, axis=1)
                    sums[h] = sums[h] + jnp.where(inside, picked, 0.0)
        for h in range(heads):
            dlog_s[h : h + 1, k * LANES : (k + 1) * LANES] = jnp.sum(sums[h], axis=0, keepdims=True)
    tab = tab_ref[...]
    dlog_s[...] = dlog_s[...] * tab * (1.0 - tab * 0.0625)
    out_high, out_low = split(outw_ref[layer])
    weights = jnp.concatenate([out_high, out_low, out_high], axis=0)

    def chunk_step(c, carry):
        grads, outs = carry
        cols = lanes_of(c, TABLE_CHUNK)
        by_row, by_col = entry_logs(c * TABLE_CHUNK, TABLE_CHUNK, window)
        low, rest = split(dlog_s[:, cols])
        get(0, c).wait()
        get(1, c).wait()
        outs = outs + mm_nt(jnp.concatenate([low, rest], axis=0), hid_s[:, cols])
        dhid = mm_tn(weights, jnp.concatenate([low, low, rest], axis=0))
        dpre, spare = split(dhid * slope_s[:, cols].astype(F32))
        which = lax.broadcasted_iota(jnp.int32, (16, TABLE_CHUNK), 0)
        pick = lambda y: jnp.broadcast_to(y[0:1], (16, TABLE_CHUNK))
        high_row = by_row.astype(BF).astype(F32)
        high_col = by_col.astype(BF).astype(F32)
        factors = jnp.where(which == 0, pick(high_row), 0.0)
        factors = jnp.where(which == 1, pick(high_col), factors)
        factors = jnp.where(which == 2, 1.0, factors)
        factors = jnp.where(which == 3, pick(by_row - high_row), factors)
        factors = jnp.where(which == 4, pick(by_col - high_col), factors)
        factors = factors.astype(BF)
        grads = grads + mm_nt(factors, dpre) + mm_nt(factors, spare)
        return grads, outs

    grads, outs = lax.fori_loop(
        0, steps, chunk_step, (jnp.zeros((16, hidden), F32), jnp.zeros((2 * heads, hidden), F32))
    )
    fetch.wait()
    straight, down, across = slopes(rel_ref, window)
    by_rows = (grads[0:1] + grads[3:4]) * down
    by_cols = (grads[1:2] + grads[4:5]) * across
    small_ref[:PLACE_OUT] = sums_ref[...]
    small_ref[PLACE_IN : PLACE_IN + 1] = jnp.where(straight, by_rows, by_cols)
    small_ref[PLACE_IN + 1 : PLACE_IN + 2] = jnp.where(straight, by_cols, by_rows)
    small_ref[PLACE_BIAS : PLACE_BIAS + 1] = grads[2:3]
    small_ref[PLACE_OUT:] = outs[:heads] + outs[heads:]
    if tail:
        tail.end(small_ref)


def bias_table_backward(layer, rel, rows, net, place_out, sums, window, left):
    tab, hid, slope = net
    heads, entries = tab.shape
    hidden = hid.shape[0]
    tail = Tail(lax.axis_size("img") // 4, [item.shape for item in left]) if left else None
    sds = jax.ShapeDtypeStruct
    return pl.pallas_call(
        functools.partial(table_back_kernel, layer, window, tail),
        in_specs=[VM] * (4 + len(left)) + [AN] * 3,
        out_specs=[VM] * (1 + (len(tail.outs) if tail else 0)),
        out_shape=[sds((SMALL, hidden), F32)] + ([sds(shape, dt) for shape, dt in tail.outs] if tail else []),
        scratch_shapes=[
            pltpu.VMEM((hidden, entries), BF), pltpu.VMEM((hidden, entries), BF), pltpu.VMEM((heads, entries), F32),
            pltpu.VMEM((32, LANES), jnp.int32), pltpu.SemaphoreType.DMA((2 * (entries // TABLE_CHUNK) + 1,)),
        ] + (tail.scratch if tail else []),
        compiler_params=params(3 if tail else None),
        name="bias_table_backward_%d" % layer,
    )(rows, tab, place_out, sums, *left, hid, slope, rel)


def final_kernel(window, depth, split_matrices, *refs):
    (
        (in_ref, small_ref), matrices, (out_ref, dx_ref),
        (
            output, input_grad, qkv_grad, qv_grad, scale_grad, place_in_grad, place_bias_grad, place_out_grad,
            proj_grad, up_grad, up_bias_grad, down_grad, out_bias_grad, gain_grad, shift_grad,
        ),
        (dx_s, out_s, sems),
    ) = take(refs, 2, len(refs) - 22, 2, 15, 3)
    half = out_ref.shape[0] // 2
    width = out_ref.shape[1]
    top, bottom = pl.ds(0, half), pl.ds(half, half)
    hops = [
        (dx_ref.at[top], dx_s.at[top], input_grad.at[top]),
        (dx_ref.at[bottom], dx_s.at[bottom], input_grad.at[bottom]),
        (out_ref.at[top], out_s.at[bottom], output.at[bottom]),
    ]
    loads = [pltpu.make_async_copy(hop[0], hop[1], sems.at[i]) for i, hop in enumerate(hops)]
    stores = [pltpu.make_async_copy(hop[1], hop[2], sems.at[3 + i]) for i, hop in enumerate(hops)]
    stores.append(pltpu.make_async_copy(out_s.at[top], output.at[top], sems.at[6]))
    for load in loads:
        load.start()
    out_s[top] = in_ref[...].astype(F32)
    stores[3].start()
    for load, store in zip(loads, stores):
        load.wait()
        store.start()
    small = small_ref
    wide = width // 2
    for b in range(2):
        if split_matrices:
            down, up, flow_a, flow_b = matrices[4 * b : 4 * b + 4]
            upper = lax.axis_index("rows") == 0
            qkv_grad[b, :, :wide] = jnp.where(upper, flow_a[0], flow_a[1])
            qkv_grad[b, :, wide : 2 * wide] = jnp.where(upper, flow_a[1], flow_a[0])
            qkv_grad[b, :, 2 * wide :] = jnp.where(upper, flow_b[0], flow_b[1])
            proj_grad[b] = jnp.where(upper, flow_b[1], flow_b[0])
            part = up.shape[2]
            for c in range(2):
                up_grad[b, :, c * part : (c + 1) * part] = up[c]
        else:
            qkv, proj, up, down = matrices[4 * b : 4 * b + 4]
            qkv_grad[b] = qkv[...]
            proj_grad[b] = proj[...]
            up_grad[b] = up[...]
        down_grad[b] = down[...]
        at = b * SMALL
        for i in range(4):
            up_bias_grad[b : b + 1, i * width : (i + 1) * width] = small[at + UP_BIAS + i : at + UP_BIAS + i + 1]
        qv_grad[b] = small[at + QV : at + QV + 2]
        out_bias_grad[b] = small[at + OUT_BIAS : at + OUT_BIAS + 2]
        gain_grad[b] = small[at + GAIN : at + GAIN + 2]
        shift_grad[b] = small[at + SHIFT : at + SHIFT + 2]
        place_in_grad[b] = small[at + PLACE_IN : at + PLACE_IN + 2]
        place_bias_grad[b : b + 1] = small[at + PLACE_BIAS : at + PLACE_BIAS + 1]
        place_out_grad[b] = small[at + PLACE_OUT : at + SMALL]
        heads = width // depth
        head = lax.broadcasted_iota(jnp.int32, (heads, width), 0)
        owner = lax.broadcasted_iota(jnp.int32, (heads, width), 1) // depth
        logit = jnp.where(head == owner, small[at + LOGIT : at + LOGIT + 1], 0.0)
        scale_grad[b : b + 1] = jnp.sum(logit, axis=1, keepdims=True).T
    for store in stores:
        store.wait()


def final_outputs(out, incoming, dx, small, matrices, shapes, window, depth, split_matrices):
    ins = [incoming, small] + list(matrices)
    return pl.pallas_call(
        functools.partial(final_kernel, window, depth, split_matrices),
        in_specs=[VM] * len(ins) + [AN] * 2,
        out_specs=[AN] * 2 + [VM] * (len(shapes) - 2),
        out_shape=[jax.ShapeDtypeStruct(shape, F32) for shape in shapes],
        scratch_shapes=[pltpu.VMEM(out.shape, F32), pltpu.VMEM(out.shape, F32), pltpu.SemaphoreType.DMA((7,))],
        compiler_params=params(),
        name="final_outputs",
    )(*ins, out, dx)


def shares(array, images, bands):
    rows, cols = array.shape
    cut = array.reshape(images, rows // images, bands, cols // bands)
    return jnp.transpose(cut, (0, 2, 1, 3)).reshape(images * bands, -1)


def summed_shares(arrays):
    images, bands = lax.axis_size("img"), lax.axis_size("rows")
    joined = jnp.concatenate([shares(array, images, bands) for array in arrays], axis=1)
    mine = lax.psum_scatter(joined, ("img", "rows"), scatter_dimension=0, tiled=True)
    mine = mine.reshape(-1).astype(F32)
    out = []
    at = 0
    for array in arrays:
        rows, cols = array.shape[0] // images, array.shape[1] // bands
        out.append(mine[at : at + rows * cols].reshape(rows, cols))
        at += rows * cols
    return out


def per_device(
    inputs,
    cotangent,
    region,
    rel_index,
    qkv_weight,
    qv_bias,
    logit_scale,
    place_in,
    place_bias,
    place_out,
    proj_weight,
    up_weight,
    up_bias,
    down_weight,
    out_bias,
    norm_gain,
    norm_shift,
):
    window, width = inputs.shape[2], inputs.shape[3]
    heads = logit_scale.shape[1]
    depth = width // heads
    tokens = window * window
    half = tokens // 2
    ff = up_weight.shape[2]
    images, bands = lax.axis_size("img"), lax.axis_size("rows")
    riding = images * bands == 32 and bands == 2
    x = inputs.reshape(tokens, width)
    cot = cotangent.reshape(tokens, width)
    cot_low = cot[:half].astype(BF)
    vectors = (qv_bias, out_bias, norm_gain, norm_shift, logit_scale, up_bias)
    turned_out = jnp.transpose(place_out, (0, 2, 1))
    weights = (qkv_weight, proj_weight, up_weight, down_weight)
    table_zero, *net_zero = bias_table(0, rel_index, place_in, place_bias, turned_out, window)
    hidden, sent, *saved_zero = block_forward(0, (x,), (), vectors, table_zero, weights, window, heads)
    came = passed_along(sent, "rows", -1)
    table_one, *net_one = bias_table(1, rel_index, place_in, place_bias, turned_out, window)
    cot_low, table_one = lax.optimization_barrier((cot_low, table_one))
    cot_in = passed_along(cot_low, "rows", -1)
    shifted_out, sent, *saved_one = block_forward(
        1, (hidden, came), (region.reshape(window, window),), vectors, table_one, weights, window, heads
    )
    out_in = passed_along(sent, "rows", 1)

    def backward(b, own, incoming, saved, left):
        return block_backward(
            b, own, incoming, norm_gain, logit_scale, saved, weights, table_zero.shape, window, heads, riding, left
        )

    def pull(b, rows, net, sums, left=()):
        return bias_table_backward(b, rel_index, rows, net, turned_out, sums, window, left)

    dx_one, sent, sums_one, rows_one, *left = backward(1, cot, cot_in, saved_one, ())
    came = passed_along(sent, "rows", 1)
    (small_one,) = pull(1, rows_one, net_one, sums_one)
    if riding:
        dx_zero, _, sums_zero, rows_zero, *left = backward(0, dx_one, came, saved_zero, left)
        matrices_one = left[4:]
        _, *matrices_zero, small = pull(0, rows_zero, net_zero, sums_zero, (*left[:4], small_one))
    else:
        down, up, proj, qkv = left
        matrix = lambda qkv: jnp.transpose(qkv, (1, 0, 2)).reshape(width, 3 * width)
        matrices_one = summed_shares((matrix(qkv), proj, up, down))
        dx_zero, _, sums_zero, rows_zero, down, up, proj, qkv = backward(0, dx_one, came, saved_zero, ())
        matrices_zero = summed_shares((matrix(qkv), proj, up, down))
        (small_zero,) = pull(0, rows_zero, net_zero, sums_zero)
        small = lax.psum(jnp.concatenate([small_zero, small_one], axis=0), ("img", "rows"))
    cut = lambda rows, cols: (2, rows // images, cols // bands)
    shapes = [
        (tokens, width), (tokens, width), cut(width, 3 * width), (2, 2, width), (2, heads), (2, 2, width), (2, width),
        (2, heads, width), cut(width, width), cut(width, ff), (2, ff), cut(ff, width), (2, 2, width), (2, 2, width),
        (2, 2, width),
    ]
    output, input_grad, *rest = final_outputs(
        shifted_out, out_in, dx_zero, small, list(matrices_zero) + list(matrices_one), shapes, window, depth, riding
    )
    rest[5] = jnp.transpose(rest[5], (0, 2, 1))
    return (output.reshape(inputs.shape), input_grad.reshape(inputs.shape), *rest)


def solution(mesh):
    token = P("img", "rows", None, None)
    matrix = P(None, "img", "rows")
    return jax.shard_map(
        per_device,
        mesh=mesh,
        in_specs=(token, token, P("img", "rows", None)) + (P(),) * 14,
        out_specs=(
            token, token, matrix, P(), P(), P(), P(), P(), matrix, matrix, P(), matrix, P(), P(), P(),
        ),
        check_vma=False,
    )
```

```python
import functools

import jax
import jax.numpy as jnp
from jax import lax
from jax.experimental import pallas as pl
from jax.experimental.pallas import tpu as pltpu
from jax.sharding import PartitionSpec as P

BF = jnp.bfloat16
F32 = jnp.float32
LOG2E = 1.4426950408889634
MASKED = 1.0e9
LANES = 128


def passed_along(array, axis, by):
    devices = lax.axis_size(axis)
    return lax.ppermute(array, axis, [(i, (i + by) % devices) for i in range(devices)])


def mm(a, b):
    return lax.dot_general(a, b, (((1,), (0,)), ((), ())), preferred_element_type=F32)


def mm_nt(a, b):
    return lax.dot_general(a, b, (((1,), (1,)), ((), ())), preferred_element_type=F32)


def mm_tn(a, b):
    return lax.dot_general(a, b, (((0,), (0,)), ((), ())), preferred_element_type=F32)


def group_ones(depth):
    rows = lax.broadcasted_iota(jnp.int32, (LANES, LANES), 0) // depth
    cols = lax.broadcasted_iota(jnp.int32, (LANES, LANES), 1) // depth
    return jnp.where(rows == cols, 1.0, 0.0).astype(BF)


def group_sums(ones, first, second):
    rows = first.shape[0]
    both = group_sum(ones, jnp.concatenate([first, second], axis=0))
    return both[:rows], both[rows:]


def group_sum(ones, values):
    high, low = split(values)
    return mm(jnp.concatenate([high, low], axis=1), jnp.concatenate([ones, ones], axis=0))


def split(values):
    high = values.astype(BF)
    return high, (values - high.astype(F32)).astype(BF)


def head_scales(logit_ref, layer, width):
    heads = logit_ref.shape[1]
    column = jnp.broadcast_to(logit_ref[layer : layer + 1], (heads, heads)).T[:, :1]
    head = lax.broadcasted_iota(jnp.int32, (heads, width), 0)
    owner = lax.broadcasted_iota(jnp.int32, (heads, width), 1) // (width // heads)
    return jnp.exp(jnp.sum(jnp.where(head == owner, column, 0.0), axis=0, keepdims=True))


def normal_parts(values):
    cdf = 0.5 + 0.5 * lax.erf(values * 0.7071067811865476)
    return cdf, jnp.exp2(values * values * (-0.5 * LOG2E)) * 0.3989422804014327


def norm_stats(values):
    centre = values - jnp.mean(values, axis=-1, keepdims=True)
    spread = jnp.mean(centre * centre, axis=-1, keepdims=True)
    rstd = lax.rsqrt(spread + 1e-05)
    return centre * rstd, rstd


def norm_pull(values, gain, grad):
    hat, rstd = norm_stats(values)
    scaled = grad * gain
    first = jnp.mean(scaled, axis=-1, keepdims=True)
    second = jnp.mean(scaled * hat, axis=-1, keepdims=True)
    pulled = rstd * (scaled - first - hat * second)
    gain_grad = jnp.sum(grad * hat, axis=0, keepdims=True)
    shift_grad = jnp.sum(grad, axis=0, keepdims=True)
    return pulled, gain_grad, shift_grad


def place():
    me, y = lax.axis_index("img"), lax.axis_index("rows")
    return me, me % 2, (me // 2) % 2, me // 4, y


def partner(which, step=1):
    me, core, x, z, y = place()
    if which == "core":
        return (me + 1 - 2 * core, y)
    if which == "x":
        return (me + 2 - 4 * x, y)
    if which == "y":
        return (me, 1 - y)
    depth = lax.axis_size("img") // 4
    return ((z + step) % depth * 4 + me % 4, y)


def greet(which):
    depth = lax.axis_size("img") // 4
    others = []
    for name in which:
        others += [partner("z", step) for step in range(1, depth)] if name == "z" else [partner(name)]
    barrier = pltpu.get_barrier_semaphore()
    for other in others:
        pl.semaphore_signal(barrier, inc=1, device_id=other, device_id_type=pl.DeviceIdType.MESH)
    pl.semaphore_wait(barrier, len(others))


def remote(source, target, sems, at, device):
    return pltpu.make_async_remote_copy(
        src_ref=source, dst_ref=target, send_sem=sems[0].at[at], recv_sem=sems[1].at[at],
        device_id=device, device_id_type=pl.DeviceIdType.MESH,
    )


def half_at(index, size):
    return pl.ds(pl.multiple_of(index * size, LANES), size)


class Across:
    copies = 4

    def __init__(self, first, second):
        self.sums = [first[2:], second[2:]]
        self.scratch = []
        for shape in (first, second):
            self.scratch += [pltpu.VMEM(shape[1:], BF), pltpu.VMEM(shape[1:], BF), pltpu.VMEM(shape[2:], BF)]

    def bind(self, ins, outs, scratch, sems, base):
        self.flows = [(ins[i], outs[i]) + tuple(scratch[3 * i : 3 * i + 3]) for i in range(2)]
        self.sems, self.base = sems, base

    def axes(self, flow):
        _, _, x, _, y = place()
        return (("x", x), ("y", y)) if flow == 0 else (("y", y), ("x", x))

    def copy(self, flow, stage):
        source, _, got, sums, last = self.flows[flow]
        name, here = self.axes(flow)[stage]
        if stage == 0:
            return remote(source.at[1 - here], got, self.sems, self.base + flow, partner(name))
        return remote(sums.at[1 - here], last, self.sems, self.base + 2 + flow, partner(name))

    def start(self):
        self.copy(0, 0).start()
        self.copy(1, 0).start()

    def turn(self):
        for flow in range(2):
            source, _, got, sums, _ = self.flows[flow]
            here = self.axes(flow)[0][1]
            self.copy(flow, 0).wait()
            sums[...] = source[here] + got[...]
            self.copy(flow, 1).start()

    def finish(self):
        for flow in range(2):
            _, out, _, sums, last = self.flows[flow]
            here = self.axes(flow)[1][1]
            self.copy(flow, 1).wait()
            out[...] = sums[here] + last[...]


PICKS = {
    "down": lambda z: (z % 2, z // 2),
    "up": lambda z: (slice(None), z),
    "flow": lambda z: (slice(None), z),
}


class Along:
    def __init__(self, depth, kinds, shapes):
        self.depth = depth
        self.picks = [PICKS[kind] for kind in kinds]
        drop = {"down": lambda shape: shape[2:], "up": lambda shape: shape[:1] + shape[2:], "flow": lambda shape: shape[:1] + shape[2:]}
        self.sums = [drop[kind](shape) for kind, shape in zip(kinds, shapes)]
        self.scratch = [pltpu.VMEM((depth - 1,) + shape, BF) for shape in self.sums]
        self.copies = (depth - 1) * len(shapes)

    def bind(self, ins, outs, scratch, sems, base):
        self.ins, self.outs, self.got = ins, outs, scratch
        self.sems, self.base = sems, base

    def each(self):
        _, _, _, z, _ = place()
        for i, (source, got, pick) in enumerate(zip(self.ins, self.got, self.picks)):
            for step in range(1, self.depth):
                at = self.base + i * (self.depth - 1) + step - 1
                share = source.at[pick((z + step) % self.depth)]
                yield remote(share, got.at[step - 1], self.sems, at, partner("z", step))

    def start(self):
        for copy in self.each():
            copy.start()

    def finish(self):
        _, _, _, z, _ = place()
        for copy in self.each():
            copy.wait()
        for source, out, got, pick in zip(self.ins, self.outs, self.got, self.picks):
            total = source[pick(z)].astype(F32)
            for step in range(1, self.depth):
                total = total + got[step - 1].astype(F32)
            out[...] = total


def sems_for(count):
    return [pltpu.SemaphoreType.DMA((count,)), pltpu.SemaphoreType.DMA((count,))]


def take(refs, *counts):
    out = []
    at = 0
    for count in counts:
        out.append(refs[at : at + count])
        at += count
    assert at == len(refs), (at, len(refs))
    return out


def whole(shape):
    return pl.BlockSpec(shape, lambda *s: (0,) * len(shape))


VM = pl.BlockSpec(memory_space=pltpu.VMEM)
AN = pl.BlockSpec(memory_space=pl.ANY)
LIMIT = 62 * 2**20


def params(number=None):
    if number is None:
        return pltpu.CompilerParams(vmem_limit_bytes=LIMIT)
    return pltpu.CompilerParams(vmem_limit_bytes=LIMIT, collective_id=number, has_side_effects=True)


def lanes_of(group, size=LANES):
    return pl.ds(pl.multiple_of(group * size, size), size)


CHUNK = 512


def forward_kernel(layer, window, depth, *refs):
    masked = layer == 1
    tokens = window * window
    width = refs[0].shape[1]
    groups = width // LANES
    per = LANES // depth
    (
        x_refs, region_refs, (qv_ref, ob_ref, gain_ref, shift_ref, logit_ref, ub_ref),
        (bias, wqkv, wp, wu, wd), (out_ref, send_ref), saved, keep, (z_s, m_s, qkv_s, scale_s, qm_s, km_s, bias_ref),
        (wqkv_s, wp_s, wu_s, wd_s), (load, store),
    ) = take(refs, 2 if masked else 1, 1 if masked else 0, 6, 5, 2, 14, 14, 7, 4, 2)
    chunks = ub_ref.shape[1] // CHUNK
    e_s, qn_s, kn_s, v_s, o_s, iq_s, ik_s, rinv_s, p_s, a_s, zr_s, g_s, gd_s, mo_s = keep
    lane = lax.broadcasted_iota(jnp.int32, (1, LANES), 1) // depth

    def load_qkv(i):
        return pltpu.make_async_copy(wqkv.at[layer, :, lanes_of(i, width)], wqkv_s.at[i], load.at[i])

    def load_rest(i):
        source, target = ((wp, wp_s), (wu, wu_s), (wd, wd_s))[i]
        return pltpu.make_async_copy(source.at[layer], target, load.at[3 + i])

    def put(i):
        return pltpu.make_async_copy(keep[i], saved[i], store.at[i])

    def put_p(g):
        rows = pl.ds(g * per, per)
        return pltpu.make_async_copy(p_s.at[rows], saved[8].at[rows], store.at[14 + g])

    def put_g(i, c):
        cols = lanes_of(c, CHUNK)
        return pltpu.make_async_copy(
            keep[11 + i].at[:, cols], saved[11 + i].at[:, cols], store.at[14 + groups + 2 * c + i]
        )

    load_bias = pltpu.make_async_copy(bias, bias_ref, load.at[6])
    for i in range(3):
        load_qkv(i).start()
    load_bias.start()
    for i in range(3):
        load_rest(i).start()
    scale_s[...] = head_scales(logit_ref, layer, width) * LOG2E
    ones = group_ones(depth)
    if masked:
        token = lax.broadcasted_iota(jnp.int32, (tokens, window), 0)
        place_in_row = lax.broadcasted_iota(jnp.int32, (tokens, window), 1)
        rows_pick = jnp.where(token // window == place_in_row, 1.0, 0.0).astype(BF)
        labels = mm(rows_pick, region_refs[0][...].astype(F32).astype(BF))
        mine = column_of(token % window, window, True) == place_in_row
        labels = jnp.sum(jnp.where(mine, labels, 0.0), axis=1, keepdims=True)
        each = lax.broadcasted_iota(jnp.int32, (tokens, LANES), 1)
        same = labels == each.astype(F32)
        qm_s[...] = jnp.where(same, 1.0, 0.0).astype(BF)
        km_s[...] = jnp.where(same | (each >= 8), 0.0, -MASKED).astype(BF)
    half = tokens // 2
    if masked:
        z_s[:half] = x_refs[0][half:]
        z_s[half:] = x_refs[1][...].astype(F32)
        x_ref = z_s
    else:
        x_ref = x_refs[0]
    e_s[...] = x_ref[...].astype(BF)
    put(0).start()
    for i in range(3):
        load_qkv(i).wait()
        raw = mm(e_s[...], wqkv_s[i])
        if i != 1:
            raw = raw + qv_ref[layer, i // 2 : i // 2 + 1]
        qkv_s[i] = raw
    load_bias.wait()

    def group_step(g, carry):
        cols = lanes_of(g)
        q = qkv_s[0, :, cols]
        k = qkv_s[1, :, cols]
        v = qkv_s[2, :, cols]
        iq, ik = group_sums(ones, q * q, k * k)
        iq = lax.rsqrt(iq + 1e-06)
        ik = lax.rsqrt(ik + 1e-06)
        qn = q * iq
        kn = (k * ik).astype(BF)
        iq_s[:, cols] = iq
        ik_s[:, cols] = ik
        qn_s[:, cols] = qn.astype(BF)
        kn_s[:, cols] = kn
        v_s[:, cols] = v.astype(BF)
        scales = scale_s[:, cols]
        rhs = jnp.concatenate([kn, km_s[...]], axis=1) if masked else kn
        mixed = jnp.zeros((tokens, LANES), F32)
        total = mixed
        for h in range(per):
            mine = lane == h
            lhs = jnp.where(mine, qn, 0.0).astype(BF)
            if masked:
                lhs = jnp.concatenate([lhs, qm_s[...]], axis=1)
            cosine = mm_nt(lhs, rhs)
            scale = scales[:, h * depth : h * depth + 1]
            table = bias_ref[g * per + h]
            for pair in range(window // 2):
                parts = []
                for r in (2 * pair, 2 * pair + 1):
                    at = window * (window - 1 - r)
                    parts.append(
                        cosine[r * window : (r + 1) * window] * scale + table[:, at : at + tokens]
                    )
                both = jnp.concatenate(parts, axis=0)
                p_s[g * per + h, 2 * pair * window : (2 * pair + 2) * window, :] = jnp.exp2(both).astype(BF)
            both = mm(p_s[g * per + h], jnp.where(mine, v, 1.0).astype(BF))
            mixed = jnp.where(mine, both, mixed)
            total = jnp.where(lane == (h + 1) % per, both, total)
        rinv = pltpu.roll(1.0 / total, LANES - depth, 1)
        rinv_s[:, cols] = rinv
        o_s[:, cols] = mixed * rinv
        put_p(g).start()
        return carry

    lax.fori_loop(0, groups, group_step, 0)
    for i in range(1, 8):
        put(i).start()
    load_rest(0).wait()
    a = mm(o_s[...].astype(BF), wp_s[...]) + ob_ref[layer, 0:1]
    a_s[...] = a
    put(9).start()
    hat, _ = norm_stats(a)
    z = x_ref[...] + (hat * gain_ref[layer, 0:1] + shift_ref[layer, 0:1])
    z_s[...] = z
    zr_s[...] = z.astype(BF)
    put(10).start()
    m_s[...] = jnp.zeros_like(m_s)
    load_rest(1).wait()
    load_rest(2).wait()

    def chunk_step(c, carry):
        cols = lanes_of(c, CHUNK)
        pre = mm(zr_s[...], wu_s[:, cols]) + ub_ref[layer : layer + 1, cols]
        cdf, density = normal_parts(pre)
        act = (pre * cdf).astype(BF)
        g_s[:, cols] = act
        gd_s[:, cols] = (cdf + pre * density).astype(BF)
        put_g(0, c).start()
        put_g(1, c).start()
        m_s[...] += mm(act, wd_s[cols, :])
        return carry

    lax.fori_loop(0, chunks, chunk_step, 0)
    m = m_s[...] + ob_ref[layer, 1:2]
    mo_s[...] = m
    put(13).start()
    hat, _ = norm_stats(m)
    out = z_s[...] + (hat * gain_ref[layer, 1:2] + shift_ref[layer, 1:2])
    out_ref[...] = out
    send_ref[...] = (out[half:] if masked else out[:half]).astype(BF)
    for i in range(14):
        if i not in (8, 11, 12):
            put(i).wait()
    for g in range(groups):
        put_p(g).wait()
    for c in range(chunks):
        put_g(0, c).wait()
        put_g(1, c).wait()


def block_forward(layer, xs, region, vectors, table, weights, window, heads):
    tokens, width = window * window, xs[0].shape[1]
    depth = width // heads
    w_qkv, w_proj, w_up, w_down = weights
    ff = w_up.shape[2]
    groups = width // LANES
    sds = jax.ShapeDtypeStruct
    tok = lambda dt, cols=width: sds((tokens, cols), dt)
    saved = [
        tok(BF), tok(BF), tok(BF), tok(BF), tok(F32), tok(F32), tok(F32), tok(F32),
        sds((heads, tokens, tokens), BF), tok(F32), tok(BF), tok(BF, ff), tok(BF, ff), tok(F32),
    ]
    ins = list(xs) + list(region) + list(vectors)
    stores = 14 + groups + 2 * (ff // CHUNK)
    return pl.pallas_call(
        functools.partial(forward_kernel, layer, window, depth),
        in_specs=[VM] * len(ins) + [AN] * 5,
        out_specs=[VM] * 2 + [AN] * 14,
        out_shape=[tok(F32), sds((tokens // 2, width), BF)] + saved,
        scratch_shapes=[pltpu.VMEM(item.shape, item.dtype) for item in saved]
        + [
            pltpu.VMEM((tokens, width), F32), pltpu.VMEM((tokens, width), F32), pltpu.VMEM((3, tokens, width), F32),
            pltpu.VMEM((1, width), F32), pltpu.VMEM((tokens, LANES), BF), pltpu.VMEM((tokens, LANES), BF),
            pltpu.VMEM(table.shape, F32),
            pltpu.VMEM((3, width, width), BF), pltpu.VMEM((width, width), BF),
            pltpu.VMEM((width, ff), BF), pltpu.VMEM((ff, width), BF),
            pltpu.SemaphoreType.DMA((7,)), pltpu.SemaphoreType.DMA((stores,)),
        ],
        compiler_params=params(),
        name="block_forward_%d" % layer,
    )(*ins, table, w_qkv, w_proj, w_up, w_down)


UP_BIAS, QV, OUT_BIAS, GAIN, SHIFT, PLACE_IN, PLACE_BIAS, LOGIT, PLACE_OUT = 0, 4, 6, 8, 10, 12, 14, 15, 16
SMALL = 32


class Plan:
    def __init__(self, width, ff, images, follows):
        deep = images // 4
        self.deep = deep
        self.down = (2, 2, 2, 2, deep // 2, ff // images, width // 2)
        self.up = (2, 2, 2, 2, deep, width // images, ff // 4)
        half = lambda shape: shape[:1] + shape[2:]
        self.half_down, self.half_up = half(self.down), half(self.up)
        self.flow = (2, 2, 2, 2, deep, width // images, width // 2)
        self.got_flow = half(self.flow)
        self.half_flow = self.flow[2:4] + (2,) + self.flow[4:]
        self.parts = [Across(self.half_down[1:], self.half_up[1:]) for _ in range(2)]
        sums = [(2,) + shape for shape in self.parts[0].sums]
        self.outs = [(shape, BF) for shape in sums] + [(self.half_flow, BF)] * 2
        self.scratch = [pltpu.VMEM(shape, BF) for shape in (
            self.down, self.up, self.half_down, self.half_up, self.flow, self.flow, self.got_flow, self.got_flow,
        )] + self.parts[0].scratch + self.parts[1].scratch
        self.core = 8
        self.copies = self.core + 8
        self.ins = []
        self.follows = follows
        if follows:
            self.old = Along(deep, ("down", "up"), sums)
            self.turned = Across(self.half_flow, self.half_flow)
            self.late = Along(deep, ("flow", "flow"), self.turned.sums)
            self.ins = sums + [self.half_flow] * 2
            self.outs += [(shape, F32) for shape in self.old.sums + self.late.sums]
            self.scratch += [pltpu.VMEM(shape, BF) for shape in self.turned.sums]
            self.scratch += self.old.scratch + self.turned.scratch + self.late.scratch
            self.copies += self.old.copies + self.turned.copies + self.late.copies
        self.scratch = self.scratch + sems_for(self.copies)

    def bind(self, ins, outs, scratch):
        sems = scratch[-2:]
        self.sems = sems
        self.down_s, self.up_s, self.got_down, self.got_up = scratch[:4]
        self.flows = ((scratch[4], scratch[6]), (scratch[5], scratch[7]))
        self.flow_outs = outs[2:4]
        for c, part in enumerate(self.parts):
            part.bind(
                [self.got_down.at[c], self.got_up.at[c]], [outs[0].at[c], outs[1].at[c]],
                scratch[8 + 6 * c : 14 + 6 * c], sems, self.core + 4 * c,
            )
        if self.follows:
            rest = scratch[20:-2]
            at = self.core + 8
            between, old, turned, late = take(rest, 2, 2, 6, 2)
            self.old.bind(ins[:2], outs[4:6], old, sems, at)
            at += self.old.copies
            self.turned.bind(ins[2:4], between, turned, sems, at)
            at += self.turned.copies
            self.late.bind(between, outs[6:8], late, sems, at)

    def feed_copy(self, c, which):
        _, core, _, _, _ = place()
        source, target = ((self.down_s, self.got_down), (self.up_s, self.got_up))[which]
        return remote(source.at[c, 1 - core], target.at[c], self.sems, 2 * c + which, partner("core"))

    def flow_copy(self, part, flow):
        _, core, _, _, _ = place()
        source, target = self.flows[flow]
        return remote(source.at[part, 1 - core], target.at[part], self.sems, 4 + 2 * part + flow, partner("core"))

    def begin(self):
        greet(["core", "x", "y"] + (["z"] if self.follows else []))
        if self.follows:
            self.turned.start()
            self.old.start()

    def feed_step(self, c, down, up):
        rows = self.down[5]
        wide = self.down[6]
        for i in range(2):
            for x in range(2):
                for core in range(2):
                    at = i * CHUNK + (2 * x + core) * rows
                    for y in range(2):
                        self.down_s[c, core, x, y, i] = down[at : at + rows, y * wide : (y + 1) * wide]
        self.feed_copy(c, 0).start()
        self.spread(self.up_s, c, 1, None, up)
        self.feed_copy(c, 1).start()

    def spread(self, target, part, flow, y, block, cols=slice(None)):
        for half in (0, 1) if y is None else (y,):
            piece = block
            if y is None:
                wide = block.shape[1] // 2
                piece = block[:, half * wide : (half + 1) * wide]
            piece = piece.reshape((self.deep, 2, 2, -1, piece.shape[1]))
            for x in range(2):
                for core in range(2):
                    first, second = (x, half) if flow == 0 else (half, x)
                    target[part, core, first, second, :, :, cols] = piece[:, x, core]

    def ready(self, c):
        _, core, _, _, _ = place()
        self.feed_copy(c, 0).wait()
        self.got_down[c] = self.got_down[c] + self.down_s[c, core]
        self.feed_copy(c, 1).wait()
        self.got_up[c] = self.got_up[c] + self.up_s[c, core]
        self.parts[c].start()

    def midway(self):
        self.ready(0)

    def between(self, proj):
        flow_b = self.flows[1][0]
        half = proj.shape[1] // 2
        self.spread(flow_b, 0, 1, 1, proj[:, half:])
        self.spread(flow_b, 1, 1, 0, proj[:, :half])
        self.ready(1)
        if self.follows:
            self.turned.turn()
            self.old.finish()
        self.parts[0].turn()

    def attend_begin(self, half):
        @pl.when(half == 1)
        def _():
            self.parts[1].turn()
            if self.follows:
                self.turned.finish()
                self.late.start()

    def attend_step(self, half, grads):
        flow_a, flow_b = self.flows[0][0], self.flows[1][0]
        wide = grads.shape[1] // 3
        q, k, v = (grads[:, i * wide : (i + 1) * wide] for i in range(3))

        @pl.when(half == 0)
        def _():
            self.spread(flow_b, 0, 1, 0, k)
            self.flow_copy(0, 1).start()
            self.spread(flow_a, 0, 0, 0, q)
            self.spread(flow_a, 0, 0, 1, v)
            self.flow_copy(0, 0).start()

        @pl.when(half == 1)
        def _():
            self.spread(flow_b, 1, 1, 1, v)
            self.flow_copy(1, 1).start()
            self.spread(flow_a, 1, 0, 0, q)
            self.spread(flow_a, 1, 0, 1, k)
            self.flow_copy(1, 0).start()

    def end(self):
        _, core, _, _, _ = place()
        self.parts[0].finish()
        for part in range(2):
            for flow in (1, 0):
                source, got = self.flows[flow]
                self.flow_copy(part, flow).wait()
                self.flow_outs[flow][:, :, part] = source[part, core] + got[part]
        if self.follows:
            self.late.finish()
        self.parts[1].finish()


def backward_kernel(layer, window, depth, plan, *refs):
    tokens = window * window
    half = tokens // 2
    n_plan_in = len(plan.ins) if plan else 0
    n_plan_out = len(plan.outs) if plan else 4
    n_plan_scratch = len(plan.scratch) if plan else 0
    (
        (own_ref, in_ref, gain_ref, logit_ref), plan_ins, saved, (wqkv, wp, wu, wd),
        (dx_ref, send_ref, sums_ref, table_out), plan_outs, keep,
        (wqkv_s, wp_s, wu_s, wd_s, dm_s, do_s, ds_s, scale_s, table_ref, load), plan_scratch,
    ) = take(refs, 4, n_plan_in, 14, 4, 4, n_plan_out, 14, 10, n_plan_scratch)
    e_s, qn_s, kn_s, v_s, o_s, iq_s, ik_s, rinv_s, p_s, a_s, zr_s, g_s, gd_s, m_s = keep
    width = own_ref.shape[1]
    ff = g_s.shape[1]
    groups = width // LANES
    per = LANES // depth
    chunks = ff // CHUNK
    wide = tokens
    lane = lax.broadcasted_iota(jnp.int32, (1, LANES), 1)

    def load_kept(i):
        return pltpu.make_async_copy(saved[i], keep[i], load.at[i])

    def load_p(g):
        return pltpu.make_async_copy(saved[8].at[pl.ds(g * per, per)], p_s.at[g % 2], load.at[14 + g])

    def put_table(half):
        rows = pl.ds(half * 2 * per, 2 * per)
        return pltpu.make_async_copy(
            table_ref.at[rows], table_out.at[rows], load.at[16 + groups + 4 * chunks + half]
        )

    def load_weights(i):
        source, target = ((wqkv, wqkv_s), (wp, wp_s))[i]
        return pltpu.make_async_copy(source.at[layer], target, load.at[14 + groups + i])

    def load_chunk(c):
        here = lanes_of(c, CHUNK)
        cols = lanes_of(c // 2 + c % 2 * 2, CHUNK)
        at = 16 + groups + 4 * c
        return [
            pltpu.make_async_copy(saved[11].at[:, cols], g_s.at[:, here], load.at[at]),
            pltpu.make_async_copy(saved[12].at[:, cols], gd_s.at[:, here], load.at[at + 1]),
            pltpu.make_async_copy(wd.at[layer, cols], wd_s.at[here], load.at[at + 2]),
            pltpu.make_async_copy(wu.at[layer, :, cols], wu_s.at[:, here], load.at[at + 3]),
        ]

    load_kept(13).start()
    load_kept(10).start()
    for c in range(chunks):
        for copy in load_chunk(c):
            copy.start()
    load_kept(9).start()
    load_kept(4).start()
    load_weights(1).start()
    if plan:
        plan.bind(plan_ins, plan_outs, plan_scratch)
        plan.begin()
    if layer == 1:
        dx_ref[:half] = own_ref[half:]
        dx_ref[half:] = in_ref[...].astype(F32)
    else:
        dx_ref[:half] = in_ref[...].astype(F32)
        dx_ref[half:] = own_ref[:half]
    scale_s[...] = head_scales(logit_ref, layer, width)
    ones = group_ones(depth)
    load_kept(13).wait()
    dm, gain_grad, shift_grad = norm_pull(m_s[...], gain_ref[layer, 1:2], dx_ref[...])
    low = dm.astype(BF)
    dm_s[...] = low
    sums_ref[...] = jnp.zeros_like(sums_ref)
    sums_ref[OUT_BIAS + 1 : OUT_BIAS + 2] = jnp.sum(low.astype(F32), axis=0, keepdims=True)
    sums_ref[GAIN + 1 : GAIN + 2] = gain_grad
    sums_ref[SHIFT + 1 : SHIFT + 2] = shift_grad
    load_kept(10).wait()

    for c in range(chunks // 2):
        for i in range(2):
            for copy in load_chunk(2 * c + i):
                copy.wait()
        if c == 0:
            for i in (0, 1, 2, 3, 5, 6, 7):
                load_kept(i).start()
            load_p(0).start()
            load_weights(0).start()
            load_p(1).start()
        cols = slice(2 * c * CHUNK, (2 * c + 2) * CHUNK)
        dm = dm_s[...]
        dh = (mm_nt(dm, wd_s[cols]) * gd_s[:, cols].astype(F32)).astype(BF)
        if plan and c == 1:
            plan.midway()
        up = mm_tn(zr_s[...], dh).astype(BF)
        down = mm_tn(g_s[:, cols], dm).astype(BF)
        bias_grad = jnp.sum(dh.astype(F32), axis=0, keepdims=True)
        for i in range(2):
            sums_ref[UP_BIAS + c + 2 * i : UP_BIAS + c + 2 * i + 1] = bias_grad[:, i * CHUNK : (i + 1) * CHUNK]
        if plan:
            plan.feed_step(c, down, up)
        else:
            for i in range(2):
                out_cols = slice((c + 2 * i) * CHUNK, (c + 2 * i + 1) * CHUNK)
                plan_outs[0][out_cols] = down[i * CHUNK : (i + 1) * CHUNK]
                plan_outs[1][:, out_cols] = up[:, i * CHUNK : (i + 1) * CHUNK]
        dx_ref[...] += mm_nt(dh, wu_s[:, cols])
    load_kept(9).wait()
    load_kept(4).wait()
    load_weights(1).wait()
    da, gain_grad, shift_grad = norm_pull(a_s[...], gain_ref[layer, 0:1], dx_ref[...])
    low = da.astype(BF)
    sums_ref[OUT_BIAS : OUT_BIAS + 1] = jnp.sum(low.astype(F32), axis=0, keepdims=True)
    sums_ref[GAIN : GAIN + 1] = gain_grad
    sums_ref[SHIFT : SHIFT + 1] = shift_grad
    proj = mm_tn(o_s[...].astype(BF), low).astype(BF)
    do_s[...] = mm_nt(low, wp_s[...]).astype(BF)
    if plan:
        plan.between(proj)
    else:
        plan_outs[2][...] = proj
    for i in (0, 1, 2, 3, 5, 6, 7):
        load_kept(i).wait()
    load_weights(0).wait()

    def one_group(g, slot):
        cols = lanes_of(g)
        load_p(g).wait()
        scale = scale_s[:, cols]
        v = v_s[:, cols]
        kn = kn_s[:, cols]
        qn = qn_s[:, cols]
        dor = (do_s[:, cols].astype(F32) * rinv_s[:, cols]).astype(BF)
        dor32 = dor.astype(F32)
        less = -group_sum(ones, dor32 * o_s[:, cols])
        high = less.astype(BF).astype(F32)
        extra = jnp.where(lane % depth == 0, high, jnp.where(lane % depth == 1, less - high, 0.0))
        extra = pltpu.roll(extra, depth, 1)
        dor_t = dor.T
        qn_t = qn.T
        v32 = v.astype(F32)
        kn32 = kn.astype(F32)
        qn32 = qn.astype(F32)
        dq = jnp.zeros((tokens, LANES), F32)
        dk_t = []
        dv_t = []
        for h in range(per):
            mine = lane // depth == h
            after = lane // depth == (h + 1) % per
            lhs = jnp.where(mine, dor32, jnp.where(after, extra, 0.0)).astype(BF)
            t = mm_nt(lhs, jnp.where(mine, v32, 1.0).astype(BF))
            head = g * per + h
            table_ref[head] = jnp.zeros(table_ref.shape[1:], F32)
            for pair in range(window // 2):
                rows = slice(2 * pair * window, (2 * pair + 2) * window)
                ds = p_s[slot, h, rows, :].astype(F32) * t[rows]
                ds_s[h % 2, rows, :] = ds.astype(BF)
                for i in range(2):
                    at = window * (window - 1 - (2 * pair + i))
                    table_ref[head, :, at : at + tokens] += ds[i * window : (i + 1) * window]
            low = ds_s[h % 2]
            dv_t.append(mm(dor_t[h * depth : (h + 1) * depth], p_s[slot, h]))
            dk_t.append(mm(qn_t[h * depth : (h + 1) * depth], low))
            dq = dq + mm(low, jnp.where(mine, kn32, 0.0).astype(BF))

        @pl.when(g + 2 < groups)
        def _():
            load_p(g + 2).start()

        dqn = dq * scale
        dkn = jnp.concatenate(dk_t, axis=0).T * scale
        dv = jnp.concatenate(dv_t, axis=0).T
        along_q = qn32 * dqn
        sum_q, sum_k = group_sums(ones, along_q, kn32 * dkn)
        dq = iq_s[:, cols] * (dqn - qn32 * sum_q)
        dk = ik_s[:, cols] * (dkn - kn32 * sum_k)
        sums_ref[LOGIT : LOGIT + 1, cols] = jnp.sum(along_q, axis=0, keepdims=True)
        parts = [part.astype(BF) for part in (dq, dk, dv)]
        sums_ref[QV : QV + 1, cols] = jnp.sum(parts[0].astype(F32), axis=0, keepdims=True)
        sums_ref[QV + 1 : QV + 2, cols] = jnp.sum(parts[2].astype(F32), axis=0, keepdims=True)
        return parts

    def group_step(j, carry):
        if plan:
            plan.attend_begin(j)
        parts = one_group(2 * j, 0) + one_group(2 * j + 1, 1)
        put_table(j).start()
        low = jnp.concatenate([parts[i // 2 + 3 * (i % 2)] for i in range(6)], axis=1)
        grads = mm_tn(e_s[...], low).astype(BF)
        if plan:
            plan.attend_step(j, grads)
        else:
            for i in range(6):
                plan_outs[3][i // 2, :, lanes_of(2 * j + i % 2)] = grads[:, i * LANES : (i + 1) * LANES]
        weights = jnp.concatenate(
            [wqkv_s[:, lanes_of(i // 2 * groups + 2 * j + i % 2)] for i in range(6)], axis=1
        )
        dx_ref[...] += mm_nt(low, weights)
        return carry

    lax.fori_loop(0, groups // 2, group_step, 0)
    if layer == 1:
        send_ref[...] = dx_ref[half:].astype(BF)
    else:
        send_ref[...] = jnp.zeros_like(send_ref)
    if plan:
        plan.end()
    for half_at_end in range(groups // 2):
        put_table(half_at_end).wait()


def block_backward(layer, own, incoming, gain, logits, saved, weights, table_shape, window, heads, riding, left):
    tokens, width = own.shape
    depth = width // heads
    ff = saved[11].shape[1]
    groups = width // LANES
    per = LANES // depth
    sds = jax.ShapeDtypeStruct
    plan = Plan(width, ff, lax.axis_size("img"), bool(left)) if riding else None
    plan_ins = list(left)
    if riding:
        plan_outs = [sds(shape, dt) for shape, dt in plan.outs]
        plan_scratch = plan.scratch
    else:
        plan_outs = [sds((ff, width), BF), sds((width, ff), BF), sds((width, width), BF), sds((3, width, width), BF)]
        plan_scratch = []
    keep = [pltpu.VMEM(item.shape, item.dtype) for item in saved]
    keep[8] = pltpu.VMEM((2, per, tokens, tokens), BF)
    return pl.pallas_call(
        functools.partial(backward_kernel, layer, window, depth, plan),
        in_specs=[VM] * (4 + len(plan_ins)) + [AN] * 18,
        out_specs=[VM] * 3 + [AN] + [VM] * len(plan_outs),
        out_shape=[
            sds((tokens, width), F32), sds((tokens // 2 if layer == 1 else 16, width), BF), sds((16, width), F32),
            sds(table_shape, F32),
        ] + plan_outs,
        scratch_shapes=keep
        + [
            pltpu.VMEM((width, 3 * width), BF), pltpu.VMEM((width, width), BF),
            pltpu.VMEM((width, ff), BF), pltpu.VMEM((ff, width), BF),
            pltpu.VMEM((tokens, width), BF), pltpu.VMEM((tokens, width), BF),
            pltpu.VMEM((2, tokens, tokens), BF), pltpu.VMEM((1, width), F32),
            pltpu.VMEM(table_shape, F32), pltpu.SemaphoreType.DMA((16 + groups + 4 * (ff // CHUNK) + groups // 2,)),
        ]
        + plan_scratch,
        compiler_params=params(2 - layer if riding else None),
        name="block_backward_%d" % layer,
    )(own, incoming, gain, logits, *plan_ins, *saved, *weights)


def entry_logs(first, count, window):
    at = first + lax.broadcasted_iota(jnp.int32, (8, count), 1)
    row = at // (2 * window)
    col = at % (2 * window)
    real = (row < 2 * window - 1) & (col < 2 * window - 1)

    def logs(offset):
        size = jnp.log2(jnp.abs(offset).astype(F32) * (8.0 / (window - 1)) + 1.0) / 3.0
        return jnp.where(offset < 0, -size, size)

    by_row = jnp.where(real, logs(window - 1 - row), 0.0)
    by_col = jnp.where(real, logs(col - (window - 1)), 0.0)
    return by_row, by_col


def column_of(token_col, window, shifted):
    if not shifted:
        return token_col
    return jnp.where(token_col >= window // 2, token_col - window // 2, token_col + window // 2)


def slopes(rel_ref, window):
    first = rel_ref[0:1, 0:1]
    down = rel_ref[window : window + 1, 0:1] - first
    across = rel_ref[1:2, 0:1] - first
    straight = jnp.abs(down) == 2 * window - 1
    sign = lambda step: jnp.where(step > 0, 1.0, -1.0)
    return straight, sign(down), sign(across)


TABLE_CHUNK = 768


def table_kernel(
    layer, window, in_ref, bias_ref, outw_ref, rel, tab_ref, rows_out, hid_out, slope_out,
    hid_s, slope_s, w_s, rel_ref, rows_ref, sems,
):
    fetch = pltpu.make_async_copy(rel.at[pl.ds(0, rel_ref.shape[0]), pl.ds(0, LANES)], rel_ref, sems.at[0])
    fetch.start()
    fetch.wait()
    shifted = layer == 1
    heads, entries = tab_ref.shape
    straight, down, across = slopes(rel_ref, window)
    first, second = in_ref[layer, 0:1], in_ref[layer, 1:2]
    by_rows = jnp.where(straight, first, second) * down
    by_cols = jnp.where(straight, second, first) * across
    w_s[...] = jnp.concatenate(
        [by_rows, by_cols, bias_ref[layer : layer + 1], jnp.zeros((LANES - 3, by_rows.shape[1]), F32)], axis=0
    ).T
    out_high, out_low = split(outw_ref[layer])
    both_w = jnp.concatenate([out_high, out_low], axis=0)

    def put(i, c):
        cols = lanes_of(c, TABLE_CHUNK)
        source, target = ((hid_s, hid_out), (slope_s, slope_out))[i]
        return pltpu.make_async_copy(source.at[:, cols], target.at[:, cols], sems.at[2 * c + i])

    def chunk_step(c, carry):
        cols = lanes_of(c, TABLE_CHUNK)
        by_row, by_col = entry_logs(c * TABLE_CHUNK, TABLE_CHUNK, window)
        pre = w_s[:, 0:1] * by_row[0:1] + w_s[:, 1:2] * by_col[0:1] + w_s[:, 2:3]
        cdf, density = normal_parts(pre)
        hidden, rest = split(pre * cdf)
        hid_s[:, cols] = hidden
        slope_s[:, cols] = (cdf + pre * density).astype(BF)
        put(0, c).start()
        put(1, c).start()
        both = mm(both_w, hidden)
        logits = both[:heads] + both[heads:] + mm(out_high, rest)
        tab_ref[:, cols] = 16.0 / (1.0 + jnp.exp(-logits))
        return carry

    steps = entries // TABLE_CHUNK
    for c in range(steps):
        chunk_step(c, 0)
    spans = entries // LANES
    wide = rows_ref.shape[2]

    def put_rows(k):
        cols = pl.ds(k * LANES, LANES)
        return pltpu.make_async_copy(rows_ref.at[:, :, cols], rows_out.at[:, :, cols], sems.at[2 * steps + k])

    row8 = lax.broadcasted_iota(jnp.int32, (8, LANES), 0)
    lane = lax.broadcasted_iota(jnp.int32, (8, LANES), 1)
    for k in range(wide // LANES):
        at = lane + LANES * k
        low = 2 * window * (LANES * k // window) // LANES
        high = min((2 * window * ((LANES * k + LANES - 1) // window) + 2 * window - 2) // LANES, spans - 1)
        picks = []
        for tile in range(window // 8):
            c1 = column_of(row8 + 8 * tile, window, shifted)
            source = 2 * window * (at // window) + c1 - column_of(at % window, window, shifted) + window - 1
            for s in range(low, high + 1):
                near = source - s * LANES
                inside = (near >= 0) & (near < LANES)
                picks.append((inside, jnp.where(inside, near, 0)))
        for h in range(heads):
            for tile in range(window // 8):
                got = jnp.zeros((8, LANES), F32)
                for s in range(low, high + 1):
                    piece = jnp.broadcast_to(tab_ref[h : h + 1, s * LANES : (s + 1) * LANES], (8, LANES))
                    inside, near = picks[tile * (high + 1 - low) + s - low]
                    got = jnp.where(inside, jnp.take_along_axis(piece, near, axis=1), got)
                rows_ref[h, 8 * tile : 8 * tile + 8, k * LANES : (k + 1) * LANES] = got * LOG2E
        put_rows(k).start()
    for c in range(steps):
        put(0, c).wait()
        put(1, c).wait()
    for k in range(wide // LANES):
        put_rows(k).wait()


def bias_table(layer, rel, place_in, place_bias, place_out, window):
    _, heads, hidden = place_out.shape
    entries = 4 * window * window
    wide = ((2 * window - 1) * window + LANES - 1) // LANES * LANES
    sds = jax.ShapeDtypeStruct
    return pl.pallas_call(
        functools.partial(table_kernel, layer, window),
        in_specs=[VM] * 3 + [AN],
        out_specs=[VM] + [AN] * 3,
        out_shape=[
            sds((heads, entries), F32), sds((heads, window, wide), F32),
            sds((hidden, entries), BF), sds((hidden, entries), BF),
        ],
        scratch_shapes=[
            pltpu.VMEM((hidden, entries), BF), pltpu.VMEM((hidden, entries), BF), pltpu.VMEM((hidden, LANES), F32),
            pltpu.VMEM((32, LANES), jnp.int32), pltpu.VMEM((heads, window, wide), F32),
            pltpu.SemaphoreType.DMA((2 * (entries // TABLE_CHUNK) + wide // LANES,)),
        ],
        compiler_params=params(),
        name="bias_table_%d" % layer,
    )(place_in, place_bias, place_out, rel)


class Tail:
    def __init__(self, depth, shapes):
        down, up, flow_a, flow_b, small = shapes
        self.depth = depth
        self.ins = list(shapes)
        self.along = Along(depth, ("down", "up"), [down, up])
        self.across = Across(flow_a, flow_b)
        self.after = Along(depth, ("flow", "flow"), self.across.sums)
        every = (2 * small[0],) + small[1:]
        piece = (every[0] // 8,) + small[1:]
        self.outs = [(shape, F32) for shape in self.along.sums + self.after.sums + [every]]
        self.small = 7 + depth - 1 + 7
        self.copies = self.along.copies + self.across.copies + self.after.copies + self.small
        self.scratch = (
            self.along.scratch + self.across.scratch + self.after.scratch
            + [pltpu.VMEM(shape, BF) for shape in self.across.sums]
            + [
                pltpu.VMEM(every, F32), pltpu.VMEM((7,) + piece, F32), pltpu.VMEM((depth - 1,) + piece, F32),
                pltpu.VMEM((7,) + piece, F32), pltpu.VMEM(piece, F32), pltpu.VMEM(piece, F32),
            ]
            + sems_for(self.copies)
        )

    def bind(self, ins, outs, scratch):
        along, across, after, between, small, sems = take(scratch, 2, 6, 2, 2, 6, 2)
        self.other_small, self.out_small, self.sems = ins[4], outs[4], sems
        self.all_s, self.got, self.deep_got, self.back, self.part, self.total = small
        at = 0
        self.along.bind(ins[:2], outs[:2], along, sems, at)
        at += self.along.copies
        self.across.bind(ins[2:4], between, across, sems, at)
        at += self.across.copies
        self.after.bind(between, outs[2:4], after, sems, at)
        self.at = at + self.after.copies

    def fellow(self, step):
        me, core, x, z, y = place()
        other = (core + 2 * x + 4 * y + step) % 8
        return (4 * z + other % 4, other // 4)

    def mine(self, step=0):
        _, core, x, _, y = place()
        return (core + 2 * x + 4 * y + step) % 8

    def rows(self, which):
        size = self.part.shape[0]
        return pl.ds(pl.multiple_of(which * size, size), size)

    def scatter(self, step):
        return remote(
            self.all_s.at[self.rows(self.mine(step))], self.got.at[step - 1], self.sems, self.at + step - 1,
            self.fellow(step),
        )

    def deep(self, step):
        return remote(self.part, self.deep_got.at[step - 1], self.sems, self.at + 6 + step, partner("z", step))

    def gather(self, step):
        return remote(
            self.total, self.back.at[step - 1], self.sems, self.at + 6 + self.depth - 1 + step, self.fellow(step)
        )

    def begin(self):
        barrier = pltpu.get_barrier_semaphore()
        others = [self.fellow(step) for step in range(1, 8)]
        others += [partner("z", step) for step in range(1, self.depth)]
        for other in others:
            pl.semaphore_signal(barrier, inc=1, device_id=other, device_id_type=pl.DeviceIdType.MESH)
        pl.semaphore_wait(barrier, len(others))
        self.across.start()
        self.along.start()

    def end(self, small_ref):
        count = small_ref.shape[0]
        self.all_s[:count] = small_ref[...]
        self.all_s[count:] = self.other_small[...]
        for step in range(1, 8):
            self.scatter(step).start()
        self.across.turn()
        self.along.finish()
        part = self.all_s[self.rows(self.mine())]
        for step in range(1, 8):
            self.scatter(step).wait()
            part = part + self.got[step - 1]
        self.part[...] = part
        for step in range(1, self.depth):
            self.deep(step).start()
        self.across.finish()
        self.after.start()
        for step in range(1, self.depth):
            self.deep(step).wait()
            part = part + self.deep_got[step - 1]
        self.total[...] = part
        for step in range(1, 8):
            self.gather(step).start()
        self.out_small[self.rows(self.mine())] = part
        for step in range(1, 8):
            self.gather(step).wait()
            self.out_small[self.rows(self.mine(8 - step))] = self.back[step - 1]
        self.after.finish()


def table_back_kernel(layer, window, tail, *refs):
    n_in, n_out, n_scratch = (len(tail.ins), len(tail.outs), len(tail.scratch)) if tail else (0, 0, 0)
    (
        (rows_ref, tab_ref, outw_ref, sums_ref), tail_ins, (hid_in, slope_in, rel), (small_ref,), tail_outs,
        (hid_s, slope_s, dlog_s, rel_ref, sems), tail_scratch,
    ) = take(refs, 4, n_in, 3, 1, n_out, 5, n_scratch)
    shifted = layer == 1
    heads, entries = tab_ref.shape
    hidden = hid_s.shape[0]
    steps = entries // TABLE_CHUNK

    def get(i, c):
        cols = lanes_of(c, TABLE_CHUNK)
        source, target = ((hid_in, hid_s), (slope_in, slope_s))[i]
        return pltpu.make_async_copy(source.at[:, cols], target.at[:, cols], sems.at[2 * c + i])

    fetch = pltpu.make_async_copy(rel.at[pl.ds(0, rel_ref.shape[0]), pl.ds(0, LANES)], rel_ref, sems.at[2 * steps])
    fetch.start()
    for c in range(steps):
        get(0, c).start()
        get(1, c).start()
    if tail:
        tail.bind(tail_ins, tail_outs, tail_scratch)
        tail.begin()
    spans = rows_ref.shape[2] // LANES
    row8 = lax.broadcasted_iota(jnp.int32, (8, LANES), 0)
    lane = lax.broadcasted_iota(jnp.int32, (8, LANES), 1)
    for k in range(entries // LANES):
        at = lane + LANES * k
        m = at // (2 * window)
        d = at % (2 * window)
        sums = [jnp.zeros((8, LANES), F32) for _ in range(heads)]
        for tile in range(window // 8):
            c1 = column_of(row8 + 8 * tile, window, shifted)
            c2 = c1 - d + window - 1
            real = (c2 >= 0) & (c2 < window) & (m < 2 * window - 1)
            source = window * m + column_of(c2, window, shifted)
            low = window * (LANES * k // (2 * window)) // LANES
            high = min((window * ((LANES * k + LANES - 1) // (2 * window)) + window - 1) // LANES, spans - 1)
            for s in range(low, high + 1):
                near = source - s * LANES
                inside = (near >= 0) & (near < LANES) & real
                near = jnp.where(inside, near, 0)
                for h in range(heads):
                    piece = rows_ref[h, 8 * tile : 8 * tile + 8, s * LANES : (s + 1) * LANES]
                    picked = jnp.take_along_axis(piece, near, axis=1)
                    sums[h] = sums[h] + jnp.where(inside, picked, 0.0)
        for h in range(heads):
            dlog_s[h : h + 1, k * LANES : (k + 1) * LANES] = jnp.sum(sums[h], axis=0, keepdims=True)
    tab = tab_ref[...]
    dlog_s[...] = dlog_s[...] * tab * (1.0 - tab * 0.0625)
    out_high, out_low = split(outw_ref[layer])
    weights = jnp.concatenate([out_high, out_low, out_high], axis=0)

    def chunk_step(c, carry):
        grads, outs = carry
        cols = lanes_of(c, TABLE_CHUNK)
        by_row, by_col = entry_logs(c * TABLE_CHUNK, TABLE_CHUNK, window)
        low, rest = split(dlog_s[:, cols])
        get(0, c).wait()
        get(1, c).wait()
        outs = outs + mm_nt(jnp.concatenate([low, rest], axis=0), hid_s[:, cols])
        dhid = mm_tn(weights, jnp.concatenate([low, low, rest], axis=0))
        dpre, spare = split(dhid * slope_s[:, cols].astype(F32))
        which = lax.broadcasted_iota(jnp.int32, (16, TABLE_CHUNK), 0)
        pick = lambda y: jnp.broadcast_to(y[0:1], (16, TABLE_CHUNK))
        high_row = by_row.astype(BF).astype(F32)
        high_col = by_col.astype(BF).astype(F32)
        factors = jnp.where(which == 0, pick(high_row), 0.0)
        factors = jnp.where(which == 1, pick(high_col), factors)
        factors = jnp.where(which == 2, 1.0, factors)
        factors = jnp.where(which == 3, pick(by_row - high_row), factors)
        factors = jnp.where(which == 4, pick(by_col - high_col), factors)
        factors = factors.astype(BF)
        grads = grads + mm_nt(factors, dpre) + mm_nt(factors, spare)
        return grads, outs

    grads, outs = lax.fori_loop(
        0, steps, chunk_step, (jnp.zeros((16, hidden), F32), jnp.zeros((2 * heads, hidden), F32))
    )
    fetch.wait()
    straight, down, across = slopes(rel_ref, window)
    by_rows = (grads[0:1] + grads[3:4]) * down
    by_cols = (grads[1:2] + grads[4:5]) * across
    small_ref[:PLACE_OUT] = sums_ref[...]
    small_ref[PLACE_IN : PLACE_IN + 1] = jnp.where(straight, by_rows, by_cols)
    small_ref[PLACE_IN + 1 : PLACE_IN + 2] = jnp.where(straight, by_cols, by_rows)
    small_ref[PLACE_BIAS : PLACE_BIAS + 1] = grads[2:3]
    small_ref[PLACE_OUT:] = outs[:heads] + outs[heads:]
    if tail:
        tail.end(small_ref)


def bias_table_backward(layer, rel, rows, net, place_out, sums, window, left):
    tab, hid, slope = net
    heads, entries = tab.shape
    hidden = hid.shape[0]
    tail = Tail(lax.axis_size("img") // 4, [item.shape for item in left]) if left else None
    sds = jax.ShapeDtypeStruct
    return pl.pallas_call(
        functools.partial(table_back_kernel, layer, window, tail),
        in_specs=[VM] * (4 + len(left)) + [AN] * 3,
        out_specs=[VM] * (1 + (len(tail.outs) if tail else 0)),
        out_shape=[sds((SMALL, hidden), F32)] + ([sds(shape, dt) for shape, dt in tail.outs] if tail else []),
        scratch_shapes=[
            pltpu.VMEM((hidden, entries), BF), pltpu.VMEM((hidden, entries), BF), pltpu.VMEM((heads, entries), F32),
            pltpu.VMEM((32, LANES), jnp.int32), pltpu.SemaphoreType.DMA((2 * (entries // TABLE_CHUNK) + 1,)),
        ] + (tail.scratch if tail else []),
        compiler_params=params(3 if tail else None),
        name="bias_table_backward_%d" % layer,
    )(rows, tab, place_out, sums, *left, hid, slope, rel)


def final_kernel(window, depth, split_matrices, *refs):
    (
        (out_ref, in_ref, dx_ref, small_ref), matrices,
        (
            output, input_grad, qkv_grad, qv_grad, scale_grad, place_in_grad, place_bias_grad, place_out_grad,
            proj_grad, up_grad, up_bias_grad, down_grad, out_bias_grad, gain_grad, shift_grad,
        ),
    ) = take(refs, 4, len(refs) - 19, 15)
    half = out_ref.shape[0] // 2
    width = out_ref.shape[1]
    output[:half] = in_ref[...].astype(F32)
    output[half:] = out_ref[:half]
    input_grad[...] = dx_ref[...]
    small = small_ref
    wide = width // 2
    for b in range(2):
        if split_matrices:
            down, up, flow_a, flow_b = matrices[4 * b : 4 * b + 4]
            upper = lax.axis_index("rows") == 0
            qkv_grad[b, :, :wide] = jnp.where(upper, flow_a[0], flow_a[1])
            qkv_grad[b, :, wide : 2 * wide] = jnp.where(upper, flow_a[1], flow_a[0])
            qkv_grad[b, :, 2 * wide :] = jnp.where(upper, flow_b[0], flow_b[1])
            proj_grad[b] = jnp.where(upper, flow_b[1], flow_b[0])
            part = up.shape[2]
            for c in range(2):
                up_grad[b, :, c * part : (c + 1) * part] = up[c]
        else:
            qkv, proj, up, down = matrices[4 * b : 4 * b + 4]
            qkv_grad[b] = qkv[...]
            proj_grad[b] = proj[...]
            up_grad[b] = up[...]
        down_grad[b] = down[...]
        at = b * SMALL
        for i in range(4):
            up_bias_grad[b : b + 1, i * width : (i + 1) * width] = small[at + UP_BIAS + i : at + UP_BIAS + i + 1]
        qv_grad[b] = small[at + QV : at + QV + 2]
        out_bias_grad[b] = small[at + OUT_BIAS : at + OUT_BIAS + 2]
        gain_grad[b] = small[at + GAIN : at + GAIN + 2]
        shift_grad[b] = small[at + SHIFT : at + SHIFT + 2]
        place_in_grad[b] = small[at + PLACE_IN : at + PLACE_IN + 2]
        place_bias_grad[b : b + 1] = small[at + PLACE_BIAS : at + PLACE_BIAS + 1]
        place_out_grad[b] = small[at + PLACE_OUT : at + SMALL]
        heads = width // depth
        head = lax.broadcasted_iota(jnp.int32, (heads, width), 0)
        owner = lax.broadcasted_iota(jnp.int32, (heads, width), 1) // depth
        logit = jnp.where(head == owner, small[at + LOGIT : at + LOGIT + 1], 0.0)
        scale_grad[b : b + 1] = jnp.sum(logit, axis=1, keepdims=True).T


def final_outputs(out, incoming, dx, small, matrices, shapes, window, depth, split_matrices):
    ins = [out, incoming, dx, small] + list(matrices)
    return pl.pallas_call(
        functools.partial(final_kernel, window, depth, split_matrices),
        in_specs=[VM] * len(ins),
        out_specs=[VM] * len(shapes),
        out_shape=[jax.ShapeDtypeStruct(shape, F32) for shape in shapes],
        compiler_params=params(),
        name="final_outputs",
    )(*ins)


def shares(array, images, bands):
    rows, cols = array.shape
    cut = array.reshape(images, rows // images, bands, cols // bands)
    return jnp.transpose(cut, (0, 2, 1, 3)).reshape(images * bands, -1)


def summed_shares(arrays):
    images, bands = lax.axis_size("img"), lax.axis_size("rows")
    joined = jnp.concatenate([shares(array, images, bands) for array in arrays], axis=1)
    mine = lax.psum_scatter(joined, ("img", "rows"), scatter_dimension=0, tiled=True)
    mine = mine.reshape(-1).astype(F32)
    out = []
    at = 0
    for array in arrays:
        rows, cols = array.shape[0] // images, array.shape[1] // bands
        out.append(mine[at : at + rows * cols].reshape(rows, cols))
        at += rows * cols
    return out


def per_device(
    inputs,
    cotangent,
    region,
    rel_index,
    qkv_weight,
    qv_bias,
    logit_scale,
    place_in,
    place_bias,
    place_out,
    proj_weight,
    up_weight,
    up_bias,
    down_weight,
    out_bias,
    norm_gain,
    norm_shift,
):
    window, width = inputs.shape[2], inputs.shape[3]
    heads = logit_scale.shape[1]
    depth = width // heads
    tokens = window * window
    half = tokens // 2
    ff = up_weight.shape[2]
    images, bands = lax.axis_size("img"), lax.axis_size("rows")
    riding = images * bands == 32 and bands == 2
    x = inputs.reshape(tokens, width)
    cot = cotangent.reshape(tokens, width)
    cot_low = cot[:half].astype(BF)
    vectors = (qv_bias, out_bias, norm_gain, norm_shift, logit_scale, up_bias)
    turned_out = jnp.transpose(place_out, (0, 2, 1))
    weights = (qkv_weight, proj_weight, up_weight, down_weight)
    tab, table_zero, *net_zero = bias_table(0, rel_index, place_in, place_bias, turned_out, window)
    hidden, sent, *saved_zero = block_forward(0, (x,), (), vectors, table_zero, weights, window, heads)
    came = passed_along(sent, "rows", -1)
    net_zero = [tab] + net_zero
    tab, table_one, *net_one = bias_table(1, rel_index, place_in, place_bias, turned_out, window)
    net_one = [tab] + net_one
    cot_low, table_one = lax.optimization_barrier((cot_low, table_one))
    cot_in = passed_along(cot_low, "rows", -1)
    shifted_out, sent, *saved_one = block_forward(
        1, (hidden, came), (region.reshape(window, window),), vectors, table_one, weights, window, heads
    )
    out_in = passed_along(sent, "rows", 1)

    def backward(b, own, incoming, saved, left):
        return block_backward(
            b, own, incoming, norm_gain, logit_scale, saved, weights, table_zero.shape, window, heads, riding, left
        )

    def pull(b, rows, net, sums, left=()):
        return bias_table_backward(b, rel_index, rows, net, turned_out, sums, window, left)

    dx_one, sent, sums_one, rows_one, *left = backward(1, cot, cot_in, saved_one, ())
    came = passed_along(sent, "rows", 1)
    (small_one,) = pull(1, rows_one, net_one, sums_one)
    if riding:
        dx_zero, _, sums_zero, rows_zero, *left = backward(0, dx_one, came, saved_zero, left)
        matrices_one = left[4:]
        _, *matrices_zero, small = pull(0, rows_zero, net_zero, sums_zero, (*left[:4], small_one))
    else:
        down, up, proj, qkv = left
        matrix = lambda qkv: jnp.transpose(qkv, (1, 0, 2)).reshape(width, 3 * width)
        matrices_one = summed_shares((matrix(qkv), proj, up, down))
        dx_zero, _, sums_zero, rows_zero, down, up, proj, qkv = backward(0, dx_one, came, saved_zero, ())
        matrices_zero = summed_shares((matrix(qkv), proj, up, down))
        (small_zero,) = pull(0, rows_zero, net_zero, sums_zero)
        small = lax.psum(jnp.concatenate([small_zero, small_one], axis=0), ("img", "rows"))
    cut = lambda rows, cols: (2, rows // images, cols // bands)
    shapes = [
        (tokens, width), (tokens, width), cut(width, 3 * width), (2, 2, width), (2, heads), (2, 2, width), (2, width),
        (2, heads, width), cut(width, width), cut(width, ff), (2, ff), cut(ff, width), (2, 2, width), (2, 2, width),
        (2, 2, width),
    ]
    output, input_grad, *rest = final_outputs(
        shifted_out, out_in, dx_zero, small, list(matrices_zero) + list(matrices_one), shapes, window, depth, riding
    )
    rest[5] = jnp.transpose(rest[5], (0, 2, 1))
    return (output.reshape(inputs.shape), input_grad.reshape(inputs.shape), *rest)


def solution(mesh):
    token = P("img", "rows", None, None)
    matrix = P(None, "img", "rows")
    return jax.shard_map(
        per_device,
        mesh=mesh,
        in_specs=(token, token, P("img", "rows", None)) + (P(),) * 14,
        out_specs=(
            token, token, matrix, P(), P(), P(), P(), P(), matrix, matrix, P(), matrix, P(), P(), P(),
        ),
        check_vma=False,
    )
```

```python
import functools

import jax
import jax.numpy as jnp
from jax import lax
from jax.experimental import pallas as pl
from jax.experimental.pallas import tpu as pltpu
from jax.sharding import PartitionSpec as P

BF = jnp.bfloat16
F32 = jnp.float32
LOG2E = 1.4426950408889634
MASKED = 1.0e9
LANES = 128


def passed_along(array, axis, by):
    devices = lax.axis_size(axis)
    return lax.ppermute(array, axis, [(i, (i + by) % devices) for i in range(devices)])


def mm(a, b):
    return lax.dot_general(a, b, (((1,), (0,)), ((), ())), preferred_element_type=F32)


def mm_nt(a, b):
    return lax.dot_general(a, b, (((1,), (1,)), ((), ())), preferred_element_type=F32)


def mm_tn(a, b):
    return lax.dot_general(a, b, (((0,), (0,)), ((), ())), preferred_element_type=F32)


def group_ones(depth):
    rows = lax.broadcasted_iota(jnp.int32, (LANES, LANES), 0) // depth
    cols = lax.broadcasted_iota(jnp.int32, (LANES, LANES), 1) // depth
    return jnp.where(rows == cols, 1.0, 0.0).astype(BF)


def group_sums(ones, first, second):
    rows = first.shape[0]
    both = group_sum(ones, jnp.concatenate([first, second], axis=0))
    return both[:rows], both[rows:]


def group_sum(ones, values):
    high, low = split(values)
    return mm(jnp.concatenate([high, low], axis=1), jnp.concatenate([ones, ones], axis=0))


def split(values):
    high = values.astype(BF)
    return high, (values - high.astype(F32)).astype(BF)


def head_scales(logit_ref, layer, width):
    heads = logit_ref.shape[1]
    column = jnp.broadcast_to(logit_ref[layer : layer + 1], (heads, heads)).T[:, :1]
    head = lax.broadcasted_iota(jnp.int32, (heads, width), 0)
    owner = lax.broadcasted_iota(jnp.int32, (heads, width), 1) // (width // heads)
    return jnp.exp(jnp.sum(jnp.where(head == owner, column, 0.0), axis=0, keepdims=True))


def normal_parts(values):
    cdf = 0.5 + 0.5 * lax.erf(values * 0.7071067811865476)
    return cdf, jnp.exp2(values * values * (-0.5 * LOG2E)) * 0.3989422804014327


def norm_stats(values):
    centre = values - jnp.mean(values, axis=-1, keepdims=True)
    spread = jnp.mean(centre * centre, axis=-1, keepdims=True)
    rstd = lax.rsqrt(spread + 1e-05)
    return centre * rstd, rstd


def norm_pull(values, gain, grad):
    hat, rstd = norm_stats(values)
    scaled = grad * gain
    first = jnp.mean(scaled, axis=-1, keepdims=True)
    second = jnp.mean(scaled * hat, axis=-1, keepdims=True)
    pulled = rstd * (scaled - first - hat * second)
    gain_grad = jnp.sum(grad * hat, axis=0, keepdims=True)
    shift_grad = jnp.sum(grad, axis=0, keepdims=True)
    return pulled, gain_grad, shift_grad


def place():
    me, y = lax.axis_index("img"), lax.axis_index("rows")
    return me, me % 2, (me // 2) % 2, me // 4, y


def partner(which, step=1):
    me, core, x, z, y = place()
    if which == "core":
        return (me + 1 - 2 * core, y)
    if which == "x":
        return (me + 2 - 4 * x, y)
    if which == "y":
        return (me, 1 - y)
    depth = lax.axis_size("img") // 4
    return ((z + step) % depth * 4 + me % 4, y)


def hail(which):
    depth = lax.axis_size("img") // 4
    others = []
    for name in which:
        others += [partner("z", step) for step in range(1, depth)] if name == "z" else [partner(name)]
    barrier = pltpu.get_barrier_semaphore()
    for other in others:
        pl.semaphore_signal(barrier, inc=1, device_id=other, device_id_type=pl.DeviceIdType.MESH)
    return len(others)


def remote(source, target, sems, at, device):
    return pltpu.make_async_remote_copy(
        src_ref=source, dst_ref=target, send_sem=sems[0].at[at], recv_sem=sems[1].at[at],
        device_id=device, device_id_type=pl.DeviceIdType.MESH,
    )


def half_at(index, size):
    return pl.ds(pl.multiple_of(index * size, LANES), size)


class Across:
    copies = 4

    def __init__(self, first, second):
        self.sums = [first[2:], second[2:]]
        self.scratch = []
        for shape in (first, second):
            self.scratch += [pltpu.VMEM(shape[1:], BF), pltpu.VMEM(shape[1:], BF), pltpu.VMEM(shape[2:], BF)]

    def bind(self, ins, outs, scratch, sems, base):
        self.flows = [(ins[i], outs[i]) + tuple(scratch[3 * i : 3 * i + 3]) for i in range(2)]
        self.sems, self.base = sems, base

    def axes(self, flow):
        _, _, x, _, y = place()
        return (("x", x), ("y", y)) if flow == 0 else (("y", y), ("x", x))

    def copy(self, flow, stage):
        source, _, got, sums, last = self.flows[flow]
        name, here = self.axes(flow)[stage]
        if stage == 0:
            return remote(source.at[1 - here], got, self.sems, self.base + flow, partner(name))
        return remote(sums.at[1 - here], last, self.sems, self.base + 2 + flow, partner(name))

    def start(self):
        self.copy(0, 0).start()
        self.copy(1, 0).start()

    def turn(self):
        for flow in range(2):
            source, _, got, sums, _ = self.flows[flow]
            here = self.axes(flow)[0][1]
            self.copy(flow, 0).wait()
            sums[...] = source[here] + got[...]
            self.copy(flow, 1).start()

    def finish(self):
        for flow in range(2):
            _, out, _, sums, last = self.flows[flow]
            here = self.axes(flow)[1][1]
            self.copy(flow, 1).wait()
            out[...] = sums[here] + last[...]


PICKS = {
    "down": lambda z: (z % 2, z // 2),
    "up": lambda z: (slice(None), z),
    "flow": lambda z: (slice(None), z),
}


class Along:
    def __init__(self, depth, kinds, shapes):
        self.depth = depth
        self.picks = [PICKS[kind] for kind in kinds]
        drop = {"down": lambda shape: shape[2:], "up": lambda shape: shape[:1] + shape[2:], "flow": lambda shape: shape[:1] + shape[2:]}
        self.sums = [drop[kind](shape) for kind, shape in zip(kinds, shapes)]
        self.scratch = [pltpu.VMEM((depth - 1,) + shape, BF) for shape in self.sums]
        self.copies = (depth - 1) * len(shapes)

    def bind(self, ins, outs, scratch, sems, base):
        self.ins, self.outs, self.got = ins, outs, scratch
        self.sems, self.base = sems, base

    def each(self):
        _, _, _, z, _ = place()
        for i, (source, got, pick) in enumerate(zip(self.ins, self.got, self.picks)):
            for step in range(1, self.depth):
                at = self.base + i * (self.depth - 1) + step - 1
                share = source.at[pick((z + step) % self.depth)]
                yield remote(share, got.at[step - 1], self.sems, at, partner("z", step))

    def start(self):
        for copy in self.each():
            copy.start()

    def finish(self):
        _, _, _, z, _ = place()
        for copy in self.each():
            copy.wait()
        for source, out, got, pick in zip(self.ins, self.outs, self.got, self.picks):
            total = source[pick(z)].astype(F32)
            for step in range(1, self.depth):
                total = total + got[step - 1].astype(F32)
            out[...] = total


def sems_for(count):
    return [pltpu.SemaphoreType.DMA((count,)), pltpu.SemaphoreType.DMA((count,))]


def take(refs, *counts):
    out = []
    at = 0
    for count in counts:
        out.append(refs[at : at + count])
        at += count
    assert at == len(refs), (at, len(refs))
    return out


def whole(shape):
    return pl.BlockSpec(shape, lambda *s: (0,) * len(shape))


VM = pl.BlockSpec(memory_space=pltpu.VMEM)
AN = pl.BlockSpec(memory_space=pl.ANY)
LIMIT = 62 * 2**20


def params(number=None):
    if number is None:
        return pltpu.CompilerParams(vmem_limit_bytes=LIMIT)
    return pltpu.CompilerParams(vmem_limit_bytes=LIMIT, collective_id=number, has_side_effects=True)


def lanes_of(group, size=LANES):
    return pl.ds(pl.multiple_of(group * size, size), size)


CHUNK = 512


def forward_kernel(layer, window, depth, *refs):
    masked = layer == 1
    tokens = window * window
    width = refs[0].shape[1]
    groups = width // LANES
    per = LANES // depth
    (
        x_refs, region_refs, (qv_ref, ob_ref, gain_ref, shift_ref, logit_ref, ub_ref),
        (bias, wqkv, wp, wu, wd), (out_ref, send_ref), saved, keep, (z_s, m_s, qkv_s, scale_s, qm_s, km_s, bias_ref),
        (wqkv_s, wp_s, wu_s, wd_s), (load, store),
    ) = take(refs, 2 if masked else 1, 1 if masked else 0, 6, 5, 2, 14, 14, 7, 4, 2)
    chunks = ub_ref.shape[1] // CHUNK
    e_s, qn_s, kn_s, v_s, o_s, iq_s, ik_s, rinv_s, p_s, a_s, zr_s, g_s, gd_s, mo_s = keep
    lane = lax.broadcasted_iota(jnp.int32, (1, LANES), 1) // depth

    def load_qkv(i):
        return pltpu.make_async_copy(wqkv.at[layer, :, lanes_of(i, width)], wqkv_s.at[i], load.at[i])

    def load_rest(i):
        source, target = ((wp, wp_s), (wu, wu_s), (wd, wd_s))[i]
        return pltpu.make_async_copy(source.at[layer], target, load.at[3 + i])

    def put(i):
        return pltpu.make_async_copy(keep[i], saved[i], store.at[i])

    def put_p(g):
        rows = pl.ds(g * per, per)
        return pltpu.make_async_copy(p_s.at[rows], saved[8].at[rows], store.at[14 + g])

    def put_g(i, c):
        cols = lanes_of(c, CHUNK)
        return pltpu.make_async_copy(
            keep[11 + i].at[:, cols], saved[11 + i].at[:, cols], store.at[14 + groups + 2 * c + i]
        )

    load_bias = pltpu.make_async_copy(bias, bias_ref, load.at[6])
    for i in range(3):
        load_qkv(i).start()
    load_bias.start()
    for i in range(3):
        load_rest(i).start()
    scale_s[...] = head_scales(logit_ref, layer, width) * LOG2E
    ones = group_ones(depth)
    if masked:
        token = lax.broadcasted_iota(jnp.int32, (tokens, window), 0)
        place_in_row = lax.broadcasted_iota(jnp.int32, (tokens, window), 1)
        rows_pick = jnp.where(token // window == place_in_row, 1.0, 0.0).astype(BF)
        labels = mm(rows_pick, region_refs[0][...].astype(F32).astype(BF))
        mine = column_of(token % window, window, True) == place_in_row
        labels = jnp.sum(jnp.where(mine, labels, 0.0), axis=1, keepdims=True)
        each = lax.broadcasted_iota(jnp.int32, (tokens, LANES), 1)
        same = labels == each.astype(F32)
        qm_s[...] = jnp.where(same, 1.0, 0.0).astype(BF)
        km_s[...] = jnp.where(same | (each >= 8), 0.0, -MASKED).astype(BF)
    half = tokens // 2
    if masked:
        z_s[:half] = x_refs[0][half:]
        z_s[half:] = x_refs[1][...].astype(F32)
        x_ref = z_s
    else:
        x_ref = x_refs[0]
    e_s[...] = x_ref[...].astype(BF)
    put(0).start()
    for i in range(3):
        load_qkv(i).wait()
        raw = mm(e_s[...], wqkv_s[i])
        if i != 1:
            raw = raw + qv_ref[layer, i // 2 : i // 2 + 1]
        qkv_s[i] = raw
    load_bias.wait()

    def group_step(g, carry):
        cols = lanes_of(g)
        q = qkv_s[0, :, cols]
        k = qkv_s[1, :, cols]
        v = qkv_s[2, :, cols]
        iq, ik = group_sums(ones, q * q, k * k)
        iq = lax.rsqrt(iq + 1e-06)
        ik = lax.rsqrt(ik + 1e-06)
        qn = q * iq
        kn = (k * ik).astype(BF)
        iq_s[:, cols] = iq
        ik_s[:, cols] = ik
        qn_s[:, cols] = qn.astype(BF)
        kn_s[:, cols] = kn
        v_s[:, cols] = v.astype(BF)
        scales = scale_s[:, cols]
        rhs = jnp.concatenate([kn, km_s[...]], axis=1) if masked else kn
        mixed = jnp.zeros((tokens, LANES), F32)
        total = mixed
        for h in range(per):
            mine = lane == h
            lhs = jnp.where(mine, qn, 0.0).astype(BF)
            if masked:
                lhs = jnp.concatenate([lhs, qm_s[...]], axis=1)
            cosine = mm_nt(lhs, rhs)
            scale = scales[:, h * depth : h * depth + 1]
            table = bias_ref[g * per + h]
            for pair in range(window // 2):
                parts = []
                for r in (2 * pair, 2 * pair + 1):
                    at = window * (window - 1 - r)
                    parts.append(
                        cosine[r * window : (r + 1) * window] * scale + table[:, at : at + tokens]
                    )
                both = jnp.concatenate(parts, axis=0)
                p_s[g * per + h, 2 * pair * window : (2 * pair + 2) * window, :] = jnp.exp2(both).astype(BF)
            both = mm(p_s[g * per + h], jnp.where(mine, v, 1.0).astype(BF))
            mixed = jnp.where(mine, both, mixed)
            total = jnp.where(lane == (h + 1) % per, both, total)
        rinv = pltpu.roll(1.0 / total, LANES - depth, 1)
        rinv_s[:, cols] = rinv
        o_s[:, cols] = mixed * rinv
        put_p(g).start()
        return carry

    lax.fori_loop(0, groups, group_step, 0)
    for i in range(1, 8):
        put(i).start()
    load_rest(0).wait()
    a = mm(o_s[...].astype(BF), wp_s[...]) + ob_ref[layer, 0:1]
    a_s[...] = a
    put(9).start()
    hat, _ = norm_stats(a)
    z = x_ref[...] + (hat * gain_ref[layer, 0:1] + shift_ref[layer, 0:1])
    z_s[...] = z
    zr_s[...] = z.astype(BF)
    put(10).start()
    m_s[...] = jnp.zeros_like(m_s)
    load_rest(1).wait()
    load_rest(2).wait()

    def chunk_step(c, carry):
        cols = lanes_of(c, CHUNK)
        pre = mm(zr_s[...], wu_s[:, cols]) + ub_ref[layer : layer + 1, cols]
        cdf, density = normal_parts(pre)
        act = (pre * cdf).astype(BF)
        g_s[:, cols] = act
        gd_s[:, cols] = (cdf + pre * density).astype(BF)
        put_g(0, c).start()
        put_g(1, c).start()
        m_s[...] += mm(act, wd_s[cols, :])
        return carry

    lax.fori_loop(0, chunks, chunk_step, 0)
    m = m_s[...] + ob_ref[layer, 1:2]
    mo_s[...] = m
    put(13).start()
    hat, _ = norm_stats(m)
    out = z_s[...] + (hat * gain_ref[layer, 1:2] + shift_ref[layer, 1:2])
    out_ref[...] = out
    send_ref[...] = (out[half:] if masked else out[:half]).astype(BF)
    for i in range(14):
        if i not in (8, 11, 12):
            put(i).wait()
    for g in range(groups):
        put_p(g).wait()
    for c in range(chunks):
        put_g(0, c).wait()
        put_g(1, c).wait()


def block_forward(layer, xs, region, vectors, table, weights, window, heads):
    tokens, width = window * window, xs[0].shape[1]
    depth = width // heads
    w_qkv, w_proj, w_up, w_down = weights
    ff = w_up.shape[2]
    groups = width // LANES
    sds = jax.ShapeDtypeStruct
    tok = lambda dt, cols=width: sds((tokens, cols), dt)
    saved = [
        tok(BF), tok(BF), tok(BF), tok(BF), tok(F32), tok(F32), tok(F32), tok(F32),
        sds((heads, tokens, tokens), BF), tok(F32), tok(BF), tok(BF, ff), tok(BF, ff), tok(F32),
    ]
    ins = list(xs) + list(region) + list(vectors)
    stores = 14 + groups + 2 * (ff // CHUNK)
    return pl.pallas_call(
        functools.partial(forward_kernel, layer, window, depth),
        in_specs=[VM] * len(ins) + [AN] * 5,
        out_specs=[VM] * 2 + [AN] * 14,
        out_shape=[tok(F32), sds((tokens // 2, width), BF)] + saved,
        scratch_shapes=[pltpu.VMEM(item.shape, item.dtype) for item in saved]
        + [
            pltpu.VMEM((tokens, width), F32), pltpu.VMEM((tokens, width), F32), pltpu.VMEM((3, tokens, width), F32),
            pltpu.VMEM((1, width), F32), pltpu.VMEM((tokens, LANES), BF), pltpu.VMEM((tokens, LANES), BF),
            pltpu.VMEM(table.shape, F32),
            pltpu.VMEM((3, width, width), BF), pltpu.VMEM((width, width), BF),
            pltpu.VMEM((width, ff), BF), pltpu.VMEM((ff, width), BF),
            pltpu.SemaphoreType.DMA((7,)), pltpu.SemaphoreType.DMA((stores,)),
        ],
        compiler_params=params(),
        name="block_forward_%d" % layer,
    )(*ins, table, w_qkv, w_proj, w_up, w_down)


UP_BIAS, QV, OUT_BIAS, GAIN, SHIFT, PLACE_IN, PLACE_BIAS, LOGIT, PLACE_OUT = 0, 4, 6, 8, 10, 12, 14, 15, 16
SMALL = 32


class Plan:
    def __init__(self, width, ff, images, follows):
        deep = images // 4
        self.deep = deep
        self.down = (2, 2, 2, 2, deep // 2, ff // images, width // 2)
        self.up = (2, 2, 2, 2, deep, width // images, ff // 4)
        half = lambda shape: shape[:1] + shape[2:]
        self.half_down, self.half_up = half(self.down), half(self.up)
        self.flow = (2, 2, 2, 2, deep, width // images, width // 2)
        self.got_flow = half(self.flow)
        self.half_flow = self.flow[2:4] + (2,) + self.flow[4:]
        self.parts = [Across(self.half_down[1:], self.half_up[1:]) for _ in range(2)]
        sums = [(2,) + shape for shape in self.parts[0].sums]
        self.outs = [(shape, BF) for shape in sums] + [(self.half_flow, BF)] * 2
        self.scratch = [pltpu.VMEM(shape, BF) for shape in (
            self.down, self.up, self.half_down, self.half_up, self.flow, self.flow, self.got_flow, self.got_flow,
        )] + self.parts[0].scratch + self.parts[1].scratch
        self.core = 8
        self.copies = self.core + 8
        self.ins = []
        self.follows = follows
        if follows:
            self.old = Along(deep, ("down", "up"), sums)
            self.turned = Across(self.half_flow, self.half_flow)
            self.late = Along(deep, ("flow", "flow"), self.turned.sums)
            self.ins = sums + [self.half_flow] * 2
            self.outs += [(shape, F32) for shape in self.old.sums + self.late.sums]
            self.scratch += [pltpu.VMEM(shape, BF) for shape in self.turned.sums]
            self.scratch += self.old.scratch + self.turned.scratch + self.late.scratch
            self.copies += self.old.copies + self.turned.copies + self.late.copies
        self.scratch = self.scratch + sems_for(self.copies)

    def bind(self, ins, outs, scratch):
        sems = scratch[-2:]
        self.sems = sems
        self.down_s, self.up_s, self.got_down, self.got_up = scratch[:4]
        self.flows = ((scratch[4], scratch[6]), (scratch[5], scratch[7]))
        self.flow_outs = outs[2:4]
        for c, part in enumerate(self.parts):
            part.bind(
                [self.got_down.at[c], self.got_up.at[c]], [outs[0].at[c], outs[1].at[c]],
                scratch[8 + 6 * c : 14 + 6 * c], sems, self.core + 4 * c,
            )
        if self.follows:
            rest = scratch[20:-2]
            at = self.core + 8
            between, old, turned, late = take(rest, 2, 2, 6, 2)
            self.old.bind(ins[:2], outs[4:6], old, sems, at)
            at += self.old.copies
            self.turned.bind(ins[2:4], between, turned, sems, at)
            at += self.turned.copies
            self.late.bind(between, outs[6:8], late, sems, at)

    def feed_copy(self, c, which):
        _, core, _, _, _ = place()
        source, target = ((self.down_s, self.got_down), (self.up_s, self.got_up))[which]
        return remote(source.at[c, 1 - core], target.at[c], self.sems, 2 * c + which, partner("core"))

    def flow_copy(self, part, flow):
        _, core, _, _, _ = place()
        source, target = self.flows[flow]
        return remote(source.at[part, 1 - core], target.at[part], self.sems, 4 + 2 * part + flow, partner("core"))

    def begin(self):
        self.hailed = hail(["core", "x", "y"] + (["z"] if self.follows else []))

    def open(self):
        pl.semaphore_wait(pltpu.get_barrier_semaphore(), self.hailed)
        if self.follows:
            self.turned.start()
            self.old.start()

    def feed_step(self, c, down, up):
        rows = self.down[5]
        wide = self.down[6]
        for i in range(2):
            for x in range(2):
                for core in range(2):
                    at = i * CHUNK + (2 * x + core) * rows
                    for y in range(2):
                        self.down_s[c, core, x, y, i] = down[at : at + rows, y * wide : (y + 1) * wide]
        self.feed_copy(c, 0).start()
        self.spread(self.up_s, c, 1, None, up)
        self.feed_copy(c, 1).start()

    def spread(self, target, part, flow, y, block, cols=slice(None)):
        for half in (0, 1) if y is None else (y,):
            piece = block
            if y is None:
                wide = block.shape[1] // 2
                piece = block[:, half * wide : (half + 1) * wide]
            piece = piece.reshape((self.deep, 2, 2, -1, piece.shape[1]))
            for x in range(2):
                for core in range(2):
                    first, second = (x, half) if flow == 0 else (half, x)
                    target[part, core, first, second, :, :, cols] = piece[:, x, core]

    def ready(self, c):
        _, core, _, _, _ = place()
        self.feed_copy(c, 0).wait()
        self.got_down[c] = self.got_down[c] + self.down_s[c, core]
        self.feed_copy(c, 1).wait()
        self.got_up[c] = self.got_up[c] + self.up_s[c, core]
        self.parts[c].start()

    def midway(self):
        self.ready(0)

    def between(self, proj):
        flow_b = self.flows[1][0]
        half = proj.shape[1] // 2
        self.spread(flow_b, 0, 1, 1, proj[:, half:])
        self.spread(flow_b, 1, 1, 0, proj[:, :half])
        self.ready(1)
        if self.follows:
            self.turned.turn()
            self.old.finish()
        self.parts[0].turn()

    def attend_begin(self, half):
        @pl.when(half == 1)
        def _():
            self.parts[1].turn()
            if self.follows:
                self.turned.finish()
                self.late.start()

    def attend_step(self, half, grads):
        flow_a, flow_b = self.flows[0][0], self.flows[1][0]
        wide = grads.shape[1] // 3
        q, k, v = (grads[:, i * wide : (i + 1) * wide] for i in range(3))

        @pl.when(half == 0)
        def _():
            self.spread(flow_b, 0, 1, 0, k)
            self.flow_copy(0, 1).start()
            self.spread(flow_a, 0, 0, 0, q)
            self.spread(flow_a, 0, 0, 1, v)
            self.flow_copy(0, 0).start()

        @pl.when(half == 1)
        def _():
            self.spread(flow_b, 1, 1, 1, v)
            self.flow_copy(1, 1).start()
            self.spread(flow_a, 1, 0, 0, q)
            self.spread(flow_a, 1, 0, 1, k)
            self.flow_copy(1, 0).start()

    def end(self):
        _, core, _, _, _ = place()
        self.parts[0].finish()
        for part in range(2):
            for flow in (1, 0):
                source, got = self.flows[flow]
                self.flow_copy(part, flow).wait()
                self.flow_outs[flow][:, :, part] = source[part, core] + got[part]
        if self.follows:
            self.late.finish()
        self.parts[1].finish()


def backward_kernel(layer, window, depth, plan, *refs):
    tokens = window * window
    half = tokens // 2
    n_plan_in = len(plan.ins) if plan else 0
    n_plan_out = len(plan.outs) if plan else 4
    n_plan_scratch = len(plan.scratch) if plan else 0
    (
        (in_ref, gain_ref, logit_ref), plan_ins, (own_ref,), saved, (wqkv, wp, wu, wd),
        (dx_ref, send_ref, sums_ref, table_out), plan_outs, keep,
        (wqkv_s, wp_s, wu_s, wd_s, dm_s, do_s, ds_s, scale_s, table_ref, load), plan_scratch,
    ) = take(refs, 3, n_plan_in, 1, 14, 4, 4, n_plan_out, 14, 10, n_plan_scratch)
    e_s, qn_s, kn_s, v_s, o_s, iq_s, ik_s, rinv_s, p_s, a_s, zr_s, g_s, gd_s, m_s = keep
    width = own_ref.shape[1]
    ff = g_s.shape[1]
    groups = width // LANES
    per = LANES // depth
    chunks = ff // CHUNK
    wide = tokens
    lane = lax.broadcasted_iota(jnp.int32, (1, LANES), 1)

    def load_kept(i):
        return pltpu.make_async_copy(saved[i], keep[i], load.at[i])

    def load_p(g):
        return pltpu.make_async_copy(saved[8].at[pl.ds(g * per, per)], p_s.at[g % 2], load.at[14 + g])

    def put_table(half):
        rows = pl.ds(half * 2 * per, 2 * per)
        return pltpu.make_async_copy(
            table_ref.at[rows], table_out.at[rows], load.at[16 + groups + 4 * chunks + half]
        )

    def load_weights(i):
        source, target = ((wqkv, wqkv_s), (wp, wp_s))[i]
        return pltpu.make_async_copy(source.at[layer], target, load.at[14 + groups + i])

    def load_chunk(c):
        here = lanes_of(c, CHUNK)
        cols = lanes_of(c // 2 + c % 2 * 2, CHUNK)
        at = 16 + groups + 4 * c
        return [
            pltpu.make_async_copy(saved[11].at[:, cols], g_s.at[:, here], load.at[at]),
            pltpu.make_async_copy(saved[12].at[:, cols], gd_s.at[:, here], load.at[at + 1]),
            pltpu.make_async_copy(wd.at[layer, cols], wd_s.at[here], load.at[at + 2]),
            pltpu.make_async_copy(wu.at[layer, :, cols], wu_s.at[:, here], load.at[at + 3]),
        ]

    own_from, own_to = (half, 0) if layer == 1 else (0, half)
    load_own = pltpu.make_async_copy(
        own_ref.at[pl.ds(own_from, half)], dx_ref.at[pl.ds(own_to, half)], load.at[16 + groups + 4 * chunks + 2]
    )
    load_own.start()
    load_kept(13).start()
    load_kept(10).start()
    for c in range(chunks):
        for copy in load_chunk(c):
            copy.start()
    load_kept(9).start()
    load_kept(4).start()
    load_weights(1).start()
    if plan:
        plan.bind(plan_ins, plan_outs, plan_scratch)
        plan.begin()
    if layer == 1:
        dx_ref[half:] = in_ref[...].astype(F32)
    else:
        dx_ref[:half] = in_ref[...].astype(F32)
    load_own.wait()
    scale_s[...] = head_scales(logit_ref, layer, width)
    ones = group_ones(depth)
    load_kept(13).wait()
    dm, gain_grad, shift_grad = norm_pull(m_s[...], gain_ref[layer, 1:2], dx_ref[...])
    low = dm.astype(BF)
    dm_s[...] = low
    sums_ref[...] = jnp.zeros_like(sums_ref)
    sums_ref[OUT_BIAS + 1 : OUT_BIAS + 2] = jnp.sum(low.astype(F32), axis=0, keepdims=True)
    sums_ref[GAIN + 1 : GAIN + 2] = gain_grad
    sums_ref[SHIFT + 1 : SHIFT + 2] = shift_grad
    load_kept(10).wait()
    if plan:
        plan.open()

    for c in range(chunks // 2):
        for i in range(2):
            for copy in load_chunk(2 * c + i):
                copy.wait()
        if c == 0:
            for i in (0, 1, 2, 3, 5, 6, 7):
                load_kept(i).start()
            load_p(0).start()
            load_weights(0).start()
            load_p(1).start()
        cols = slice(2 * c * CHUNK, (2 * c + 2) * CHUNK)
        dm = dm_s[...]
        dh = (mm_nt(dm, wd_s[cols]) * gd_s[:, cols].astype(F32)).astype(BF)
        if plan and c == 1:
            plan.midway()
        up = mm_tn(zr_s[...], dh).astype(BF)
        down = mm_tn(g_s[:, cols], dm).astype(BF)
        bias_grad = jnp.sum(dh.astype(F32), axis=0, keepdims=True)
        for i in range(2):
            sums_ref[UP_BIAS + c + 2 * i : UP_BIAS + c + 2 * i + 1] = bias_grad[:, i * CHUNK : (i + 1) * CHUNK]
        if plan:
            plan.feed_step(c, down, up)
        else:
            for i in range(2):
                out_cols = slice((c + 2 * i) * CHUNK, (c + 2 * i + 1) * CHUNK)
                plan_outs[0][out_cols] = down[i * CHUNK : (i + 1) * CHUNK]
                plan_outs[1][:, out_cols] = up[:, i * CHUNK : (i + 1) * CHUNK]
        dx_ref[...] += mm_nt(dh, wu_s[:, cols])
    load_kept(9).wait()
    load_kept(4).wait()
    load_weights(1).wait()
    da, gain_grad, shift_grad = norm_pull(a_s[...], gain_ref[layer, 0:1], dx_ref[...])
    low = da.astype(BF)
    sums_ref[OUT_BIAS : OUT_BIAS + 1] = jnp.sum(low.astype(F32), axis=0, keepdims=True)
    sums_ref[GAIN : GAIN + 1] = gain_grad
    sums_ref[SHIFT : SHIFT + 1] = shift_grad
    proj = mm_tn(o_s[...].astype(BF), low).astype(BF)
    do_s[...] = mm_nt(low, wp_s[...]).astype(BF)
    if plan:
        plan.between(proj)
    else:
        plan_outs[2][...] = proj
    for i in (0, 1, 2, 3, 5, 6, 7):
        load_kept(i).wait()
    load_weights(0).wait()

    def one_group(g, slot):
        cols = lanes_of(g)
        load_p(g).wait()
        scale = scale_s[:, cols]
        v = v_s[:, cols]
        kn = kn_s[:, cols]
        qn = qn_s[:, cols]
        dor = (do_s[:, cols].astype(F32) * rinv_s[:, cols]).astype(BF)
        dor32 = dor.astype(F32)
        less = -group_sum(ones, dor32 * o_s[:, cols])
        high = less.astype(BF).astype(F32)
        extra = jnp.where(lane % depth == 0, high, jnp.where(lane % depth == 1, less - high, 0.0))
        extra = pltpu.roll(extra, depth, 1)
        dor_t = dor.T
        qn_t = qn.T
        v32 = v.astype(F32)
        kn32 = kn.astype(F32)
        qn32 = qn.astype(F32)
        dq = jnp.zeros((tokens, LANES), F32)
        dk_t = []
        dv_t = []
        for h in range(per):
            mine = lane // depth == h
            after = lane // depth == (h + 1) % per
            lhs = jnp.where(mine, dor32, jnp.where(after, extra, 0.0)).astype(BF)
            t = mm_nt(lhs, jnp.where(mine, v32, 1.0).astype(BF))
            head = g * per + h
            table_ref[head] = jnp.zeros(table_ref.shape[1:], F32)
            for pair in range(window // 2):
                rows = slice(2 * pair * window, (2 * pair + 2) * window)
                ds = p_s[slot, h, rows, :].astype(F32) * t[rows]
                ds_s[h % 2, rows, :] = ds.astype(BF)
                for i in range(2):
                    at = window * (window - 1 - (2 * pair + i))
                    table_ref[head, :, at : at + tokens] += ds[i * window : (i + 1) * window]
            low = ds_s[h % 2]
            dv_t.append(mm(dor_t[h * depth : (h + 1) * depth], p_s[slot, h]))
            dk_t.append(mm(qn_t[h * depth : (h + 1) * depth], low))
            dq = dq + mm(low, jnp.where(mine, kn32, 0.0).astype(BF))

        @pl.when(g + 2 < groups)
        def _():
            load_p(g + 2).start()

        dqn = dq * scale
        dkn = jnp.concatenate(dk_t, axis=0).T * scale
        dv = jnp.concatenate(dv_t, axis=0).T
        along_q = qn32 * dqn
        sum_q, sum_k = group_sums(ones, along_q, kn32 * dkn)
        dq = iq_s[:, cols] * (dqn - qn32 * sum_q)
        dk = ik_s[:, cols] * (dkn - kn32 * sum_k)
        sums_ref[LOGIT : LOGIT + 1, cols] = jnp.sum(along_q, axis=0, keepdims=True)
        parts = [part.astype(BF) for part in (dq, dk, dv)]
        sums_ref[QV : QV + 1, cols] = jnp.sum(parts[0].astype(F32), axis=0, keepdims=True)
        sums_ref[QV + 1 : QV + 2, cols] = jnp.sum(parts[2].astype(F32), axis=0, keepdims=True)
        return parts

    def group_step(j, carry):
        if plan:
            plan.attend_begin(j)
        parts = one_group(2 * j, 0) + one_group(2 * j + 1, 1)
        put_table(j).start()
        low = jnp.concatenate([parts[i // 2 + 3 * (i % 2)] for i in range(6)], axis=1)
        grads = mm_tn(e_s[...], low).astype(BF)
        if plan:
            plan.attend_step(j, grads)
        else:
            for i in range(6):
                plan_outs[3][i // 2, :, lanes_of(2 * j + i % 2)] = grads[:, i * LANES : (i + 1) * LANES]
        weights = jnp.concatenate(
            [wqkv_s[:, lanes_of(i // 2 * groups + 2 * j + i % 2)] for i in range(6)], axis=1
        )
        dx_ref[...] += mm_nt(low, weights)
        return carry

    lax.fori_loop(0, groups // 2, group_step, 0)
    if layer == 1:
        send_ref[...] = dx_ref[half:].astype(BF)
    else:
        send_ref[...] = jnp.zeros_like(send_ref)
    if plan:
        plan.end()
    for half_at_end in range(groups // 2):
        put_table(half_at_end).wait()


def block_backward(layer, own, incoming, gain, logits, saved, weights, table_shape, window, heads, riding, left):
    tokens, width = own.shape
    depth = width // heads
    ff = saved[11].shape[1]
    groups = width // LANES
    per = LANES // depth
    sds = jax.ShapeDtypeStruct
    plan = Plan(width, ff, lax.axis_size("img"), bool(left)) if riding else None
    plan_ins = list(left)
    if riding:
        plan_outs = [sds(shape, dt) for shape, dt in plan.outs]
        plan_scratch = plan.scratch
    else:
        plan_outs = [sds((ff, width), BF), sds((width, ff), BF), sds((width, width), BF), sds((3, width, width), BF)]
        plan_scratch = []
    keep = [pltpu.VMEM(item.shape, item.dtype) for item in saved]
    keep[8] = pltpu.VMEM((2, per, tokens, tokens), BF)
    return pl.pallas_call(
        functools.partial(backward_kernel, layer, window, depth, plan),
        in_specs=[VM] * (3 + len(plan_ins)) + [AN] * 19,
        out_specs=[VM] * 3 + [AN] + [VM] * len(plan_outs),
        out_shape=[
            sds((tokens, width), F32), sds((tokens // 2 if layer == 1 else 16, width), BF), sds((16, width), F32),
            sds(table_shape, F32),
        ] + plan_outs,
        scratch_shapes=keep
        + [
            pltpu.VMEM((width, 3 * width), BF), pltpu.VMEM((width, width), BF),
            pltpu.VMEM((width, ff), BF), pltpu.VMEM((ff, width), BF),
            pltpu.VMEM((tokens, width), BF), pltpu.VMEM((tokens, width), BF),
            pltpu.VMEM((2, tokens, tokens), BF), pltpu.VMEM((1, width), F32),
            pltpu.VMEM(table_shape, F32), pltpu.SemaphoreType.DMA((17 + groups + 4 * (ff // CHUNK) + groups // 2,)),
        ]
        + plan_scratch,
        compiler_params=params(2 - layer if riding else None),
        name="block_backward_%d" % layer,
    )(incoming, gain, logits, *plan_ins, own, *saved, *weights)


def entry_logs(first, count, window):
    at = first + lax.broadcasted_iota(jnp.int32, (8, count), 1)
    row = at // (2 * window)
    col = at % (2 * window)
    real = (row < 2 * window - 1) & (col < 2 * window - 1)

    def logs(offset):
        size = jnp.log2(jnp.abs(offset).astype(F32) * (8.0 / (window - 1)) + 1.0) / 3.0
        return jnp.where(offset < 0, -size, size)

    by_row = jnp.where(real, logs(window - 1 - row), 0.0)
    by_col = jnp.where(real, logs(col - (window - 1)), 0.0)
    return by_row, by_col


def column_of(token_col, window, shifted):
    if not shifted:
        return token_col
    return jnp.where(token_col >= window // 2, token_col - window // 2, token_col + window // 2)


def slopes(rel_ref, window):
    first = rel_ref[0:1, 0:1]
    down = rel_ref[window : window + 1, 0:1] - first
    across = rel_ref[1:2, 0:1] - first
    straight = jnp.abs(down) == 2 * window - 1
    sign = lambda step: jnp.where(step > 0, 1.0, -1.0)
    return straight, sign(down), sign(across)


TABLE_CHUNK = 768


def table_kernel(
    layer, window, in_ref, bias_ref, outw_ref, rel, tab_ref, rows_out, hid_out, slope_out,
    hid_s, slope_s, w_s, rel_ref, rows_ref, sems,
):
    fetch = pltpu.make_async_copy(rel.at[pl.ds(0, rel_ref.shape[0]), pl.ds(0, LANES)], rel_ref, sems.at[0])
    fetch.start()
    fetch.wait()
    shifted = layer == 1
    heads, entries = tab_ref.shape
    straight, down, across = slopes(rel_ref, window)
    first, second = in_ref[layer, 0:1], in_ref[layer, 1:2]
    by_rows = jnp.where(straight, first, second) * down
    by_cols = jnp.where(straight, second, first) * across
    w_s[...] = jnp.concatenate(
        [by_rows, by_cols, bias_ref[layer : layer + 1], jnp.zeros((LANES - 3, by_rows.shape[1]), F32)], axis=0
    ).T
    out_high, out_low = split(outw_ref[layer])
    both_w = jnp.concatenate([out_high, out_low], axis=0)

    def put(i, c):
        cols = lanes_of(c, TABLE_CHUNK)
        source, target = ((hid_s, hid_out), (slope_s, slope_out))[i]
        return pltpu.make_async_copy(source.at[:, cols], target.at[:, cols], sems.at[2 * c + i])

    def chunk_step(c, carry):
        cols = lanes_of(c, TABLE_CHUNK)
        by_row, by_col = entry_logs(c * TABLE_CHUNK, TABLE_CHUNK, window)
        pre = w_s[:, 0:1] * by_row[0:1] + w_s[:, 1:2] * by_col[0:1] + w_s[:, 2:3]
        cdf, density = normal_parts(pre)
        hidden, rest = split(pre * cdf)
        hid_s[:, cols] = hidden
        slope_s[:, cols] = (cdf + pre * density).astype(BF)
        put(0, c).start()
        put(1, c).start()
        both = mm(both_w, hidden)
        logits = both[:heads] + both[heads:] + mm(out_high, rest)
        tab_ref[:, cols] = 16.0 / (1.0 + jnp.exp(-logits))
        return carry

    steps = entries // TABLE_CHUNK
    for c in range(steps):
        chunk_step(c, 0)
    spans = entries // LANES
    wide = rows_ref.shape[2]

    def put_rows(k):
        cols = pl.ds(k * LANES, LANES)
        return pltpu.make_async_copy(rows_ref.at[:, :, cols], rows_out.at[:, :, cols], sems.at[2 * steps + k])

    row8 = lax.broadcasted_iota(jnp.int32, (8, LANES), 0)
    lane = lax.broadcasted_iota(jnp.int32, (8, LANES), 1)
    for k in range(wide // LANES):
        at = lane + LANES * k
        low = 2 * window * (LANES * k // window) // LANES
        high = min((2 * window * ((LANES * k + LANES - 1) // window) + 2 * window - 2) // LANES, spans - 1)
        picks = []
        for tile in range(window // 8):
            c1 = column_of(row8 + 8 * tile, window, shifted)
            source = 2 * window * (at // window) + c1 - column_of(at % window, window, shifted) + window - 1
            for s in range(low, high + 1):
                near = source - s * LANES
                inside = (near >= 0) & (near < LANES)
                picks.append((inside, jnp.where(inside, near, 0)))
        for h in range(heads):
            for tile in range(window // 8):
                got = jnp.zeros((8, LANES), F32)
                for s in range(low, high + 1):
                    piece = jnp.broadcast_to(tab_ref[h : h + 1, s * LANES : (s + 1) * LANES], (8, LANES))
                    inside, near = picks[tile * (high + 1 - low) + s - low]
                    got = jnp.where(inside, jnp.take_along_axis(piece, near, axis=1), got)
                rows_ref[h, 8 * tile : 8 * tile + 8, k * LANES : (k + 1) * LANES] = got * LOG2E
        put_rows(k).start()
    for c in range(steps):
        put(0, c).wait()
        put(1, c).wait()
    for k in range(wide // LANES):
        put_rows(k).wait()


def bias_table(layer, rel, place_in, place_bias, place_out, window):
    _, heads, hidden = place_out.shape
    entries = 4 * window * window
    wide = ((2 * window - 1) * window + LANES - 1) // LANES * LANES
    sds = jax.ShapeDtypeStruct
    return pl.pallas_call(
        functools.partial(table_kernel, layer, window),
        in_specs=[VM] * 3 + [AN],
        out_specs=[VM] + [AN] * 3,
        out_shape=[
            sds((heads, entries), F32), sds((heads, window, wide), F32),
            sds((hidden, entries), BF), sds((hidden, entries), BF),
        ],
        scratch_shapes=[
            pltpu.VMEM((hidden, entries), BF), pltpu.VMEM((hidden, entries), BF), pltpu.VMEM((hidden, LANES), F32),
            pltpu.VMEM((32, LANES), jnp.int32), pltpu.VMEM((heads, window, wide), F32),
            pltpu.SemaphoreType.DMA((2 * (entries // TABLE_CHUNK) + wide // LANES,)),
        ],
        compiler_params=params(),
        name="bias_table_%d" % layer,
    )(place_in, place_bias, place_out, rel)


class Tail:
    def __init__(self, depth, shapes):
        down, up, flow_a, flow_b, small = shapes
        self.depth = depth
        self.ins = list(shapes)
        self.along = Along(depth, ("down", "up"), [down, up])
        self.across = Across(flow_a, flow_b)
        self.after = Along(depth, ("flow", "flow"), self.across.sums)
        every = (2 * small[0],) + small[1:]
        piece = (every[0] // 8,) + small[1:]
        self.outs = [(shape, F32) for shape in self.along.sums + self.after.sums + [every]]
        self.small = 7 + depth - 1 + 7
        self.copies = self.along.copies + self.across.copies + self.after.copies + self.small
        self.scratch = (
            self.along.scratch + self.across.scratch + self.after.scratch
            + [pltpu.VMEM(shape, BF) for shape in self.across.sums]
            + [
                pltpu.VMEM(every, F32), pltpu.VMEM((7,) + piece, F32), pltpu.VMEM((depth - 1,) + piece, F32),
                pltpu.VMEM((7,) + piece, F32), pltpu.VMEM(piece, F32), pltpu.VMEM(piece, F32),
            ]
            + sems_for(self.copies)
        )

    def bind(self, ins, outs, scratch):
        along, across, after, between, small, sems = take(scratch, 2, 6, 2, 2, 6, 2)
        self.other_small, self.out_small, self.sems = ins[4], outs[4], sems
        self.all_s, self.got, self.deep_got, self.back, self.part, self.total = small
        at = 0
        self.along.bind(ins[:2], outs[:2], along, sems, at)
        at += self.along.copies
        self.across.bind(ins[2:4], between, across, sems, at)
        at += self.across.copies
        self.after.bind(between, outs[2:4], after, sems, at)
        self.at = at + self.after.copies

    def fellow(self, step):
        me, core, x, z, y = place()
        other = (core + 2 * x + 4 * y + step) % 8
        return (4 * z + other % 4, other // 4)

    def mine(self, step=0):
        _, core, x, _, y = place()
        return (core + 2 * x + 4 * y + step) % 8

    def rows(self, which):
        size = self.part.shape[0]
        return pl.ds(pl.multiple_of(which * size, size), size)

    def scatter(self, step):
        return remote(
            self.all_s.at[self.rows(self.mine(step))], self.got.at[step - 1], self.sems, self.at + step - 1,
            self.fellow(step),
        )

    def deep(self, step):
        return remote(self.part, self.deep_got.at[step - 1], self.sems, self.at + 6 + step, partner("z", step))

    def gather(self, step):
        return remote(
            self.total, self.back.at[step - 1], self.sems, self.at + 6 + self.depth - 1 + step, self.fellow(step)
        )

    def begin(self):
        barrier = pltpu.get_barrier_semaphore()
        others = [self.fellow(step) for step in range(1, 8)]
        others += [partner("z", step) for step in range(1, self.depth)]
        for other in others:
            pl.semaphore_signal(barrier, inc=1, device_id=other, device_id_type=pl.DeviceIdType.MESH)
        pl.semaphore_wait(barrier, len(others))
        self.across.start()
        self.along.start()

    def end(self, small_ref):
        count = small_ref.shape[0]
        self.all_s[:count] = small_ref[...]
        self.all_s[count:] = self.other_small[...]
        for step in range(1, 8):
            self.scatter(step).start()
        self.across.turn()
        self.along.finish()
        part = self.all_s[self.rows(self.mine())]
        for step in range(1, 8):
            self.scatter(step).wait()
            part = part + self.got[step - 1]
        self.part[...] = part
        for step in range(1, self.depth):
            self.deep(step).start()
        self.across.finish()
        self.after.start()
        for step in range(1, self.depth):
            self.deep(step).wait()
            part = part + self.deep_got[step - 1]
        self.total[...] = part
        for step in range(1, 8):
            self.gather(step).start()
        self.out_small[self.rows(self.mine())] = part
        for step in range(1, 8):
            self.gather(step).wait()
            self.out_small[self.rows(self.mine(8 - step))] = self.back[step - 1]
        self.after.finish()


def table_back_kernel(layer, window, tail, *refs):
    n_in, n_out, n_scratch = (len(tail.ins), len(tail.outs), len(tail.scratch)) if tail else (0, 0, 0)
    (
        (rows_ref, tab_ref, outw_ref, sums_ref), tail_ins, (hid_in, slope_in, rel), (small_ref,), tail_outs,
        (hid_s, slope_s, dlog_s, rel_ref, sems), tail_scratch,
    ) = take(refs, 4, n_in, 3, 1, n_out, 5, n_scratch)
    shifted = layer == 1
    heads, entries = tab_ref.shape
    hidden = hid_s.shape[0]
    steps = entries // TABLE_CHUNK

    def get(i, c):
        cols = lanes_of(c, TABLE_CHUNK)
        source, target = ((hid_in, hid_s), (slope_in, slope_s))[i]
        return pltpu.make_async_copy(source.at[:, cols], target.at[:, cols], sems.at[2 * c + i])

    fetch = pltpu.make_async_copy(rel.at[pl.ds(0, rel_ref.shape[0]), pl.ds(0, LANES)], rel_ref, sems.at[2 * steps])
    fetch.start()
    for c in range(steps):
        get(0, c).start()
        get(1, c).start()
    if tail:
        tail.bind(tail_ins, tail_outs, tail_scratch)
        tail.begin()
    spans = rows_ref.shape[2] // LANES
    row8 = lax.broadcasted_iota(jnp.int32, (8, LANES), 0)
    lane = lax.broadcasted_iota(jnp.int32, (8, LANES), 1)
    for k in range(entries // LANES):
        at = lane + LANES * k
        m = at // (2 * window)
        d = at % (2 * window)
        sums = [jnp.zeros((8, LANES), F32) for _ in range(heads)]
        for tile in range(window // 8):
            c1 = column_of(row8 + 8 * tile, window, shifted)
            c2 = c1 - d + window - 1
            real = (c2 >= 0) & (c2 < window) & (m < 2 * window - 1)
            source = window * m + column_of(c2, window, shifted)
            low = window * (LANES * k // (2 * window)) // LANES
            high = min((window * ((LANES * k + LANES - 1) // (2 * window)) + window - 1) // LANES, spans - 1)
            for s in range(low, high + 1):
                near = source - s * LANES
                inside = (near >= 0) & (near < LANES) & real
                near = jnp.where(inside, near, 0)
                for h in range(heads):
                    piece = rows_ref[h, 8 * tile : 8 * tile + 8, s * LANES : (s + 1) * LANES]
                    picked = jnp.take_along_axis(piece, near, axis=1)
                    sums[h] = sums[h] + jnp.where(inside, picked, 0.0)
        for h in range(heads):
            dlog_s[h : h + 1, k * LANES : (k + 1) * LANES] = jnp.sum(sums[h], axis=0, keepdims=True)
    tab = tab_ref[...]
    dlog_s[...] = dlog_s[...] * tab * (1.0 - tab * 0.0625)
    out_high, out_low = split(outw_ref[layer])
    weights = jnp.concatenate([out_high, out_low, out_high], axis=0)

    def chunk_step(c, carry):
        grads, outs = carry
        cols = lanes_of(c, TABLE_CHUNK)
        by_row, by_col = entry_logs(c * TABLE_CHUNK, TABLE_CHUNK, window)
        low, rest = split(dlog_s[:, cols])
        get(0, c).wait()
        get(1, c).wait()
        outs = outs + mm_nt(jnp.concatenate([low, rest], axis=0), hid_s[:, cols])
        dhid = mm_tn(weights, jnp.concatenate([low, low, rest], axis=0))
        dpre, spare = split(dhid * slope_s[:, cols].astype(F32))
        which = lax.broadcasted_iota(jnp.int32, (16, TABLE_CHUNK), 0)
        pick = lambda y: jnp.broadcast_to(y[0:1], (16, TABLE_CHUNK))
        high_row = by_row.astype(BF).astype(F32)
        high_col = by_col.astype(BF).astype(F32)
        factors = jnp.where(which == 0, pick(high_row), 0.0)
        factors = jnp.where(which == 1, pick(high_col), factors)
        factors = jnp.where(which == 2, 1.0, factors)
        factors = jnp.where(which == 3, pick(by_row - high_row), factors)
        factors = jnp.where(which == 4, pick(by_col - high_col), factors)
        factors = factors.astype(BF)
        grads = grads + mm_nt(factors, dpre) + mm_nt(factors, spare)
        return grads, outs

    grads, outs = lax.fori_loop(
        0, steps, chunk_step, (jnp.zeros((16, hidden), F32), jnp.zeros((2 * heads, hidden), F32))
    )
    fetch.wait()
    straight, down, across = slopes(rel_ref, window)
    by_rows = (grads[0:1] + grads[3:4]) * down
    by_cols = (grads[1:2] + grads[4:5]) * across
    small_ref[:PLACE_OUT] = sums_ref[...]
    small_ref[PLACE_IN : PLACE_IN + 1] = jnp.where(straight, by_rows, by_cols)
    small_ref[PLACE_IN + 1 : PLACE_IN + 2] = jnp.where(straight, by_cols, by_rows)
    small_ref[PLACE_BIAS : PLACE_BIAS + 1] = grads[2:3]
    small_ref[PLACE_OUT:] = outs[:heads] + outs[heads:]
    if tail:
        tail.end(small_ref)


def bias_table_backward(layer, rel, rows, net, place_out, sums, window, left):
    tab, hid, slope = net
    heads, entries = tab.shape
    hidden = hid.shape[0]
    tail = Tail(lax.axis_size("img") // 4, [item.shape for item in left]) if left else None
    sds = jax.ShapeDtypeStruct
    return pl.pallas_call(
        functools.partial(table_back_kernel, layer, window, tail),
        in_specs=[VM] * (4 + len(left)) + [AN] * 3,
        out_specs=[VM] * (1 + (len(tail.outs) if tail else 0)),
        out_shape=[sds((SMALL, hidden), F32)] + ([sds(shape, dt) for shape, dt in tail.outs] if tail else []),
        scratch_shapes=[
            pltpu.VMEM((hidden, entries), BF), pltpu.VMEM((hidden, entries), BF), pltpu.VMEM((heads, entries), F32),
            pltpu.VMEM((32, LANES), jnp.int32), pltpu.SemaphoreType.DMA((2 * (entries // TABLE_CHUNK) + 1,)),
        ] + (tail.scratch if tail else []),
        compiler_params=params(3 if tail else None),
        name="bias_table_backward_%d" % layer,
    )(rows, tab, place_out, sums, *left, hid, slope, rel)


def final_kernel(window, depth, split_matrices, *refs):
    (
        (out_ref, in_ref, dx_ref, small_ref), matrices,
        (
            output, input_grad, qkv_grad, qv_grad, scale_grad, place_in_grad, place_bias_grad, place_out_grad,
            proj_grad, up_grad, up_bias_grad, down_grad, out_bias_grad, gain_grad, shift_grad,
        ),
    ) = take(refs, 4, len(refs) - 19, 15)
    half = out_ref.shape[0] // 2
    width = out_ref.shape[1]
    output[:half] = in_ref[...].astype(F32)
    output[half:] = out_ref[:half]
    input_grad[...] = dx_ref[...]
    small = small_ref
    wide = width // 2
    for b in range(2):
        if split_matrices:
            down, up, flow_a, flow_b = matrices[4 * b : 4 * b + 4]
            upper = lax.axis_index("rows") == 0
            qkv_grad[b, :, :wide] = jnp.where(upper, flow_a[0], flow_a[1])
            qkv_grad[b, :, wide : 2 * wide] = jnp.where(upper, flow_a[1], flow_a[0])
            qkv_grad[b, :, 2 * wide :] = jnp.where(upper, flow_b[0], flow_b[1])
            proj_grad[b] = jnp.where(upper, flow_b[1], flow_b[0])
            part = up.shape[2]
            for c in range(2):
                up_grad[b, :, c * part : (c + 1) * part] = up[c]
        else:
            qkv, proj, up, down = matrices[4 * b : 4 * b + 4]
            qkv_grad[b] = qkv[...]
            proj_grad[b] = proj[...]
            up_grad[b] = up[...]
        down_grad[b] = down[...]
        at = b * SMALL
        for i in range(4):
            up_bias_grad[b : b + 1, i * width : (i + 1) * width] = small[at + UP_BIAS + i : at + UP_BIAS + i + 1]
        qv_grad[b] = small[at + QV : at + QV + 2]
        out_bias_grad[b] = small[at + OUT_BIAS : at + OUT_BIAS + 2]
        gain_grad[b] = small[at + GAIN : at + GAIN + 2]
        shift_grad[b] = small[at + SHIFT : at + SHIFT + 2]
        place_in_grad[b] = small[at + PLACE_IN : at + PLACE_IN + 2]
        place_bias_grad[b : b + 1] = small[at + PLACE_BIAS : at + PLACE_BIAS + 1]
        place_out_grad[b] = small[at + PLACE_OUT : at + SMALL]
        heads = width // depth
        head = lax.broadcasted_iota(jnp.int32, (heads, width), 0)
        owner = lax.broadcasted_iota(jnp.int32, (heads, width), 1) // depth
        logit = jnp.where(head == owner, small[at + LOGIT : at + LOGIT + 1], 0.0)
        scale_grad[b : b + 1] = jnp.sum(logit, axis=1, keepdims=True).T


def final_outputs(out, incoming, dx, small, matrices, shapes, window, depth, split_matrices):
    ins = [out, incoming, dx, small] + list(matrices)
    return pl.pallas_call(
        functools.partial(final_kernel, window, depth, split_matrices),
        in_specs=[VM] * len(ins),
        out_specs=[VM] * len(shapes),
        out_shape=[jax.ShapeDtypeStruct(shape, F32) for shape in shapes],
        compiler_params=params(),
        name="final_outputs",
    )(*ins)


def shares(array, images, bands):
    rows, cols = array.shape
    cut = array.reshape(images, rows // images, bands, cols // bands)
    return jnp.transpose(cut, (0, 2, 1, 3)).reshape(images * bands, -1)


def summed_shares(arrays):
    images, bands = lax.axis_size("img"), lax.axis_size("rows")
    joined = jnp.concatenate([shares(array, images, bands) for array in arrays], axis=1)
    mine = lax.psum_scatter(joined, ("img", "rows"), scatter_dimension=0, tiled=True)
    mine = mine.reshape(-1).astype(F32)
    out = []
    at = 0
    for array in arrays:
        rows, cols = array.shape[0] // images, array.shape[1] // bands
        out.append(mine[at : at + rows * cols].reshape(rows, cols))
        at += rows * cols
    return out


def per_device(
    inputs,
    cotangent,
    region,
    rel_index,
    qkv_weight,
    qv_bias,
    logit_scale,
    place_in,
    place_bias,
    place_out,
    proj_weight,
    up_weight,
    up_bias,
    down_weight,
    out_bias,
    norm_gain,
    norm_shift,
):
    window, width = inputs.shape[2], inputs.shape[3]
    heads = logit_scale.shape[1]
    depth = width // heads
    tokens = window * window
    half = tokens // 2
    ff = up_weight.shape[2]
    images, bands = lax.axis_size("img"), lax.axis_size("rows")
    riding = images * bands == 32 and bands == 2
    x = inputs.reshape(tokens, width)
    cot = cotangent.reshape(tokens, width)
    cot_low = cot[:half].astype(BF)
    vectors = (qv_bias, out_bias, norm_gain, norm_shift, logit_scale, up_bias)
    turned_out = jnp.transpose(place_out, (0, 2, 1))
    weights = (qkv_weight, proj_weight, up_weight, down_weight)
    tab, table_zero, *net_zero = bias_table(0, rel_index, place_in, place_bias, turned_out, window)
    hidden, sent, *saved_zero = block_forward(0, (x,), (), vectors, table_zero, weights, window, heads)
    came = passed_along(sent, "rows", -1)
    net_zero = [tab] + net_zero
    tab, table_one, *net_one = bias_table(1, rel_index, place_in, place_bias, turned_out, window)
    net_one = [tab] + net_one
    cot_low, table_one = lax.optimization_barrier((cot_low, table_one))
    cot_in = passed_along(cot_low, "rows", -1)
    shifted_out, sent, *saved_one = block_forward(
        1, (hidden, came), (region.reshape(window, window),), vectors, table_one, weights, window, heads
    )
    out_in = passed_along(sent, "rows", 1)

    def backward(b, own, incoming, saved, left):
        return block_backward(
            b, own, incoming, norm_gain, logit_scale, saved, weights, table_zero.shape, window, heads, riding, left
        )

    def pull(b, rows, net, sums, left=()):
        return bias_table_backward(b, rel_index, rows, net, turned_out, sums, window, left)

    dx_one, sent, sums_one, rows_one, *left = backward(1, cot, cot_in, saved_one, ())
    came = passed_along(sent, "rows", 1)
    (small_one,) = pull(1, rows_one, net_one, sums_one)
    if riding:
        dx_zero, _, sums_zero, rows_zero, *left = backward(0, dx_one, came, saved_zero, left)
        matrices_one = left[4:]
        _, *matrices_zero, small = pull(0, rows_zero, net_zero, sums_zero, (*left[:4], small_one))
    else:
        down, up, proj, qkv = left
        matrix = lambda qkv: jnp.transpose(qkv, (1, 0, 2)).reshape(width, 3 * width)
        matrices_one = summed_shares((matrix(qkv), proj, up, down))
        dx_zero, _, sums_zero, rows_zero, down, up, proj, qkv = backward(0, dx_one, came, saved_zero, ())
        matrices_zero = summed_shares((matrix(qkv), proj, up, down))
        (small_zero,) = pull(0, rows_zero, net_zero, sums_zero)
        small = lax.psum(jnp.concatenate([small_zero, small_one], axis=0), ("img", "rows"))
    cut = lambda rows, cols: (2, rows // images, cols // bands)
    shapes = [
        (tokens, width), (tokens, width), cut(width, 3 * width), (2, 2, width), (2, heads), (2, 2, width), (2, width),
        (2, heads, width), cut(width, width), cut(width, ff), (2, ff), cut(ff, width), (2, 2, width), (2, 2, width),
        (2, 2, width),
    ]
    output, input_grad, *rest = final_outputs(
        shifted_out, out_in, dx_zero, small, list(matrices_zero) + list(matrices_one), shapes, window, depth, riding
    )
    rest[5] = jnp.transpose(rest[5], (0, 2, 1))
    return (output.reshape(inputs.shape), input_grad.reshape(inputs.shape), *rest)


def solution(mesh):
    token = P("img", "rows", None, None)
    matrix = P(None, "img", "rows")
    return jax.shard_map(
        per_device,
        mesh=mesh,
        in_specs=(token, token, P("img", "rows", None)) + (P(),) * 14,
        out_specs=(
            token, token, matrix, P(), P(), P(), P(), P(), matrix, matrix, P(), matrix, P(), P(), P(),
        ),
        check_vma=False,
    )
```
